32 devices in a mesh: dp: 8 (over y, x, core), tensor: 4 (over z).
Axes of the slice: x: 2, y: 2, z: 4, core: 2. Of those that a mesh axis runs over, the one named last changes fastest.
Arguments:
- tokens: bfloat16 [8192, 1536], P('dp'), may hold values from -6 to 6
- cotangent: bfloat16 [8192, 1536], P('dp'), may hold values from -6 to 6
- segment_ids: int32 [8, 1024], P('dp'), may hold values from 0 to 3, never falling along the last dimension, each value on 1 to 512 neighbouring positions
- parents: int32 [8, 4], P('dp'), may hold values from 0 to 2, as said below
- expert_ids: int32 [8192, 8], P('dp'), may hold values from 0 to 15, all different within a row
- gate_weights: float32 [8192, 8], P('dp'), may hold values from 0.15 to 0.6
- placement_order: int32 [8, 8192], P('dp'), may hold values from 0 to 8191, each once within a row
- capacity: int32 [16], replicated, may hold values from 320 to 640, as said below
- w_qkv: float32 [1536, 2560], P(None, 'tensor')
- w_out: float32 [1536, 1536], P('tensor')
- w_gate_up: float32 [16, 1536, 1024], P('tensor')
- w_down: float32 [16, 512, 1536], P('tensor')
- norm_gains: float32 [2, 1536], replicated
- first_qkv: float32 [1536, 2560], P('dp', 'tensor')
- first_out: float32 [1536, 1536], P('tensor', 'dp')
- first_gate_up: float32 [16, 1536, 1024], P('tensor', 'dp')
- first_down: float32 [16, 512, 1536], P('tensor', None, 'dp')
- first_gains: float32 [2, 1536], P(None, 'dp')
- second_moment_projection: float32 [1536, 2560], P('dp', 'tensor'), may hold values from 8192 to 32768
- second_out: float32 [1536, 1536], P('tensor', 'dp'), may hold values from 81 to 327
- second_gate_up: float32 [16, 1536, 1024], P('tensor', 'dp'), may hold values from 368 to 1474
- second_down: float32 [16, 512, 1536], P('tensor', None, 'dp'), may hold values from 69 to 278
- second_gains: float32 [2, 1536], P(None, 'dp'), may hold values from 2949 to 11796
Outputs:
- block_out: bfloat16 [8192, 1536], P('dp')
- input_grad: bfloat16 [8192, 1536], P('dp')
- updated_qkv: float32 [1536, 2560], P('dp', 'tensor')
- updated_out: float32 [1536, 1536], P('tensor', 'dp')
- updated_gate_up: float32 [16, 1536, 1024], P('tensor', 'dp')
- updated_down: float32 [16, 512, 1536], P('tensor', None, 'dp')
- updated_gains: float32 [2, 1536], P(None, 'dp')
- next_first_qkv: float32 [1536, 2560], P('dp', 'tensor')
- next_first_out: float32 [1536, 1536], P('tensor', 'dp')
- next_first_gate_up: float32 [16, 1536, 1024], P('tensor', 'dp')
- next_first_down: float32 [16, 512, 1536], P('tensor', None, 'dp')
- next_first_gains: float32 [2, 1536], P(None, 'dp')
- next_second_qkv: float32 [1536, 2560], P('dp', 'tensor')
- next_second_out: float32 [1536, 1536], P('tensor', 'dp')
- next_second_gate_up: float32 [16, 1536, 1024], P('tensor', 'dp')
- next_second_down: float32 [16, 512, 1536], P('tensor', None, 'dp')
- next_second_gains: float32 [2, 1536], P(None, 'dp')
- trust_norms: float32 [6, 2], replicated
The draws below stay inside these ranges and needn't reach their ends.
Inputs may be any that keep to these rules, and one draw needn't show every extreme that they name: parents[t, s] is below s for s > 0, and parents[t, 0] = 0; some tree has 2 as the parent of its last segment. capacity[e] is the most pairs of one tree that expert e takes; some expert has exactly 640.
All inputs are finite; a program needn't handle non-finite values.
Results may differ from the reference program's by a relative error of at most 0.017.
The reference program's roundings to bfloat16 on the way count: a program that leaves them out, or rounds other values in their place, can miss the bound.
Values sent between devices are 32-bit elements; how exact they have to be, the bound alone decides.
No kernel may reach another device: no remote copies, remote signals or barrier semaphores. Data moves between devices by JAX's collectives and lax.ppermute only.
A program may use at most 320 MiB of HBM per device.

```python
import math
import jax
import jax.numpy as jnp
import numpy as np
from jax import lax

MODEL_DIM = 1536
QUERY_HEADS = 24
KEY_VALUE_HEADS = 8
HEAD_SIZE = 64
FF = 512
TOP = 8
EXPERTS = 16
NSEG = 4
STEP = 3
TOK = 1024
GROUP_COLUMNS = 320
CAP = 640
PAIRS = 8192
TOKENS = 8192
N_DP = 8


def ramp_factor(array_extents, dims, ratio):
    factor = jnp.ones(array_extents, jnp.float32)
    for axis_dim in dims:
        extent = array_extents[axis_dim]
        ramp = jnp.arange(extent, dtype=jnp.float32) / max(extent - 1, 1) - 0.5
        layout = [1] * len(array_extents)
        layout[axis_dim] = extent
        factor = factor * jnp.exp(math.log(ratio) * ramp).reshape(layout)
    return factor


def draw_parents(key, part):
    key = jax.random.fold_in(key, 13)
    spread_key, tree_key = jax.random.split(key)
    spread = jax.random.randint(spread_key, (N_DP, NSEG), 0, 1 << 20)
    above_count = jnp.maximum(jnp.arange(NSEG, dtype=jnp.int32), 1)
    drawn = (spread % above_count[None, :]).astype(jnp.int32)
    chosen = jax.random.randint(tree_key, (), 0, N_DP)
    force = (jnp.arange(N_DP)[:, None] == chosen) & (jnp.arange(NSEG)[None, :] == NSEG - 1)
    return jnp.where(force, NSEG - 2, drawn).astype(jnp.int32)


def draw_capacity(key, part):
    key = jax.random.fold_in(key, 11)
    value_key, pick_key = jax.random.split(key)
    values = jax.random.randint(value_key, (EXPERTS,), CAP // 2, CAP + 1)
    chosen = jax.random.randint(pick_key, (), 0, EXPERTS)
    return jnp.where(jnp.arange(EXPERTS) == chosen, CAP, values).astype(jnp.int32)


def draw_w_qkv(key, part):
    key = jax.random.fold_in(key, 21)
    array_extents = (MODEL_DIM, KEY_VALUE_HEADS * GROUP_COLUMNS)
    noise = jax.random.normal(key, array_extents, jnp.float32)
    ratio = 1.7320508
    return noise * ramp_factor(array_extents, (0, 1), ratio) / math.sqrt(MODEL_DIM)


def draw_w_out(key, part):
    key = jax.random.fold_in(key, 22)
    array_extents = (QUERY_HEADS * HEAD_SIZE, MODEL_DIM)
    noise = jax.random.normal(key, array_extents, jnp.float32)
    ratio = 1.7320508
    return noise * ramp_factor(array_extents, (0, 1), ratio) / math.sqrt(max(1, QUERY_HEADS * HEAD_SIZE * 8 // TOK))


def draw_w_gate_up(key, part):
    key = jax.random.fold_in(key, 23)
    array_extents = (EXPERTS, MODEL_DIM, 2 * FF)
    noise = jax.random.normal(key, array_extents, jnp.float32)
    ratio = 1.7320508
    return noise * ramp_factor(array_extents, (0, 1), ratio) / math.sqrt(MODEL_DIM)


def draw_w_down(key, part):
    key = jax.random.fold_in(key, 24)
    array_extents = (EXPERTS, FF, MODEL_DIM)
    noise = jax.random.normal(key, array_extents, jnp.float32)
    ratio = 1.7320508
    return noise * ramp_factor(array_extents, (0, 2), ratio) / math.sqrt(FF)


def draw_norm_gains(key, part):
    key = jax.random.fold_in(key, 25)
    array_extents = (2, MODEL_DIM)
    noise = jnp.clip(jax.random.normal(key, array_extents, jnp.float32), -4.0, 4.0)
    ratio = 1.7320508
    return (1.0 + 0.1 * noise) * ramp_factor(array_extents, (1,), ratio)


def draw_first_qkv(key, part):
    key = jax.random.fold_in(key, 31)
    array_extents = (MODEL_DIM, KEY_VALUE_HEADS * GROUP_COLUMNS)
    noise = jax.random.normal(key, array_extents, jnp.float32)
    ratio = 1.7320508
    return noise * ramp_factor(array_extents, (0, 1), ratio) * math.sqrt(TOKENS)


def draw_first_out(key, part):
    key = jax.random.fold_in(key, 32)
    array_extents = (QUERY_HEADS * HEAD_SIZE, MODEL_DIM)
    noise = jax.random.normal(key, array_extents, jnp.float32)
    ratio = 1.7320508
    return noise * ramp_factor(array_extents, (0, 1), ratio) * 0.1 * math.sqrt(TOKENS)


def draw_first_gate_up(key, part):
    key = jax.random.fold_in(key, 33)
    array_extents = (EXPERTS, MODEL_DIM, 2 * FF)
    noise = jax.random.normal(key, array_extents, jnp.float32)
    ratio = 1.7320508
    return noise * ramp_factor(array_extents, (0, 1), ratio) * 0.3 * math.sqrt(TOKENS * TOP / EXPERTS)


def draw_first_down(key, part):
    key = jax.random.fold_in(key, 34)
    array_extents = (EXPERTS, FF, MODEL_DIM)
    noise = jax.random.normal(key, array_extents, jnp.float32)
    ratio = 1.7320508
    return noise * ramp_factor(array_extents, (0, 2), ratio) * 0.13 * math.sqrt(TOKENS * TOP / EXPERTS)


def draw_first_gains(key, part):
    key = jax.random.fold_in(key, 35)
    array_extents = (2, MODEL_DIM)
    noise = jax.random.normal(key, array_extents, jnp.float32)
    ratio = 1.7320508
    return noise * ramp_factor(array_extents, (1,), ratio) * 0.6 * math.sqrt(TOKENS)


def steps_of(stream_key, shape, cuts, low, high):
    level, own = 1.0, jax.random.fold_in(stream_key, 6)
    for axis_at, shards_of in cuts:
        heights = jnp.exp(jax.random.uniform(jax.random.fold_in(own, axis_at), (shards_of,), jnp.float32, low / len(cuts), high / len(cuts)))
        level = level * jnp.repeat(heights, shape[axis_at] // shards_of).reshape([-1 if axis == axis_at else 1 for axis in range(len(shape))])
    return level


def picks_of(own_key, rows, number_of, top, lift):
    order = jax.random.permutation(jax.random.fold_in(own_key, 1), number_of)
    pull = order
    for power in range(3):
        pull = pull * pull // number_of
    pull = pull * lift // number_of
    chance = jax.random.randint(jax.random.fold_in(own_key, 2), (rows, number_of), 0, 4096) + pull
    sure = jax.random.permutation(jax.random.fold_in(own_key, 3), rows)[jnp.arange(number_of) % rows]
    chance = jnp.where(jnp.arange(rows)[:, None] == sure[None, :], 1 << 14, chance)
    merit = chance * number_of + jnp.arange(number_of)
    return lax.top_k(merit.astype(jnp.int32), top)[1].astype(jnp.int32)


def profile(count, total, limit, slope):
    weights = [(1 << 20) // math.isqrt(standing ** slope) + 1 for standing in range(2, count + 1)]
    rest, holding = total - limit - (count - 1), [1] * (count - 1)
    while rest > 0:
        candidates = [i for i in range(count - 1) if holding[i] < limit]
        whole, budget = sum([weights[i] for i in candidates]), rest
        for i in candidates:
            extra = min(limit - holding[i], max(1, budget * weights[i] // whole), rest)
            holding[i] = holding[i] + extra
            rest = rest - extra
    return np.array([limit] + holding)


def uneven_parts(stream_key, amount, total, bound, skew):
    if amount == 2:
        one = jax.random.randint(stream_key, (), max(1, total - bound), min(bound, total - 1) + 1)
        return jnp.stack([one, total - one])
    tallies = jnp.asarray(profile(amount, total, bound, skew), jnp.int32)
    pairs = (amount - 1) // 2
    source_of, taker = tallies[1:1 + 2 * pairs:2], tallies[2:2 + 2 * pairs:2]
    room = jnp.minimum(source_of - 1, bound - taker)
    passed = jax.random.randint(jax.random.fold_in(stream_key, 1), (pairs,), 0, 1 << 20) % (room + 1)
    tallies = tallies.at[1:1 + 2 * pairs:2].set(source_of - passed).at[2:2 + 2 * pairs:2].set(taker + passed)
    return tallies[jax.random.permutation(jax.random.fold_in(stream_key, 2), amount)]


def scatter_about(own_key, shape, scale, most, shards=(), held_as=jnp.bfloat16):
    loudness = steps_of(own_key, shape, shards, -0.22, 0.18) if shards else 1.0
    result = jax.random.normal(own_key, shape, jnp.float32) * scale * loudness
    return jnp.minimum(jnp.maximum(result, -most), most).astype(held_as)


def setup_inputs(seed: int = 0) -> dict:
    arg_keys = jax.random.split(jax.random.key(seed), 24)
    return {
        "tokens": scatter_about(arg_keys[0], (TOKENS, MODEL_DIM), 1.0, 6.0, ((0, 8),)),
        "cotangent": scatter_about(arg_keys[1], (TOKENS, MODEL_DIM), 1.0, 6.0, ((0, 8),)),
        "segment_ids": jax.vmap(lambda own: jnp.searchsorted(jnp.cumsum(uneven_parts(own, NSEG, TOK, TOK // 2, 0)), jnp.arange(TOK), side="right"))(jax.random.split(arg_keys[2], N_DP)).reshape((N_DP, TOK)).astype(jnp.int32),
        "parents": draw_parents(jax.random.fold_in(arg_keys[23], 71), 0),
        "expert_ids": picks_of(arg_keys[4], TOKENS, EXPERTS, TOP, 4096),
        "gate_weights": jnp.clip(jnp.exp(math.log(0.6) - 1.3862944 * jax.random.uniform(arg_keys[5], (TOKENS, TOP), jnp.float32) ** steps_of(arg_keys[5], (TOKENS, TOP), ((0, 8),), -0.2, 0.2)), 0.15, 0.6),
        "placement_order": jax.vmap(lambda own: jax.random.permutation(own, PAIRS))(jax.random.split(arg_keys[6], N_DP)).reshape((N_DP, PAIRS)).astype(jnp.int32),
        "capacity": draw_capacity(jax.random.fold_in(arg_keys[23], 71), 0),
        "w_qkv": draw_w_qkv(jax.random.fold_in(arg_keys[23], 71), 0),
        "w_out": draw_w_out(jax.random.fold_in(arg_keys[23], 71), 0),
        "w_gate_up": draw_w_gate_up(jax.random.fold_in(arg_keys[23], 71), 0),
        "w_down": draw_w_down(jax.random.fold_in(arg_keys[23], 71), 0),
        "norm_gains": draw_norm_gains(jax.random.fold_in(arg_keys[23], 71), 0),
        "first_qkv": draw_first_qkv(jax.random.fold_in(arg_keys[23], 71), 0),
        "first_out": draw_first_out(jax.random.fold_in(arg_keys[23], 71), 0),
        "first_gate_up": draw_first_gate_up(jax.random.fold_in(arg_keys[23], 71), 0),
        "first_down": draw_first_down(jax.random.fold_in(arg_keys[23], 71), 0),
        "first_gains": draw_first_gains(jax.random.fold_in(arg_keys[23], 71), 0),
        "second_moment_projection": jnp.clip(jnp.exp(math.log(32768.0) - 1.3862944 * jax.random.uniform(arg_keys[18], (MODEL_DIM, KEY_VALUE_HEADS * GROUP_COLUMNS), jnp.float32) ** steps_of(arg_keys[18], (MODEL_DIM, KEY_VALUE_HEADS * GROUP_COLUMNS), ((0, 8), (1, 4)), -0.2, 0.2)), 8192.0, 32768.0),
        "second_out": jnp.clip(jnp.exp(math.log(327.0) - 1.395511 * jax.random.uniform(arg_keys[19], (QUERY_HEADS * HEAD_SIZE, MODEL_DIM), jnp.float32) ** steps_of(arg_keys[19], (QUERY_HEADS * HEAD_SIZE, MODEL_DIM), ((0, 4), (1, 8)), -0.2, 0.2)), 81.0, 327.0),
        "second_gate_up": jnp.clip(jnp.exp(math.log(1474.0) - 1.3876521 * jax.random.uniform(arg_keys[20], (EXPERTS, MODEL_DIM, 2 * FF), jnp.float32) ** steps_of(arg_keys[20], (EXPERTS, MODEL_DIM, 2 * FF), ((0, 4), (1, 8)), -0.2, 0.2)), 368.0, 1474.0),
        "second_down": jnp.clip(jnp.exp(math.log(278.0) - 1.3935146 * jax.random.uniform(arg_keys[21], (EXPERTS, FF, MODEL_DIM), jnp.float32) ** steps_of(arg_keys[21], (EXPERTS, FF, MODEL_DIM), ((0, 4), (2, 8)), -0.2, 0.2)), 69.0, 278.0),
        "second_gains": jnp.clip(jnp.exp(math.log(11796.0) - 1.3862944 * jax.random.uniform(arg_keys[22], (2, MODEL_DIM), jnp.float32) ** steps_of(arg_keys[22], (2, MODEL_DIM), ((1, 8),), -0.2, 0.2)), 2949.0, 11796.0),
    }


NORM_EPS = 1e-06
ROPE_BASE = 10000.0
BETA = 0.5
WEIGHT_DECAY = 0.01
ADAM_EPS = 1e-06
RATE = 0.5
MASKED = -1e+30
HIGHEST = lax.Precision.HIGHEST

@jax.custom_vjp
def low(v):
    return lax.optimization_barrier(v.astype(jnp.bfloat16)).astype(jnp.float32)

@jax.custom_vjp
def low_back(v):
    return v

def low_keep(v):
    return (low(v), None)

def low_pass(kept, grad):
    return (grad,)

def back_keep(v):
    return (v, None)

def back_low(kept, grad):
    return (low(grad),)
low.defvjp(low_keep, low_pass)
low_back.defvjp(back_keep, back_low)

def norm_apply(rows_in, gain):
    return rows_in * lax.rsqrt(lax.optimization_barrier(jnp.mean(rows_in * rows_in, axis=-1, keepdims=True)) + NORM_EPS) * gain

def tree_layout(segment_row, parent_row):
    seg_count = parent_row.shape[0]
    sequence_length = segment_row.shape[0]
    labels = jnp.arange(seg_count, dtype=jnp.int32)
    member = (segment_row[:, None] == labels[None, :]).astype(jnp.int32)
    lengths = lax.optimization_barrier(jnp.sum(member, axis=0)).astype(jnp.int32)
    starts = (jnp.cumsum(lengths) - lengths).astype(jnp.int32)
    ancestor = labels[:, None] == labels[None, :]
    current = labels
    for repeat in range(seg_count):
        current = lax.optimization_barrier(jnp.sum(jnp.where(current[:, None] == labels[None, :], parent_row[None, :], 0), axis=1)).astype(jnp.int32)
        ancestor = ancestor | (current[:, None] == labels[None, :])
    proper = ancestor & (labels[:, None] != labels[None, :])
    above_len = lax.optimization_barrier(jnp.sum(jnp.where(proper, lengths[None, :], 0), axis=1)).astype(jnp.int32)
    offset = lax.optimization_barrier(jnp.sum(member * (above_len - starts)[None, :], axis=1)).astype(jnp.int32)
    position = jnp.arange(sequence_length, dtype=jnp.int32) + offset
    return (member.astype(jnp.float32), ancestor.astype(jnp.float32), position)

def rope_tables(position, head_dim):
    half_dim = head_dim // 2
    frequency = ROPE_BASE ** (-2.0 * jnp.arange(half_dim, dtype=jnp.float32) / head_dim)
    angles = position.astype(jnp.float32)[:, None] * frequency[None, :]
    return (jnp.cos(angles), jnp.sin(angles))

def rotate(source, cos_table, sine_table):
    half_dim = source.shape[-1] // 2
    leading = source[..., :half_dim]
    trailing = source[..., half_dim:]
    return jnp.concatenate([leading * cos_table - trailing * sine_table, trailing * cos_table + leading * sine_table], axis=-1)

def routing(expert_ids, placement_order, capacity, first_expert, local_count, slots, top_count):
    flat_experts = expert_ids.reshape(-1).astype(jnp.int32)
    order_flat = placement_order.reshape(-1).astype(jnp.int32)
    pair_count = flat_experts.shape[0]
    ranked = jnp.zeros((pair_count,), jnp.int32).at[order_flat].set(jnp.arange(pair_count, dtype=jnp.int32))
    ranked_experts = flat_experts[ranked]
    expert_labels = jnp.arange(capacity.shape[0], dtype=jnp.int32)
    limits = lax.optimization_barrier(jnp.sum(jnp.where(ranked_experts[:, None] == expert_labels[None, :], capacity[None, :], 0), axis=1))
    local_labels = jnp.arange(local_count, dtype=jnp.int32)
    local_expert = (ranked_experts - first_expert).astype(jnp.int32)
    member = (local_expert[:, None] == local_labels[None, :]).astype(jnp.int32)
    before = jnp.cumsum(member, axis=0) - member
    slot = lax.optimization_barrier(jnp.sum(before * member, axis=1)).astype(jnp.int32)
    keep = (lax.optimization_barrier(jnp.sum(member, axis=1)) > 0) & (slot < limits)
    dump = local_count * slots
    target = jnp.where(keep, local_expert * slots + slot, dump).astype(jnp.int32)
    pair_table = jnp.zeros((dump + 1,), jnp.int32).at[target].set(ranked)[:dump]
    filled = jnp.zeros((dump + 1,), jnp.int32).at[target].set(1)[:dump]
    token_table = (pair_table // top_count).astype(jnp.int32)
    return (token_table, pair_table, filled)

def attention_block(query_block, row_member, row_start, key_heads, value_heads, member, seg_table):
    rows_per_block = query_block.shape[2]
    sequence_length = key_heads.shape[1]
    reach = jnp.dot(jnp.dot(row_member, seg_table, precision=HIGHEST), member.T, precision=HIGHEST) > 0.5
    causal = jnp.arange(sequence_length, dtype=jnp.int32)[None, :] <= (row_start + jnp.arange(rows_per_block, dtype=jnp.int32))[:, None]
    scores = low_back(jnp.einsum('gqbd,gkd->gqbk', query_block, key_heads, precision=HIGHEST) * query_block.shape[-1] ** (-0.5))
    scores = jnp.where((reach & causal)[None, None], scores, MASKED)
    attn_probs = low(jax.nn.softmax(scores, axis=-1))
    return jnp.einsum('gqbk,gkd->gqbd', attn_probs, value_heads, precision=HIGHEST)

def block_forward(params, inputs_f, member, seg_table, cos_table, sine_table, token_table, filled_float, slot_gate):
    w_qkv, w_out, w_gate_up, w_down, norm_gains = params
    sequence_length = inputs_f.shape[0]
    model_width = inputs_f.shape[1]
    heads_per_group = QUERY_HEADS // KEY_VALUE_HEADS
    normed_one = low(norm_apply(inputs_f, norm_gains[0]))
    mixed_projection = low_back(jnp.dot(normed_one, low(w_qkv), precision=HIGHEST))
    mixed_projection = mixed_projection.reshape(sequence_length, KEY_VALUE_HEADS, heads_per_group + 2, HEAD_SIZE).transpose(1, 2, 0, 3)
    query_rows = low(rotate(mixed_projection[:, :heads_per_group], cos_table, sine_table))
    key_heads = low(rotate(mixed_projection[:, heads_per_group], cos_table, sine_table))
    value_heads = low(mixed_projection[:, heads_per_group + 1])
    rows_per_block = min(512, sequence_length)
    count_of_blocks = sequence_length // rows_per_block
    blocks_of_queries = query_rows.reshape(KEY_VALUE_HEADS, heads_per_group, count_of_blocks, rows_per_block, HEAD_SIZE).transpose(2, 0, 1, 3, 4)
    member_blocks = member.reshape(count_of_blocks, rows_per_block, member.shape[1])
    row_starts = (jnp.arange(count_of_blocks, dtype=jnp.int32) * rows_per_block).astype(jnp.int32)

    def one_block(pieces):
        return attention_block(pieces[0], pieces[1], pieces[2], key_heads, value_heads, member, seg_table)
    attended_blocks = lax.map(jax.checkpoint(one_block), (blocks_of_queries, member_blocks, row_starts))
    heads_flat = low(low_back(attended_blocks.transpose(0, 3, 1, 2, 4).reshape(sequence_length, QUERY_HEADS * HEAD_SIZE)))
    attn_total = low_back(jnp.dot(heads_flat, low(w_out), precision=HIGHEST))
    residual = inputs_f + attn_total
    normed_two = low(norm_apply(residual, norm_gains[1]))
    slot_inputs = (normed_two[token_table] * filled_float[:, None]).reshape(EXPERTS, CAP, model_width)
    gate_up = low_back(jnp.einsum('ecd,edf->ecf', slot_inputs, low(w_gate_up), precision=HIGHEST))
    hidden = low(jax.nn.silu(gate_up[..., :FF]) * gate_up[..., FF:])
    expert_out = low_back(jnp.einsum('ecf,efd->ecd', hidden, low(w_down), precision=HIGHEST))
    weighted = (expert_out * slot_gate[..., None]).reshape(-1, model_width)
    combined = jnp.zeros((sequence_length, model_width), jnp.float32).at[token_table].add(weighted)
    return residual + combined

def lamb_moments(weight, moment_one, moment_two, gradient):
    first_new = BETA * moment_one + (1.0 - BETA) * gradient
    second_new = BETA * moment_two + (1.0 - BETA) * gradient * gradient
    correction = 1.0 - BETA ** STEP
    update = first_new / correction / (jnp.sqrt(second_new / correction) + ADAM_EPS) + WEIGHT_DECAY * weight
    return (first_new, second_new, update)

def square_list(arrays):
    return jnp.stack([jnp.sum(arrays[0] * arrays[0]), jnp.sum(arrays[1] * arrays[1]), jnp.sum(arrays[2] * arrays[2]), jnp.sum(arrays[3] * arrays[3]), jnp.sum(arrays[4][0] * arrays[4][0]), jnp.sum(arrays[4][1] * arrays[4][1])])

def reference(tokens, cotangent, segment_ids, parents, expert_ids, gate_weights, placement_order, capacity, w_qkv, w_out, w_gate_up, w_down, norm_gains, first_qkv, first_out, first_gate_up, first_down, first_gains, second_moment_projection, second_out, second_gate_up, second_down, second_gains):
    params = (w_qkv, w_out, w_gate_up, w_down, norm_gains)
    tree_tokens = tokens.astype(jnp.float32).reshape(N_DP, TOK, MODEL_DIM)
    tree_upstream = cotangent.astype(jnp.float32).reshape(N_DP, TOK, MODEL_DIM)
    tree_experts = expert_ids.reshape(N_DP, TOK, TOP)
    tree_gates = gate_weights.reshape(N_DP, TOK * TOP)

    def per_tree(running, pieces):
        inputs_f, upstream, segment_row, parent_row, expert_tree, gate_row, order_row = pieces
        member, seg_table, position = tree_layout(segment_row, parent_row)
        cos_table, sine_table = rope_tables(position, HEAD_SIZE)
        token_table, pair_table, filled = routing(expert_tree, order_row, capacity, 0, EXPERTS, CAP, TOP)
        filled_float = filled.astype(jnp.float32)
        slot_gate = (gate_row[pair_table] * filled_float).reshape(EXPERTS, CAP)

        def forward(weights, rows_in):
            return block_forward(weights, rows_in, member, seg_table, cos_table, sine_table, token_table, filled_float, slot_gate)
        output, pullback = jax.vjp(forward, params, inputs_f)
        weight_grads, tree_input_grad = pullback(upstream)
        running = jax.tree.map(lambda total_in, term_in: total_in + term_in, running, weight_grads)
        return (running, (output.astype(jnp.bfloat16), tree_input_grad.astype(jnp.bfloat16)))
    starting = jax.tree.map(jnp.zeros_like, params)
    gradients, (outputs, input_grads) = lax.scan(per_tree, starting, (tree_tokens, tree_upstream, segment_ids, parents, tree_experts, tree_gates, placement_order))
    firsts = (first_qkv, first_out, first_gate_up, first_down, first_gains)
    seconds = (second_moment_projection, second_out, second_gate_up, second_down, second_gains)
    next_firsts = []
    next_seconds = []
    updates = []
    for weight, moment_one, moment_two, gradient in zip(params, firsts, seconds, gradients):
        first_new, second_new, update = lamb_moments(weight, moment_one, moment_two, gradient)
        next_firsts.append(first_new)
        next_seconds.append(second_new)
        updates.append(update)
    weight_norms = jnp.sqrt(square_list(params))
    update_norms = jnp.sqrt(square_list(updates))
    trust_ratio = weight_norms / update_norms
    updated = [params[index] - RATE * trust_ratio[index] * updates[index] for index in range(4)]
    updated.append(params[4] - RATE * trust_ratio[4:6][:, None] * updates[4])
    trust_norms = jnp.stack([weight_norms, update_norms], axis=1)
    return (outputs.reshape(TOKENS, MODEL_DIM), input_grads.reshape(TOKENS, MODEL_DIM), updated[0], updated[1], updated[2], updated[3], updated[4], next_firsts[0], next_firsts[1], next_firsts[2], next_firsts[3], next_firsts[4], next_seconds[0], next_seconds[1], next_seconds[2], next_seconds[3], next_seconds[4], trust_norms)
```

```python
import jax
import jax.numpy as jnp
from jax import lax
from jax.experimental import pallas as pl
from jax.experimental.pallas import tpu as pltpu
from jax.sharding import PartitionSpec as P

QUERY_HEADS = 24
KEY_VALUE_HEADS = 8
PER_GROUP = QUERY_HEADS // KEY_VALUE_HEADS
HEAD_SIZE = 64
HALF = HEAD_SIZE // 2
TOP = 8
STEP = 3
GROUP_COLUMNS = 320

NORM_EPS = 1e-06
ROPE_BASE = 10000.0
BETA = 0.5
WEIGHT_DECAY = 0.01
ADAM_EPS = 1e-06
RATE = 0.5
MASKED = -1e30

ROWS = 256
MIB = 1 << 20
F32 = jnp.float32
LOW = jnp.bfloat16


def dot(a, b):
    return jnp.dot(a, b, preferred_element_type=F32)


def dot_nt(a, b):
    return lax.dot_general(a, b, (((1,), (1,)), ((), ())), preferred_element_type=F32)


def dot_tn(a, b):
    return lax.dot_general(a, b, (((0,), (0,)), ((), ())), preferred_element_type=F32)


def params(mib):
    return pltpu.CompilerParams(vmem_limit_bytes=mib * MIB)


def prep_kernel(
    parents_ref, capacity_ref, first_ref, row_ref, col_ref, freq_ref, ids_ref, order_ref,
    cos_ref, sin_ref, bias_ref, limit_ref,
):
    seg_count = parents_ref.shape[1]
    row = row_ref[...]
    bits = []
    lengths = []
    for s in range(seg_count):
        current = jnp.int32(s)
        mask = jnp.int32(1 << s)
        for repeat in range(seg_count):
            current = parents_ref[0, current]
            mask = mask | (jnp.int32(1) << current)
        bits.append(mask)
        lengths.append(jnp.sum((row == s).astype(jnp.int32), axis=1, keepdims=True))
    start = jnp.zeros((1, 1), jnp.int32)
    offset = jnp.zeros(row.shape, jnp.int32)
    reach = jnp.zeros(row.shape, jnp.int32)
    for s in range(seg_count):
        above = jnp.zeros((1, 1), jnp.int32)
        for a in range(seg_count):
            if a != s:
                above = above + lengths[a] * ((bits[s] >> a) & 1)
        offset = jnp.where(row == s, above - start, offset)
        reach = jnp.where(row == s, bits[s], reach)
        start = start + lengths[s]
    position = lax.broadcasted_iota(jnp.int32, row.shape, 1) + offset
    angles = position.astype(F32) * freq_ref[...]
    cos_ref[...] = jnp.cos(angles)
    sin_ref[...] = jnp.sin(angles)
    tok = row.shape[1]
    for block in range(tok // ROWS):
        lo = block * ROWS
        col = col_ref[lo : lo + ROWS]
        key = lax.broadcasted_iota(jnp.int32, (ROWS, tok), 0) + lo
        query = lax.broadcasted_iota(jnp.int32, (ROWS, tok), 1)
        seen = (jnp.right_shift(reach, col) & 1) > 0
        bias_ref[lo : lo + ROWS] = jnp.where(seen & (key <= query), 0.0, MASKED)
    ids = ids_ref[...]
    order = order_ref[...]
    pairs = ids.shape[0] * ids.shape[1]
    own = []
    caps = []
    limits = []
    for e in range(limit_ref.shape[0]):
        label = first_ref[0] + e
        own.append(jnp.where(ids == label, order, pairs))
        caps.append(capacity_ref[label])
        limits.append(jnp.zeros((1, 1), jnp.int32))
    step = pairs
    while step > 1:
        step //= 2
        for e in range(len(own)):
            trial = limits[e] + step
            count = jnp.sum((own[e] < trial).astype(jnp.int32), axis=(0, 1), keepdims=True)
            limits[e] = jnp.where(count < caps[e], trial, limits[e])
    for e in range(len(own)):
        limit_ref[e : e + 1] = jnp.broadcast_to(limits[e], (1, limit_ref.shape[1]))


def prepare(segment_ids, parents, expert_ids, placement_order, capacity, first_expert, local_count):
    tok = segment_ids.shape[1]
    frequency = ROPE_BASE ** (-2.0 * jnp.arange(HALF, dtype=F32) / HEAD_SIZE)
    smem = pl.BlockSpec(memory_space=pltpu.SMEM)
    vmem = pl.BlockSpec(memory_space=pltpu.VMEM)
    return pl.pallas_call(
        prep_kernel,
        in_specs=[smem, smem, smem, vmem, vmem, vmem, vmem, vmem],
        out_specs=[vmem] * 4,
        out_shape=[
            jax.ShapeDtypeStruct((HALF, tok), F32),
            jax.ShapeDtypeStruct((HALF, tok), F32),
            jax.ShapeDtypeStruct((tok, tok), F32),
            jax.ShapeDtypeStruct((local_count, 128), jnp.int32),
        ],
        compiler_params=params(32),
        name="prepare",
    )(
        parents,
        capacity,
        first_expert.reshape(1),
        segment_ids,
        segment_ids.reshape(tok, 1),
        frequency.reshape(HALF, 1),
        expert_ids.reshape(-1, 128),
        placement_order.reshape(-1, 128),
    )


def rotate(source, cos, sin):
    a = source[:HALF]
    b = source[HALF:]
    return jnp.concatenate([a * cos - b * sin, b * cos + a * sin], 0)


def rotate_back(source, cos, sin):
    a = source[:HALF]
    b = source[HALF:]
    return jnp.concatenate([a * cos + b * sin, b * cos - a * sin], 0)


def probabilities(keys, query_t, bias):
    scores = dot(keys, query_t) + bias
    top = jnp.max(scores, axis=0, keepdims=True)
    raised = jnp.exp(scores - top)
    return raised * (1.0 / jnp.sum(raised, axis=0, keepdims=True))


SCALE = HEAD_SIZE**-0.5


def forward_kernel(n1_ref, w_ref, cos_ref, sin_ref, bias_ref, out_ref, out_t):
    tok = n1_ref.shape[0]
    groups = w_ref.shape[1] // GROUP_COLUMNS
    mixed = dot(n1_ref[...], w_ref[...].astype(LOW)).T
    cos = cos_ref[...]
    sin = sin_ref[...]
    for g in range(groups):
        base = g * GROUP_COLUMNS
        at_key = base + PER_GROUP * HEAD_SIZE
        at_value = at_key + HEAD_SIZE
        keys = rotate(mixed[at_key:at_value], cos, sin).T.astype(LOW)
        value_t = mixed[at_value : at_value + HEAD_SIZE].astype(LOW)
        for h in range(PER_GROUP):
            lo = base + h * HEAD_SIZE
            query_t = rotate(mixed[lo : lo + HEAD_SIZE], cos, sin).astype(LOW) * SCALE
            query_t = query_t.astype(LOW)
            at = (g * PER_GROUP + h) * HEAD_SIZE
            for block in range(tok // ROWS):
                q0 = block * ROWS
                ext = q0 + ROWS
                probs = probabilities(
                    keys[:ext], query_t[:, q0:ext], bias_ref[:ext, q0:ext]
                ).astype(LOW)
                out_t[at : at + HEAD_SIZE, q0:ext] = dot(value_t[:, :ext], probs)
    out_ref[...] = out_t[...].T.astype(LOW).astype(F32)


def attention_forward(n1, w_slices, cos, sin, bias):
    slices, width, cols = w_slices.shape
    tok = n1.shape[0]
    heads = cols // GROUP_COLUMNS * PER_GROUP * HEAD_SIZE
    whole = lambda *shape: pl.BlockSpec(shape, lambda t: (0,) * len(shape))
    return pl.pallas_call(
        forward_kernel,
        grid=(slices,),
        in_specs=[
            whole(tok, width),
            pl.BlockSpec((None, width, cols), lambda t: (t, 0, 0)),
            whole(HALF, tok),
            whole(HALF, tok),
            whole(tok, tok),
        ],
        out_specs=pl.BlockSpec((None, tok, heads), lambda t: (t, 0, 0)),
        out_shape=jax.ShapeDtypeStruct((slices, tok, heads), F32),
        scratch_shapes=[pltpu.VMEM((heads, tok), F32)],
        compiler_params=params(56),
        name="attention_forward",
    )(n1, w_slices, cos, sin, bias)


def out_kernel(heads_ref, w_ref, x_ref, gain_ref, res_ref, n2_ref, low_ref):
    @pl.when(pl.program_id(0) == 0)
    def _():
        shares, slices, rows, _ = w_ref.shape
        for t in range(slices):
            for d in range(shares):
                at = (t * shares + d) * rows
                low_ref[at : at + rows] = w_ref[d, t].astype(LOW)

    part = heads_ref.shape[2]
    attn = dot(heads_ref[0].astype(LOW), low_ref[:part])
    for t in range(1, heads_ref.shape[0]):
        attn = attn + dot(heads_ref[t].astype(LOW), low_ref[t * part : (t + 1) * part])
    total = x_ref[...].astype(F32) + attn
    res_ref[...] = total
    s = lax.rsqrt(jnp.mean(total * total, axis=-1, keepdims=True) + NORM_EPS)
    n2_ref[...] = (total * s * gain_ref[...]).astype(LOW)


def out_projection(heads, w_out, x, gain):
    slices, tok, part = heads.shape
    width = x.shape[1]
    rows = pl.BlockSpec((ROWS, width), lambda i: (i, 0))
    weights = pl.BlockSpec((slices * part, width), lambda i: (0, 0))
    return pl.pallas_call(
        out_kernel,
        grid=(tok // ROWS,),
        in_specs=[
            pl.BlockSpec((slices, ROWS, part), lambda i: (0, i, 0)),
            pl.BlockSpec(w_out.shape, lambda i: (0, 0, 0, 0)),
            rows,
            pl.BlockSpec((1, width), lambda i: (0, 0)),
        ],
        out_specs=[rows, rows, weights],
        out_shape=[
            jax.ShapeDtypeStruct((tok, width), F32),
            jax.ShapeDtypeStruct((tok, width), LOW),
            jax.ShapeDtypeStruct((slices * part, width), LOW),
        ],
        compiler_params=params(56),
        name="out_projection",
    )(heads, w_out, x, gain)


def expert_column(weights, e):
    lane = lax.broadcasted_iota(jnp.int32, weights.shape, 1)
    return jnp.sum(jnp.where(lane == e, weights, 0.0), axis=1, keepdims=True)


def expert_kernel(n2_ref, dy_ref, we_ref, wgu_ref, wd_ref, *refs):
    out_ref, dn2_ref, hid_ref, dgu_ref = refs[-4:]
    e = pl.program_id(0)
    ff = wd_ref.shape[0]
    weight = expert_column(we_ref[...], e)
    kept = weight > 0.0
    wgu = wgu_ref[...]
    wd = wd_ref[...]
    gate_up = dot(n2_ref[...], wgu)
    gate = gate_up[:, :ff]
    up = gate_up[:, ff:]
    sig = 1.0 / (1.0 + jnp.exp(-gate))
    silu = gate * sig
    hidden = jnp.where(kept, silu * up, 0.0).astype(LOW)
    hid_ref[...] = hidden
    out = weight * dot(hidden, wd)
    d_out = (weight * dy_ref[...].astype(F32)).astype(LOW)
    d_hidden = dot_nt(d_out, wd)
    d_gate = d_hidden * up * sig * (1.0 + gate * (1.0 - sig))
    d_up = d_hidden * silu
    d_gate_up = jnp.where(kept, jnp.concatenate([d_gate, d_up], 1), 0.0).astype(LOW)
    dgu_ref[...] = d_gate_up
    d_n2 = dot_nt(d_gate_up, wgu)

    @pl.when(e == 0)
    def _():
        out_ref[...] = out
        dn2_ref[...] = d_n2

    @pl.when(e > 0)
    def _():
        out_ref[...] += out
        dn2_ref[...] += d_n2


def experts(chunk, n2, dy, weights, wgu, wd, kept):
    tok, width = n2.shape
    count, ff, _ = wd.shape
    wide = pl.BlockSpec((ROWS, width), lambda e: (chunk, 0))
    first = pl.BlockSpec((ROWS, width), lambda e: (0, 0))
    return pl.pallas_call(
        expert_kernel,
        grid=(count,),
        in_specs=[
            wide,
            wide,
            pl.BlockSpec((ROWS, count), lambda e: (chunk, 0)),
            pl.BlockSpec((None, width, 2 * ff), lambda e: (e, 0, 0)),
            pl.BlockSpec((None, ff, width), lambda e: (e, 0, 0)),
            *[pl.BlockSpec(memory_space=pl.ANY) for _ in kept],
        ],
        out_specs=[
            first,
            first,
            pl.BlockSpec((None, ROWS, ff), lambda e: (e, chunk, 0)),
            pl.BlockSpec((None, ROWS, 2 * ff), lambda e: (e, chunk, 0)),
        ],
        out_shape=[
            jax.ShapeDtypeStruct((ROWS, width), F32),
            jax.ShapeDtypeStruct((ROWS, width), F32),
            jax.ShapeDtypeStruct((count, tok, ff), LOW),
            jax.ShapeDtypeStruct((count, tok, 2 * ff), LOW),
        ],
        input_output_aliases={5 + i: 2 + i for i in range(len(kept))},
        compiler_params=params(56),
        name="experts",
    )(n2, dy, weights, wgu, wd, *kept)


def split_store(out_ref, lo, value):
    rows = out_ref.shape[1]
    cols = slice(lo, lo + value.shape[1])
    for i in range(out_ref.shape[0]):
        out_ref[i, :, cols] = value[i * rows : (i + 1) * rows]


def grad_kernel(left_ref, right_ref, out_ref):
    split_store(out_ref, 0, dot_tn(left_ref[...], right_ref[...]))


def weight_grads(left, right, shares):
    tok, width = left.shape
    cols = right.shape[1]
    share = width // shares
    parts = shares // 2
    return pl.pallas_call(
        grad_kernel,
        grid=(shares // parts,),
        in_specs=[
            pl.BlockSpec((tok, parts * share), lambda i: (0, i)),
            pl.BlockSpec((tok, cols), lambda i: (0, 0)),
        ],
        out_specs=pl.BlockSpec((parts, share, cols), lambda i: (i, 0, 0)),
        out_shape=jax.ShapeDtypeStruct((shares, share, cols), F32),
        compiler_params=params(56),
        name="weight_grads",
    )(left, right)


def expert_grad_kernel(n2_ref, dy_ref, we_ref, dgu_ref, hid_ref, out_ref):
    weight = expert_column(we_ref[...], pl.program_id(0))
    d_out = (weight * dy_ref[...].astype(F32)).astype(LOW)
    split_store(out_ref, 0, dot_tn(n2_ref[...], dgu_ref[...]))
    split_store(out_ref, dgu_ref.shape[1], dot_tn(d_out, hid_ref[...]))


def expert_grads(n2, dy, weights, d_gate_up, hidden, shares):
    tok, width = n2.shape
    count, _, wide = d_gate_up.shape
    ff = hidden.shape[2]
    share = width // shares
    parts = shares // 2
    rows = pl.BlockSpec((tok, parts * share), lambda e, i: (0, i))
    return pl.pallas_call(
        expert_grad_kernel,
        grid=(count, shares // parts),
        in_specs=[
            rows,
            rows,
            pl.BlockSpec(weights.shape, lambda e, i: (0, 0)),
            pl.BlockSpec((None, tok, wide), lambda e, i: (e, 0, 0)),
            pl.BlockSpec((None, tok, ff), lambda e, i: (e, 0, 0)),
        ],
        out_specs=pl.BlockSpec((parts, None, share, wide + ff), lambda e, i: (i, e, 0, 0)),
        out_shape=jax.ShapeDtypeStruct((shares, count, share, wide + ff), F32),
        compiler_params=params(56),
        name="expert_grads",
    )(n2, dy, weights, d_gate_up, hidden)


def heads_kernel(n1_ref, w_ref, cos_ref, sin_ref, low_ref, qt_ref, q_ref, kt_ref, k_ref, v_ref):
    cols = w_ref.shape[-1]
    w_low = w_ref[...].reshape(-1, cols).astype(LOW)
    low_ref[...] = w_low
    mixed = dot(n1_ref[...], w_low).T
    cos = cos_ref[...]
    sin = sin_ref[...]
    queries = []
    keys = []
    values = []
    for g in range(cols // GROUP_COLUMNS):
        base = g * GROUP_COLUMNS
        for h in range(PER_GROUP):
            lo = base + h * HEAD_SIZE
            queries.append(rotate(mixed[lo : lo + HEAD_SIZE], cos, sin))
        at_key = base + PER_GROUP * HEAD_SIZE
        at_value = at_key + HEAD_SIZE
        keys.append(rotate(mixed[at_key:at_value], cos, sin))
        values.append(mixed[at_value : at_value + HEAD_SIZE])
    queries = jnp.concatenate(queries, 0)
    keys = jnp.concatenate(keys, 0)
    qt_ref[...] = (queries.astype(LOW) * SCALE).astype(LOW)
    q_ref[...] = queries.T.astype(LOW)
    kt_ref[...] = keys.astype(LOW)
    k_ref[...] = keys.T.astype(LOW)
    v_ref[...] = jnp.concatenate(values, 0).T.astype(LOW)


def all_heads(n1, w_slices, cos, sin):
    shares, slices, rows, cols = w_slices.shape
    tok, width = n1.shape
    groups = cols // GROUP_COLUMNS
    keys = groups * HEAD_SIZE
    queries = keys * PER_GROUP
    shapes = [(width, cols), (queries, tok), (tok, queries), (keys, tok), (tok, keys), (tok, keys)]
    whole = lambda *shape: pl.BlockSpec(shape, lambda t: (0,) * len(shape))
    return pl.pallas_call(
        heads_kernel,
        grid=(slices,),
        in_specs=[
            whole(tok, width),
            pl.BlockSpec((shares, None, rows, cols), lambda t: (0, t, 0, 0)),
            whole(HALF, tok),
            whole(HALF, tok),
        ],
        out_specs=[pl.BlockSpec((None, *shape), lambda t: (t, 0, 0)) for shape in shapes],
        out_shape=[jax.ShapeDtypeStruct((slices, *shape), LOW) for shape in shapes],
        compiler_params=params(56),
        name="all_heads",
    )(n1, w_slices, cos, sin)


def norm_terms(rows_in, gain, upstream):
    s = lax.rsqrt(jnp.mean(rows_in * rows_in, axis=-1, keepdims=True) + NORM_EPS)
    pulled = upstream * gain
    inner = jnp.mean(rows_in * pulled, axis=-1, keepdims=True)
    grad = s * pulled - rows_in * (s * s * s) * inner
    return grad, jnp.sum(upstream * rows_in * s, axis=0, keepdims=True)


def backward_kernel(
    dn2_ref, res_ref, dy_ref, x_ref, gains_ref, low_ref, wo_ref, qt_ref, q_ref, kt_ref, k_ref,
    v_ref, cos_ref, sin_ref, bias_ref, *refs,
):
    later = len(refs) > 10
    d_gains_ref, dattn_ref, igrad_ref, dmix_ref, dk_ref, dv_ref = refs[-10:-4]
    dmix_t, dres_ref, dn1_ref, low_dattn = refs[-4:]
    t = pl.program_id(0)
    last = pl.num_programs(0) - 1
    ext = bias_ref.shape[0]
    old = ext - ROWS

    @pl.when(t == 0)
    def _():
        grad, gain = norm_terms(res_ref[...], gains_ref[1:2], dn2_ref[...])
        grad = grad + dy_ref[...].astype(F32)
        dres_ref[...] = grad
        low_dattn[...] = grad.astype(LOW)
        dattn_ref[...] = grad.astype(LOW)
        d_gains_ref[1:2] = gain

    d_heads = dot_nt(low_dattn[...], wo_ref[...])
    d_heads_t = d_heads.T.astype(LOW)
    d_heads = d_heads.astype(LOW)
    cos = cos_ref[...]
    sin = sin_ref[...]
    bias = bias_ref[...]
    for g in range(k_ref.shape[1] // HEAD_SIZE):
        at_g = g * HEAD_SIZE
        keys = k_ref[:, at_g : at_g + HEAD_SIZE]
        keys_t = kt_ref[at_g : at_g + HEAD_SIZE]
        values = v_ref[:, at_g : at_g + HEAD_SIZE]
        d_keys = jnp.zeros((ext, HEAD_SIZE), F32)
        d_values = jnp.zeros((ext, HEAD_SIZE), F32)
        base = g * GROUP_COLUMNS
        for h in range(PER_GROUP):
            at = (g * PER_GROUP + h) * HEAD_SIZE
            probs = probabilities(keys, qt_ref[at : at + HEAD_SIZE], bias)
            d_probs = dot(values, d_heads_t[at : at + HEAD_SIZE])
            delta = jnp.sum(probs * d_probs, axis=0, keepdims=True)
            d_scores = (probs * (d_probs - delta)).astype(LOW)
            d_query = dot(keys_t, d_scores) * SCALE
            d_keys = d_keys + dot(d_scores, q_ref[:, at : at + HEAD_SIZE])
            d_values = d_values + dot(probs.astype(LOW), d_heads[:, at : at + HEAD_SIZE])
            lo = base + h * HEAD_SIZE
            dmix_t[lo : lo + HEAD_SIZE] = rotate_back(d_query, cos, sin)
        if later:
            dk_in, dv_in = refs[-12:-10]
            d_keys = d_keys + dk_in[:, at_g : at_g + HEAD_SIZE]
            d_values = d_values + dv_in[:, at_g : at_g + HEAD_SIZE]
        if old:
            dk_ref[:, at_g : at_g + HEAD_SIZE] = d_keys
            dv_ref[:, at_g : at_g + HEAD_SIZE] = d_values
        at_key = base + PER_GROUP * HEAD_SIZE
        at_value = at_key + HEAD_SIZE
        dmix_t[at_key:at_value] = rotate_back(d_keys[old:].T * SCALE, cos, sin)
        dmix_t[at_value : at_value + HEAD_SIZE] = d_values[old:].T
    d_mixed = dmix_t[...].T.astype(LOW)
    dmix_ref[...] = d_mixed
    part = dot_nt(d_mixed, low_ref[...])

    @pl.when(t == 0)
    def _():
        dn1_ref[...] = part

    @pl.when(t > 0)
    def _():
        dn1_ref[...] += part

    @pl.when(t == last)
    def _():
        grad, gain = norm_terms(x_ref[...].astype(F32), gains_ref[0:1], dn1_ref[...])
        igrad_ref[...] = (dres_ref[...] + grad).astype(LOW)
        d_gains_ref[0:1] = gain


def attention_backward(chunk, dn2, residual, dy, x, gains, heads, wo, cos, sin, bias, done):
    low, qt, q, kt, k, v = heads
    slices, width, cols = low.shape
    tok, keys = k.shape[1:]
    queries = q.shape[2]
    ext = (chunk + 1) * ROWS
    rows = pl.BlockSpec((ROWS, width), lambda t: (chunk, 0))
    first = pl.BlockSpec((ROWS, width), lambda t: (0, 0))
    sums = pl.BlockSpec((None, ext, keys), lambda t: (t, 0, 0))
    angles = pl.BlockSpec((HALF, ROWS), lambda t: (0, chunk))
    anywhere = pl.BlockSpec(memory_space=pl.ANY)
    part = lambda *shape: pl.BlockSpec((None, *shape), lambda t: (t, 0, 0))
    done_specs = [anywhere, anywhere, anywhere, sums, sums][: len(done)]
    return pl.pallas_call(
        backward_kernel,
        grid=(slices,),
        in_specs=[
            first,
            rows,
            rows,
            rows,
            pl.BlockSpec(gains.shape, lambda t: (0, 0)),
            part(width, cols),
            pl.BlockSpec((queries, width), lambda t: (t, 0)),
            pl.BlockSpec((None, queries, ROWS), lambda t: (t, 0, chunk)),
            pl.BlockSpec((None, ROWS, queries), lambda t: (t, chunk, 0)),
            part(keys, ext),
            part(ext, keys),
            part(ext, keys),
            angles,
            angles,
            pl.BlockSpec((ext, ROWS), lambda t: (0, chunk)),
            *done_specs,
        ],
        out_specs=[
            pl.BlockSpec(gains.shape, lambda t: (0, 0)),
            rows,
            rows,
            pl.BlockSpec((None, ROWS, cols), lambda t: (t, chunk, 0)),
            sums,
            sums,
        ],
        out_shape=[
            jax.ShapeDtypeStruct(gains.shape, F32),
            jax.ShapeDtypeStruct((tok, width), LOW),
            jax.ShapeDtypeStruct((tok, width), LOW),
            jax.ShapeDtypeStruct((slices, tok, cols), LOW),
            jax.ShapeDtypeStruct((slices, tok, keys), F32),
            jax.ShapeDtypeStruct((slices, tok, keys), F32),
        ],
        scratch_shapes=[
            pltpu.VMEM((cols, ROWS), F32),
            pltpu.VMEM((ROWS, width), F32),
            pltpu.VMEM((ROWS, width), F32),
            pltpu.VMEM((ROWS, width), LOW),
        ],
        input_output_aliases={15 + i: 1 + i for i in range(len(done))},
        compiler_params=params(56),
        name="attention_backward",
    )(dn2, residual, dy, x, gains, low, wo, qt, q, kt, k, v, cos, sin, bias, *done)


def gather_heads(own, index, count, meanwhile):
    if count != 4:
        return lax.all_gather(own, "tensor"), meanwhile
    up = [own]
    down = [own]
    for hop in range(1, count):
        if hop == count - 1:
            up[-1], down[-1], meanwhile = lax.optimization_barrier((up[-1], down[-1], meanwhile))
        up.append(lax.ppermute(up[-1], "tensor", [(i, i + 1) for i in range(hop - 1, count - 1)]))
        down.append(
            lax.ppermute(down[-1], "tensor", [(i + 1, i) for i in range(count - hop)])
        )
    gathered = []
    for j in range(count):
        value = own
        for i in range(count):
            if i != j:
                value = jnp.where(index == i, up[i - j] if i > j else down[j - i], value)
        gathered.append(value)
    return jnp.stack(gathered), meanwhile


class Totals:
    def __init__(self, index, count):
        self.count = count
        self.inner = (index == 1) | (index == 2)
        self.summed = None
        self.total = None

    def step(self, piece, work, *inputs):
        flight = (piece, self.summed, self.total, inputs)
        piece, summed, total, inputs = lax.optimization_barrier(flight)
        if self.count != 4:
            made = work(*inputs)
            added = None if piece is None else lax.psum(piece, "tensor")
            done, self.total, self.summed = total, summed, added
        else:
            if piece is not None:
                end = lax.ppermute(piece, "tensor", [(0, 1), (3, 2)])
            if summed is not None:
                across = lax.ppermute(summed, "tensor", [(1, 2), (2, 1)])
            if total is not None:
                out = lax.ppermute(total, "tensor", [(1, 0), (2, 3)])
            made = work(*inputs)
            done = None if total is None else jnp.where(self.inner, total, out)
            self.total = None if summed is None else summed + across
            self.summed = None if piece is None else piece + end
        landed = (done, self.summed, self.total, made)
        done, self.summed, self.total, made = lax.optimization_barrier(landed)
        return done, made


def lamb_moments(weight, moment_one, moment_two, gradient):
    first_new = BETA * moment_one + (1.0 - BETA) * gradient
    second_new = BETA * moment_two + (1.0 - BETA) * gradient * gradient
    correction = 1.0 - BETA**STEP
    update = (
        first_new / correction / (jnp.sqrt(second_new / correction) + ADAM_EPS)
        + WEIGHT_DECAY * weight
    )
    return (first_new, second_new, update)


def body(
    tokens, cotangent, segment_ids, parents, expert_ids, gate_weights, placement_order, capacity,
    w_qkv, w_out, w_gate_up, w_down, norm_gains,
    first_qkv, first_out, first_gate_up, first_down, first_gains,
    second_moment_projection, second_out, second_gate_up, second_down, second_gains,
):
    tok, width = tokens.shape
    local_experts = w_gate_up.shape[0]
    tensor_index = lax.axis_index("tensor")
    tensor_count = lax.axis_size("tensor")
    data_index = lax.axis_index("dp")
    data_count = lax.axis_size("dp")
    owner_mask = (tensor_index == 0).astype(F32)
    share = tok // tensor_count

    def own_slice(source, axis_dim):
        share_len = source.shape[axis_dim] // data_count
        return lax.dynamic_slice_in_dim(source, data_index * share_len, share_len, axis_dim)

    def own_rows(source):
        return lax.dynamic_slice_in_dim(source, tensor_index * share, share, 0)

    def square_sums(arrays):
        return jnp.stack(
            [
                jnp.sum(arrays[0] * arrays[0]),
                jnp.sum(arrays[1] * arrays[1]),
                jnp.sum(arrays[2] * arrays[2]),
                jnp.sum(arrays[3] * arrays[3]),
                owner_mask * jnp.sum(arrays[4][0] * arrays[4][0]),
                owner_mask * jnp.sum(arrays[4][1] * arrays[4][1]),
            ]
        )

    weight_shards = (
        own_slice(w_qkv, 0),
        own_slice(w_out, 1),
        own_slice(w_gate_up, 1),
        own_slice(w_down, 2),
        own_slice(norm_gains, 1),
    )
    first_expert = tensor_index * local_experts
    cos, sin, bias, limits = prepare(
        segment_ids, parents, expert_ids, placement_order, capacity, first_expert, local_experts
    )
    local_ids = expert_ids - first_expert
    order = placement_order.reshape(expert_ids.shape)
    columns = []
    for e in range(local_experts):
        kept = (local_ids == e) & (order <= limits[e, 0])
        columns.append(jnp.sum(jnp.where(kept, gate_weights, 0.0), axis=1))
    expert_weights = jnp.stack(columns, axis=1)

    inputs_f = tokens.astype(F32)
    gain_attn = norm_gains[0]
    gain_ffn = norm_gains[1]
    s_one = lax.rsqrt(jnp.mean(inputs_f * inputs_f, axis=-1, keepdims=True) + NORM_EPS)
    n1 = (inputs_f * s_one * gain_attn).astype(LOW)
    out_shares = lax.all_gather(own_slice(w_out, 0), "tensor")
    heads_own = attention_forward(n1, w_qkv[None], cos, sin, bias)[0]
    heads_own, out_shares = lax.optimization_barrier((heads_own, out_shares))
    all_out = lax.all_gather(out_shares, "dp")
    heads, all_out = gather_heads(heads_own, tensor_index, tensor_count, all_out)
    heads, qkv_share = lax.optimization_barrier((heads, weight_shards[0]))
    qkv_shares = lax.all_gather(qkv_share, "tensor")
    residual, n2, wo_low = out_projection(heads, all_out, tokens, norm_gains[1:2])
    wgu_low = w_gate_up.astype(LOW)
    wd_low = w_down.astype(LOW)

    chunks = tok // ROWS
    totals = Totals(tensor_index, tensor_count)

    def expert_chunk(c, n2, kept):
        return experts(c, n2, cotangent, expert_weights, wgu_low, wd_low, kept)

    def expert_chunks(n2, kept):
        parts = []
        for c in reversed(range(chunks - 1)):
            out_part, dn2_part, *kept = expert_chunk(c, n2, kept)
            parts.append((out_part, dn2_part))
        return parts, kept

    def scattered(source):
        return lax.psum_scatter(source, "dp", tiled=True)[0]

    def back_chunk(c, dn2, projected, done):
        return attention_backward(
            c, dn2, residual, cotangent, tokens, norm_gains, projected, wo_low, cos, sin, bias, done
        )

    out_part, dn2_part, *kept = expert_chunk(chunks - 1, n2, ())
    outs = [out_part]
    dn2_part, qkv_shares = lax.optimization_barrier((dn2_part, qkv_shares))
    all_qkv = lax.all_gather(qkv_shares, "dp")
    _, (parts, kept) = totals.step(dn2_part, expert_chunks, n2, kept)
    pieces = [dn2_part for _, dn2_part in parts] + outs + [out_part for out_part, _ in parts]
    hidden, d_gate_up = kept

    def first_work(n2, d_gate_up, hidden):
        return expert_grads(n2, cotangent, expert_weights, d_gate_up, hidden, data_count)

    _, grads = totals.step(pieces.pop(0), first_work, n2, d_gate_up, hidden)
    expert_shard = scattered(grads)
    dn2, projected = totals.step(
        pieces.pop(0), lambda w: all_heads(n1, w, cos, sin), all_qkv
    )
    done = ()
    grad_gains = 0.0
    moe = []
    for c in reversed(range(chunks)):
        total, (d_gains, *done) = totals.step(
            pieces.pop(0), lambda *given: back_chunk(c, *given), dn2, projected, done
        )
        if c:
            dn2 = total
        else:
            moe.append(total)
        grad_gains = grad_gains + d_gains
    d_attn, input_grad, d_mixed = done[:3]

    def last_grads(d_attn, d_mixed):
        own_mixed = lax.dynamic_index_in_dim(d_mixed, tensor_index, 0, False)
        return (
            weight_grads(n1, own_mixed, data_count),
            weight_grads(d_attn, heads_own.astype(LOW), data_count),
        )

    piece = pieces.pop(0) if pieces else None
    total, (grad_qkv, grad_out_t) = totals.step(piece, last_grads, d_attn, d_mixed)
    moe.append(total)
    grad_qkv, expert_shard = lax.optimization_barrier((grad_qkv, expert_shard))
    while len(moe) < chunks:
        piece = pieces.pop(0) if pieces else None
        total, _ = totals.step(piece, lambda: ())
        moe.append(total)
    block_out = jnp.concatenate(
        [
            (residual[c * ROWS : (c + 1) * ROWS] + moe[chunks - 1 - c]).astype(LOW)
            for c in range(chunks)
        ]
    )
    grad_gains = grad_gains.reshape(2, data_count, -1).transpose(1, 0, 2)
    share = grad_gains.shape[-1]
    cols = grad_qkv.shape[-1] + grad_out_t.shape[-1]
    grad_gains = jnp.pad(grad_gains, ((0, 0), (0, 6), (0, cols - share)))
    late = jnp.concatenate([jnp.concatenate([grad_qkv, grad_out_t], 2), grad_gains], 1)

    wide = w_gate_up.shape[2]
    late = scattered(late)
    grad_shards = (
        late[:share, : w_qkv.shape[1]],
        late[:share, w_qkv.shape[1] :].T,
        expert_shard[:, :, :wide],
        expert_shard[:, :, wide:].transpose(0, 2, 1),
        late[share : share + 2, :share],
    )
    firsts = (first_qkv, first_out, first_gate_up, first_down, first_gains)
    seconds = (second_moment_projection, second_out, second_gate_up, second_down, second_gains)
    next_firsts = []
    next_seconds = []
    updates = []
    for weight, moment_one, moment_two, gradient in zip(
        weight_shards, firsts, seconds, grad_shards
    ):
        first_new, second_new, update = lamb_moments(weight, moment_one, moment_two, gradient)
        next_firsts.append(first_new)
        next_seconds.append(second_new)
        updates.append(update)
    weight_squares, update_squares = lax.psum(
        (square_sums(weight_shards), square_sums(updates)), ("dp", "tensor")
    )
    weight_norms = jnp.sqrt(weight_squares)
    update_norms = jnp.sqrt(update_squares)
    trust_ratio = weight_norms / update_norms
    updated = [
        weight_shards[index] - RATE * trust_ratio[index] * updates[index] for index in range(4)
    ]
    updated.append(weight_shards[4] - RATE * trust_ratio[4:6][:, None] * updates[4])
    trust_norms = jnp.stack([weight_norms, update_norms], axis=1)
    return (block_out, input_grad, *updated, *next_firsts, *next_seconds, trust_norms)


def solution(mesh):
    moments = (
        P("dp", "tensor"),
        P("tensor", "dp"),
        P("tensor", "dp", None),
        P("tensor", None, "dp"),
        P(None, "dp"),
    )
    in_specs = (
        *((P("dp", None),) * 7),
        P(),
        P(None, "tensor"),
        P("tensor", None),
        P("tensor", None, None),
        P("tensor", None, None),
        P(),
        *moments,
        *moments,
    )
    out_specs = (P("dp", None), P("dp", None), *moments, *moments, *moments, P())
    return jax.shard_map(body, mesh=mesh, in_specs=in_specs, out_specs=out_specs, check_vma=False)
```

```python
import functools

import jax
import jax.numpy as jnp
from jax import lax
from jax.experimental import pallas as pl
from jax.experimental.pallas import tpu as pltpu
from jax.sharding import PartitionSpec as P

QUERY_HEADS = 24
KEY_VALUE_HEADS = 8
PER_GROUP = QUERY_HEADS // KEY_VALUE_HEADS
HEAD_SIZE = 64
HALF = HEAD_SIZE // 2
TOP = 8
STEP = 3
GROUP_COLUMNS = 320

NORM_EPS = 1e-06
ROPE_BASE = 10000.0
BETA = 0.5
WEIGHT_DECAY = 0.01
ADAM_EPS = 1e-06
RATE = 0.5
MASKED = -1e30

ROWS = 256
MIB = 1 << 20
NO_COST = pl.CostEstimate(flops=0, bytes_accessed=0, transcendentals=0)
F32 = jnp.float32
LOW = jnp.bfloat16


def dot(a, b):
    return jnp.dot(a, b, preferred_element_type=F32)


def dot_nt(a, b):
    return lax.dot_general(a, b, (((1,), (1,)), ((), ())), preferred_element_type=F32)


def dot_tn(a, b):
    return lax.dot_general(a, b, (((0,), (0,)), ((), ())), preferred_element_type=F32)


def params(mib):
    return pltpu.CompilerParams(vmem_limit_bytes=mib * MIB)


def limits_kernel(capacity_ref, first_ref, ids_ref, order_ref, limit_ref):
    ids = ids_ref[...]
    order = order_ref[...]
    pairs = ids.shape[0] * ids.shape[1]
    own = []
    caps = []
    limits = []
    for e in range(limit_ref.shape[0]):
        label = first_ref[0] + e
        own.append(jnp.where(ids == label, order, pairs))
        caps.append(capacity_ref[label])
        limits.append(jnp.zeros((1, 1), jnp.int32))
    step = pairs
    while step > 1:
        step //= 2
        for e in range(len(own)):
            trial = limits[e] + step
            count = jnp.sum((own[e] < trial).astype(jnp.int32), axis=(0, 1), keepdims=True)
            limits[e] = jnp.where(count < caps[e], trial, limits[e])
    for e in range(len(own)):
        limit_ref[e : e + 1] = jnp.broadcast_to(limits[e], (1, limit_ref.shape[1]))


def order_limits(expert_ids, placement_order, capacity, first_expert, local_count):
    smem = pl.BlockSpec(memory_space=pltpu.SMEM)
    vmem = pl.BlockSpec(memory_space=pltpu.VMEM)
    return pl.pallas_call(
        limits_kernel,
        in_specs=[smem, smem, vmem, vmem],
        out_specs=vmem,
        out_shape=jax.ShapeDtypeStruct((local_count, 128), jnp.int32),
        compiler_params=params(16),
        cost_estimate=NO_COST,
        name="order_limits",
    )(
        capacity,
        first_expert.reshape(1),
        expert_ids.reshape(-1, 128),
        placement_order.reshape(-1, 128),
    )


def rotate(source, cos, sin):
    a = source[:HALF]
    b = source[HALF:]
    return jnp.concatenate([a * cos - b * sin, b * cos + a * sin], 0)


def rotate_back(source, cos, sin):
    a = source[:HALF]
    b = source[HALF:]
    return jnp.concatenate([a * cos + b * sin, b * cos - a * sin], 0)


def probabilities(keys, query_t, bias):
    scores = dot(keys, query_t) + bias
    top = jnp.max(scores, axis=0, keepdims=True)
    raised = jnp.exp(scores - top)
    return raised * (1.0 / jnp.sum(raised, axis=0, keepdims=True))


SCALE = HEAD_SIZE**-0.5


def tree_layout(parents_ref, row):
    seg_count = parents_ref.shape[1]
    bits = []
    lengths = []
    for s in range(seg_count):
        current = jnp.int32(s)
        mask = jnp.int32(1 << s)
        for repeat in range(seg_count):
            current = parents_ref[0, current]
            mask = mask | (jnp.int32(1) << current)
        bits.append(mask)
        lengths.append(jnp.sum((row == s).astype(jnp.int32), axis=1, keepdims=True))
    start = jnp.zeros((1, 1), jnp.int32)
    offset = jnp.zeros(row.shape, jnp.int32)
    reach = jnp.zeros(row.shape, jnp.int32)
    for s in range(seg_count):
        above = jnp.zeros((1, 1), jnp.int32)
        for a in range(seg_count):
            if a != s:
                above = above + lengths[a] * ((bits[s] >> a) & 1)
        offset = jnp.where(row == s, above - start, offset)
        reach = jnp.where(row == s, bits[s], reach)
        start = start + lengths[s]
    return lax.broadcasted_iota(jnp.int32, row.shape, 1) + offset, reach


def forward_kernel(
    parents_ref, row_ref, col_ref, freq_ref, x_ref, gain_ref, w_hbm,
    n1_hbm, bias_hbm, out_ref, cos_ref, sin_ref,
    w_ref, n1_ref, bias_ref, out_t, sems,
):
    tok = x_ref.shape[0]
    load = pltpu.make_async_copy(w_hbm, w_ref, sems.at[0])
    load.start()
    for lo in range(0, tok, ROWS):
        x = x_ref[lo : lo + ROWS].astype(F32)
        s = lax.rsqrt(jnp.mean(x * x, axis=-1, keepdims=True) + NORM_EPS)
        n1_ref[lo : lo + ROWS] = (x * s * gain_ref[...]).astype(LOW)
    save_n1 = pltpu.make_async_copy(n1_ref, n1_hbm, sems.at[1])
    save_n1.start()
    position, reach = tree_layout(parents_ref, row_ref[...])
    angles = position.astype(F32) * freq_ref[...]
    cos = jnp.cos(angles)
    sin = jnp.sin(angles)
    cos_ref[...] = cos
    sin_ref[...] = sin
    for lo in range(0, tok, ROWS):
        key = lax.broadcasted_iota(jnp.int32, (ROWS, tok), 0) + lo
        query = lax.broadcasted_iota(jnp.int32, (ROWS, tok), 1)
        seen = (jnp.right_shift(reach, col_ref[lo : lo + ROWS]) & 1) > 0
        bias_ref[lo : lo + ROWS] = jnp.where(seen & (key <= query), 0.0, MASKED)
    save_bias = pltpu.make_async_copy(bias_ref, bias_hbm, sems.at[2])
    save_bias.start()
    load.wait()
    mixed = dot(n1_ref[...], w_ref[...].astype(LOW)).T
    for g in range(w_ref.shape[1] // GROUP_COLUMNS):
        base = g * GROUP_COLUMNS
        at_key = base + PER_GROUP * HEAD_SIZE
        at_value = at_key + HEAD_SIZE
        keys = rotate(mixed[at_key:at_value], cos, sin).T.astype(LOW)
        value_t = mixed[at_value : at_value + HEAD_SIZE].astype(LOW)
        for h in range(PER_GROUP):
            lo = base + h * HEAD_SIZE
            query_t = rotate(mixed[lo : lo + HEAD_SIZE], cos, sin).astype(LOW) * SCALE
            query_t = query_t.astype(LOW)
            at = (g * PER_GROUP + h) * HEAD_SIZE
            for block in range(tok // ROWS):
                q0 = block * ROWS
                ext = q0 + ROWS
                probs = probabilities(
                    keys[:ext], query_t[:, q0:ext], bias_ref[:ext, q0:ext]
                ).astype(LOW)
                out_t[at : at + HEAD_SIZE, q0:ext] = dot(value_t[:, :ext], probs)
    out_ref[...] = out_t[...].T.astype(LOW).astype(F32)
    save_n1.wait()
    save_bias.wait()


def attention_forward(segment_ids, parents, x, gain, w_qkv):
    tok, width = x.shape
    cols = w_qkv.shape[1]
    heads = cols // GROUP_COLUMNS * PER_GROUP * HEAD_SIZE
    frequency = ROPE_BASE ** (-2.0 * jnp.arange(HALF, dtype=F32) / HEAD_SIZE)
    smem = pl.BlockSpec(memory_space=pltpu.SMEM)
    vmem = pl.BlockSpec(memory_space=pltpu.VMEM)
    anywhere = pl.BlockSpec(memory_space=pl.ANY)
    return pl.pallas_call(
        forward_kernel,
        in_specs=[smem, vmem, vmem, vmem, vmem, vmem, anywhere],
        out_specs=[anywhere, anywhere, vmem, vmem, vmem],
        out_shape=[
            jax.ShapeDtypeStruct((tok, width), LOW),
            jax.ShapeDtypeStruct((tok, tok), F32),
            jax.ShapeDtypeStruct((tok, heads), F32),
            jax.ShapeDtypeStruct((HALF, tok), F32),
            jax.ShapeDtypeStruct((HALF, tok), F32),
        ],
        scratch_shapes=[
            pltpu.VMEM((width, cols), F32),
            pltpu.VMEM((tok, width), LOW),
            pltpu.VMEM((tok, tok), F32),
            pltpu.VMEM((heads, tok), F32),
            pltpu.SemaphoreType.DMA((3,)),
        ],
        compiler_params=params(56),
        cost_estimate=NO_COST,
        name="attention_forward",
    )(
        parents,
        segment_ids,
        segment_ids.reshape(tok, 1),
        frequency.reshape(HALF, 1),
        x,
        gain,
        w_qkv,
    )


def out_kernel(first, sources, index_ref, *refs):
    heads = refs[: len(sources)]
    w_ref, x_ref, gain_ref = refs[len(sources) : len(sources) + 3]
    if first:
        res_ref, n2_ref, low_ref, stage = refs[-4:]
        shares, slices, rows, _ = w_ref.shape
        for t in range(slices):
            for d in range(shares):
                at = (t * shares + d) * rows
                low_ref[at : at + rows] = w_ref[d, t].astype(LOW)
    else:
        res_ref, n2_ref, stage = refs[-3:]
        low_ref = w_ref
    index = index_ref[0]
    count, _, part = stage.shape
    for i, (ref, offset) in enumerate(zip(heads, sources)):
        if offset is None:
            stage[i] = ref[...].astype(LOW)
        else:
            for j in range(count):

                @pl.when(index + offset == j)
                def _():
                    stage[j] = ref[...].astype(LOW)

    attn = dot(stage[0], low_ref[:part])
    for t in range(1, count):
        attn = attn + dot(stage[t], low_ref[t * part : (t + 1) * part])
    total = x_ref[...].astype(F32) + attn
    res_ref[...] = total
    s = lax.rsqrt(jnp.mean(total * total, axis=-1, keepdims=True) + NORM_EPS)
    n2_ref[...] = (total * s * gain_ref[...]).astype(LOW)


def out_projection(chunk, calls, heads, sources, index, count, weights, x, gain, done):
    first = not done
    tok, part = heads[0].shape
    width = x.shape[1]
    at = lambda i: (chunk - calls + 1 + i, 0)
    rows = pl.BlockSpec((ROWS, width), at)
    low = jax.ShapeDtypeStruct((count * part, width), LOW)
    low_spec = pl.BlockSpec(low.shape, lambda i: (0, 0))
    return pl.pallas_call(
        functools.partial(out_kernel, first, sources),
        grid=(calls,),
        in_specs=[
            pl.BlockSpec(memory_space=pltpu.SMEM),
            *[pl.BlockSpec((ROWS, part), at) for _ in heads],
            pl.BlockSpec(weights.shape, lambda i: (0,) * weights.ndim),
            rows,
            pl.BlockSpec((1, width), lambda i: (0, 0)),
            *[pl.BlockSpec(memory_space=pl.ANY) for _ in done],
        ],
        out_specs=[rows, rows] + [low_spec] * first,
        out_shape=[
            jax.ShapeDtypeStruct((tok, width), F32),
            jax.ShapeDtypeStruct((tok, width), LOW),
        ]
        + [low] * first,
        scratch_shapes=[pltpu.VMEM((count, ROWS, part), LOW)],
        input_output_aliases={len(heads) + 4 + i: i for i in range(len(done))},
        compiler_params=params(56),
        cost_estimate=NO_COST,
        name="out_projection",
    )(index.reshape(1), *heads, weights, x, gain, *done)


def expert_column(weights, e):
    lane = lax.broadcasted_iota(jnp.int32, weights.shape, 1)
    return jnp.sum(jnp.where(lane == e, weights, 0.0), axis=1, keepdims=True)


def expert_kernel(pieces, n2_ref, dy_ref, we_ref, wgu_ref, wd_ref, *refs):
    hid_ref, dgu_ref = refs[-2 - 2 * pieces : len(refs) - 2 * pieces]
    dn2_refs = refs[-2 * pieces : len(refs) - pieces]
    out_refs = refs[-pieces:]
    e = pl.program_id(0)
    ff = wd_ref.shape[0]
    weight = expert_column(we_ref[...], e)
    kept = weight > 0.0
    wgu = wgu_ref[...]
    wd = wd_ref[...]
    gate_up = dot(n2_ref[...], wgu)
    gate = gate_up[:, :ff]
    up = gate_up[:, ff:]
    sig = 1.0 / (1.0 + jnp.exp(-gate))
    silu = gate * sig
    hidden = jnp.where(kept, silu * up, 0.0).astype(LOW)
    hid_ref[...] = hidden
    out = weight * dot(hidden, wd)
    d_out = (weight * dy_ref[...].astype(F32)).astype(LOW)
    d_hidden = dot_nt(d_out, wd)
    d_gate = d_hidden * up * sig * (1.0 + gate * (1.0 - sig))
    d_up = d_hidden * silu
    d_gate_up = jnp.where(kept, jnp.concatenate([d_gate, d_up], 1), 0.0).astype(LOW)
    dgu_ref[...] = d_gate_up
    d_n2 = dot_nt(d_gate_up, wgu)

    for sums, refs in ((d_n2, dn2_refs), (out, out_refs)):
        for i, ref in enumerate(refs):
            part = sums[i * ROWS : (i + 1) * ROWS]

            @pl.when(e == 0)
            def _():
                ref[...] = part

            @pl.when(e > 0)
            def _():
                ref[...] += part


def experts(chunk, pieces, n2, dy, weights, wgu, wd, done):
    tok, width = n2.shape
    count, ff, _ = wd.shape
    rows = pieces * ROWS
    at = chunk * ROWS
    wide = pl.BlockSpec((pl.Element(rows), pl.Element(width)), lambda e: (at, 0))
    tall = lambda cols: pl.BlockSpec(
        (None, pl.Element(rows), pl.Element(cols)), lambda e: (e, at, 0)
    )
    return pl.pallas_call(
        functools.partial(expert_kernel, pieces),
        grid=(count,),
        in_specs=[
            wide,
            wide,
            pl.BlockSpec((pl.Element(rows), pl.Element(count)), lambda e: (at, 0)),
            pl.BlockSpec((None, width, 2 * ff), lambda e: (e, 0, 0)),
            pl.BlockSpec((None, ff, width), lambda e: (e, 0, 0)),
            *[pl.BlockSpec(memory_space=pl.ANY) for _ in done],
        ],
        out_specs=[
            tall(ff),
            tall(2 * ff),
            *[pl.BlockSpec((ROWS, width), lambda e: (0, 0))] * (2 * pieces),
        ],
        out_shape=[
            jax.ShapeDtypeStruct((count, tok, ff), LOW),
            jax.ShapeDtypeStruct((count, tok, 2 * ff), LOW),
            *[jax.ShapeDtypeStruct((ROWS, width), F32)] * (2 * pieces),
        ],
        input_output_aliases={5 + i: i for i in range(len(done))},
        compiler_params=params(56),
        cost_estimate=NO_COST,
        name="experts",
    )(n2, dy, weights, wgu, wd, *done)


def split_store(out_ref, lo, value):
    rows = out_ref.shape[1]
    cols = slice(lo, lo + value.shape[1])
    for i in range(out_ref.shape[0]):
        out_ref[i, :, cols] = value[i * rows : (i + 1) * rows]


def late_grad_kernel(n1_ref, dmix_ref, dattn_ref, heads_ref, gains_ref, out_ref):
    shares, lanes = gains_ref.shape[0], gains_ref.shape[2]
    share = n1_ref.shape[1] // shares
    split = dmix_ref.shape[1]
    out_ref[:, share:, :] = jnp.zeros((shares, 8, out_ref.shape[2]), F32)
    out_ref[:, share:, :lanes] = gains_ref[...]
    for left, right, lo in ((n1_ref, dmix_ref, 0), (dattn_ref, heads_ref, split)):
        value = dot_tn(left[...], right[...].astype(LOW))
        for i in range(shares):
            out_ref[i, :share, lo : lo + right.shape[1]] = value[i * share : (i + 1) * share]


def late_grads(n1, d_mixed, d_attn, heads, gains):
    tok, width = n1.shape
    count = gains.shape[0]
    half = count // 2
    rows = width // count + 8
    cols = d_mixed.shape[1] + heads.shape[1]
    part = pl.BlockSpec((tok, width // 2), lambda i: (0, i))
    whole = lambda array: pl.BlockSpec(array.shape, lambda i: (0, 0))
    return pl.pallas_call(
        late_grad_kernel,
        grid=(2,),
        in_specs=[
            part,
            whole(d_mixed),
            part,
            whole(heads),
            pl.BlockSpec((half, *gains.shape[1:]), lambda i: (i, 0, 0)),
        ],
        out_specs=pl.BlockSpec((half, rows, cols), lambda i: (i, 0, 0)),
        out_shape=jax.ShapeDtypeStruct((count, rows, cols), F32),
        compiler_params=params(56),
        cost_estimate=NO_COST,
        name="late_grads",
    )(n1, d_mixed, d_attn, heads, gains)


def expert_grad_kernel(n2_ref, dy_ref, we_ref, dgu_ref, hid_ref, out_ref):
    weight = expert_column(we_ref[...], pl.program_id(0))
    d_out = (weight * dy_ref[...].astype(F32)).astype(LOW)
    split_store(out_ref, 0, dot_tn(n2_ref[...], dgu_ref[...]))
    split_store(out_ref, dgu_ref.shape[1], dot_tn(d_out, hid_ref[...]))


def expert_grads(n2, dy, weights, d_gate_up, hidden, shares):
    tok, width = n2.shape
    count, _, wide = d_gate_up.shape
    ff = hidden.shape[2]
    share = width // shares
    parts = shares // 2
    rows = pl.BlockSpec((tok, parts * share), lambda e, i: (0, i))
    return pl.pallas_call(
        expert_grad_kernel,
        grid=(count, shares // parts),
        in_specs=[
            rows,
            rows,
            pl.BlockSpec(weights.shape, lambda e, i: (0, 0)),
            pl.BlockSpec((None, tok, wide), lambda e, i: (e, 0, 0)),
            pl.BlockSpec((None, tok, ff), lambda e, i: (e, 0, 0)),
        ],
        out_specs=pl.BlockSpec((parts, None, share, wide + ff), lambda e, i: (i, e, 0, 0)),
        out_shape=jax.ShapeDtypeStruct((shares, count, share, wide + ff), F32),
        compiler_params=params(56),
        cost_estimate=NO_COST,
        name="expert_grads",
    )(n2, dy, weights, d_gate_up, hidden)


def heads_kernel(n1_ref, w_ref, cos_ref, sin_ref, low_ref, qt_ref, kt_ref, k_ref, v_ref):
    cols = w_ref.shape[-1]
    w_low = w_ref[...].reshape(-1, cols).astype(LOW)
    low_ref[...] = w_low
    mixed = dot(n1_ref[...], w_low).T
    cos = cos_ref[...]
    sin = sin_ref[...]
    queries = []
    keys = []
    values = []
    for g in range(cols // GROUP_COLUMNS):
        base = g * GROUP_COLUMNS
        for h in range(PER_GROUP):
            lo = base + h * HEAD_SIZE
            queries.append(rotate(mixed[lo : lo + HEAD_SIZE], cos, sin))
        at_key = base + PER_GROUP * HEAD_SIZE
        at_value = at_key + HEAD_SIZE
        keys.append(rotate(mixed[at_key:at_value], cos, sin))
        values.append(mixed[at_value : at_value + HEAD_SIZE])
    queries = jnp.concatenate(queries, 0)
    keys = jnp.concatenate(keys, 0)
    qt_ref[...] = (queries.astype(LOW) * SCALE).astype(LOW)
    kt_ref[...] = keys.astype(LOW)
    k_ref[...] = keys.T.astype(LOW)
    v_ref[...] = jnp.concatenate(values, 0).T.astype(LOW)


def all_heads(n1, w_slices, cos, sin):
    shares, slices, rows, cols = w_slices.shape
    tok, width = n1.shape
    groups = cols // GROUP_COLUMNS
    keys = groups * HEAD_SIZE
    queries = keys * PER_GROUP
    shapes = [(width, cols), (queries, tok), (keys, tok), (tok, keys), (tok, keys)]
    whole = lambda *shape: pl.BlockSpec(shape, lambda t: (0,) * len(shape))
    return pl.pallas_call(
        heads_kernel,
        grid=(slices,),
        in_specs=[
            whole(tok, width),
            pl.BlockSpec((shares, None, rows, cols), lambda t: (0, t, 0, 0)),
            whole(HALF, tok),
            whole(HALF, tok),
        ],
        out_specs=[pl.BlockSpec((None, *shape), lambda t: (t, 0, 0)) for shape in shapes],
        out_shape=[jax.ShapeDtypeStruct((slices, *shape), LOW) for shape in shapes],
        compiler_params=params(56),
        cost_estimate=NO_COST,
        name="all_heads",
    )(n1, w_slices, cos, sin)


def norm_terms(rows_in, gain, upstream):
    s = lax.rsqrt(jnp.mean(rows_in * rows_in, axis=-1, keepdims=True) + NORM_EPS)
    pulled = upstream * gain
    inner = jnp.mean(rows_in * pulled, axis=-1, keepdims=True)
    grad = s * pulled - rows_in * (s * s * s) * inner
    return grad, jnp.sum(upstream * rows_in * s, axis=0, keepdims=True)


def backward_kernel(
    inner_ref, dn2_hbm, dn2_end_hbm, res_ref, dy_ref, x_ref, gains_ref, low_ref, wo_ref, qt_ref, kt_ref, k_ref,
    v_ref, cos_ref, sin_ref, bias_ref, *refs,
):
    later = len(refs) > 11
    d_gains_ref, dattn_ref, igrad_ref, dmix_ref, dk_ref, dv_ref = refs[-11:-5]
    dmix_t, dres_ref, dn1_ref, low_dattn, sem = refs[-5:]
    t = pl.program_id(0)
    last = pl.num_programs(0) - 1
    ext = bias_ref.shape[0]
    old = ext - ROWS

    @pl.when(t == 0)
    def _():
        for flag, source in ((1, dn2_hbm), (0, dn2_end_hbm)):

            @pl.when(inner_ref[0] == flag)
            def _():
                copy = pltpu.make_async_copy(source, dn1_ref, sem)
                copy.start()
                copy.wait()

        grad, gain = norm_terms(res_ref[...], gains_ref[1:2], dn1_ref[...])
        grad = grad + dy_ref[...].astype(F32)
        dres_ref[...] = grad
        low_dattn[...] = grad.astype(LOW)
        dattn_ref[...] = grad.astype(LOW)
        d_gains_ref[1:2] = gain

    d_heads_t = dot_nt(wo_ref[...], low_dattn[...]).astype(LOW)
    cos = cos_ref[...]
    sin = sin_ref[...]
    bias = bias_ref[...]
    for g in range(k_ref.shape[1] // HEAD_SIZE):
        at_g = g * HEAD_SIZE
        keys = k_ref[:, at_g : at_g + HEAD_SIZE]
        keys_t = kt_ref[at_g : at_g + HEAD_SIZE]
        values = v_ref[:, at_g : at_g + HEAD_SIZE]
        d_keys = jnp.zeros((HEAD_SIZE, ext), F32)
        d_values = jnp.zeros((HEAD_SIZE, ext), F32)
        base = g * GROUP_COLUMNS
        for h in range(PER_GROUP):
            at = (g * PER_GROUP + h) * HEAD_SIZE
            probs = probabilities(keys, qt_ref[at : at + HEAD_SIZE], bias)
            d_probs = dot(values, d_heads_t[at : at + HEAD_SIZE])
            delta = jnp.sum(probs * d_probs, axis=0, keepdims=True)
            d_scores = (probs * (d_probs - delta)).astype(LOW)
            d_query = dot(keys_t, d_scores) * SCALE
            d_keys = d_keys + dot_nt(qt_ref[at : at + HEAD_SIZE], d_scores)
            d_values = d_values + dot_nt(d_heads_t[at : at + HEAD_SIZE], probs.astype(LOW))
            lo = base + h * HEAD_SIZE
            dmix_t[lo : lo + HEAD_SIZE] = rotate_back(d_query, cos, sin)
        if later:
            dk_in, dv_in = refs[-13:-11]
            d_keys = d_keys + dk_in[at_g : at_g + HEAD_SIZE]
            d_values = d_values + dv_in[at_g : at_g + HEAD_SIZE]
        if old:
            dk_ref[at_g : at_g + HEAD_SIZE] = d_keys
            dv_ref[at_g : at_g + HEAD_SIZE] = d_values
        at_key = base + PER_GROUP * HEAD_SIZE
        at_value = at_key + HEAD_SIZE
        dmix_t[at_key:at_value] = rotate_back(d_keys[:, old:], cos, sin)
        dmix_t[at_value : at_value + HEAD_SIZE] = d_values[:, old:]
    d_mixed = dmix_t[...].T.astype(LOW)
    dmix_ref[...] = d_mixed
    part = dot_nt(d_mixed, low_ref[...])

    @pl.when(t == 0)
    def _():
        dn1_ref[...] = part

    @pl.when(t > 0)
    def _():
        dn1_ref[...] += part

    @pl.when(t == last)
    def _():
        grad, gain = norm_terms(x_ref[...].astype(F32), gains_ref[0:1], dn1_ref[...])
        igrad_ref[...] = (dres_ref[...] + grad).astype(LOW)
        d_gains_ref[0:1] = gain


def attention_backward(chunk, inner, dn2, residual, dy, x, gains, heads, wo, cos, sin, bias, done):
    low, qt, kt, k, v = heads
    slices, width, cols = low.shape
    tok, keys = k.shape[1:]
    queries = qt.shape[1]
    ext = (chunk + 1) * ROWS
    rows = pl.BlockSpec((ROWS, width), lambda t: (chunk, 0))
    sums = pl.BlockSpec((None, keys, ext), lambda t: (t, 0, 0))
    angles = pl.BlockSpec((HALF, ROWS), lambda t: (0, chunk))
    anywhere = pl.BlockSpec(memory_space=pl.ANY)
    part = lambda *shape: pl.BlockSpec((None, *shape), lambda t: (t, 0, 0))
    done_specs = [anywhere, anywhere, anywhere, sums, sums][: len(done)]
    return pl.pallas_call(
        backward_kernel,
        grid=(slices,),
        in_specs=[
            pl.BlockSpec(memory_space=pltpu.SMEM),
            pl.BlockSpec(memory_space=pltpu.HBM),
            pl.BlockSpec(memory_space=pltpu.HBM),
            rows,
            rows,
            rows,
            pl.BlockSpec(gains.shape, lambda t: (0, 0)),
            part(width, cols),
            pl.BlockSpec((queries, width), lambda t: (t, 0)),
            pl.BlockSpec((None, queries, ROWS), lambda t: (t, 0, chunk)),
            part(keys, ext),
            part(ext, keys),
            part(ext, keys),
            angles,
            angles,
            pl.BlockSpec((ext, ROWS), lambda t: (0, chunk)),
            *done_specs,
        ],
        out_specs=[
            pl.BlockSpec(gains.shape, lambda t: (0, 0)),
            rows,
            rows,
            pl.BlockSpec((None, ROWS, cols), lambda t: (t, chunk, 0)),
            sums,
            sums,
        ],
        out_shape=[
            jax.ShapeDtypeStruct(gains.shape, F32),
            jax.ShapeDtypeStruct((tok, width), LOW),
            jax.ShapeDtypeStruct((tok, width), LOW),
            jax.ShapeDtypeStruct((slices, tok, cols), LOW),
            jax.ShapeDtypeStruct((slices, keys, tok), F32),
            jax.ShapeDtypeStruct((slices, keys, tok), F32),
        ],
        scratch_shapes=[
            pltpu.VMEM((cols, ROWS), F32),
            pltpu.VMEM((ROWS, width), F32),
            pltpu.VMEM((ROWS, width), F32),
            pltpu.VMEM((ROWS, width), LOW),
            pltpu.SemaphoreType.DMA,
        ],
        input_output_aliases={16 + i: 1 + i for i in range(len(done))},
        compiler_params=params(56),
        cost_estimate=NO_COST,
        name="attention_backward",
    )(inner, *dn2, residual, dy, x, gains, low, wo, qt, kt, k, v, cos, sin, bias, *done)


def gather_heads(own, index, count, meanwhile):
    if count != 4:
        gathered = lax.all_gather(own, "tensor")
        return [gathered[j] for j in range(count)], [None] * count, meanwhile
    up = [own]
    down = [own]
    for hop in range(1, count):
        if hop == count - 1:
            up[-1], down[-1], meanwhile = lax.optimization_barrier((up[-1], down[-1], meanwhile))
        up.append(lax.ppermute(up[-1], "tensor", [(i, i + 1) for i in range(hop - 1, count - 1)]))
        down.append(
            lax.ppermute(down[-1], "tensor", [(i + 1, i) for i in range(count - hop)])
        )
    sources = [0, *[-hop for hop in range(1, count)], *range(1, count)]
    return [own, *up[1:], *down[1:]], sources, meanwhile


def combine_kernel(
    inner_ref, mid_hbm, crossed_hbm, piece_hbm, got_hbm, next_hbm, send_hbm, sum_hbm,
    mid, crossed, piece, got, sems,
):
    inner = inner_ref[0] > 0
    half = mid.shape[0] // 2

    @pl.when(inner)
    def _():
        loads = []
        for i in range(2):
            rows = pl.ds(i * half, half)
            pairs = ((mid_hbm, mid), (crossed_hbm, crossed), (piece_hbm, piece), (got_hbm, got))
            for j, (source, target) in enumerate(pairs):
                copy = pltpu.make_async_copy(source.at[rows], target.at[rows], sems.at[i, j])
                copy.start()
                loads.append(copy)
        stores = []
        for i in range(2):
            rows = pl.ds(i * half, half)
            for first, left, right, target in ((0, mid, crossed, send_hbm), (2, piece, got, sum_hbm)):
                loads[i * 4 + first].wait()
                loads[i * 4 + first + 1].wait()
                left[rows] = left[rows] + right[rows]
                copy = pltpu.make_async_copy(left.at[rows], target.at[rows], sems.at[i, 4 + first // 2])
                copy.start()
                stores.append(copy)
        for copy in stores:
            copy.wait()

    @pl.when(jnp.logical_not(inner))
    def _():
        copy = pltpu.make_async_copy(next_hbm, send_hbm, sems.at[0, 0])
        copy.start()
        copy.wait()


def combine(inner, *arrays):
    shape = arrays[0].shape
    hbm = pl.BlockSpec(memory_space=pltpu.HBM)
    return pl.pallas_call(
        combine_kernel,
        in_specs=[pl.BlockSpec(memory_space=pltpu.SMEM), *[hbm] * 5],
        out_specs=[hbm, hbm],
        out_shape=[jax.ShapeDtypeStruct(shape, F32)] * 2,
        scratch_shapes=[*[pltpu.VMEM(shape, F32)] * 4, pltpu.SemaphoreType.DMA((2, 6))],
        compiler_params=params(32),
        cost_estimate=NO_COST,
        name="combine",
    )(inner, *arrays)


class Totals:
    def __init__(self, index, count, piece, following, last):
        self.count = count
        self.last = last
        inner = (index == 1) | (index == 2)
        self.inner = inner.astype(jnp.int32).reshape(1)
        self.sent = self.mid = self.piece = piece
        self.following = following
        self.queue = []
        self.at = 0

    def step(self, work, *inputs):
        flight = (self.sent, self.mid, self.piece, inputs)
        sent, mid, piece, inputs = lax.optimization_barrier(flight)
        if self.count != 4:
            made = work(*inputs)
            self.queue.append(lax.psum(piece, "tensor"))
            done = (self.queue[-3:][0],) * 2
            self.piece = self.following()
        else:
            got = lax.ppermute(sent, "tensor", [(0, 1), (1, 0), (2, 3), (3, 2)])
            crossed = mid
            if 0 < self.at < self.last:
                crossed = lax.ppermute(mid, "tensor", [(1, 2), (2, 1)])
            made = work(*inputs)
            following = self.following()
            done = (sent, got)
            if self.at < self.last:
                self.sent, self.mid = combine(self.inner, mid, crossed, piece, got, following)
            self.piece = following
            self.at += 1
        landed = (done, self.sent, self.mid, self.piece, made)
        done, self.sent, self.mid, self.piece, made = lax.optimization_barrier(landed)
        return done, made


def sum_over(values, axis, count):
    if count & (count - 1):
        return lax.psum(values, axis)
    hop = 1
    while hop < count:
        values = values + lax.ppermute(values, axis, [(i, i ^ hop) for i in range(count)])
        hop *= 2
    return values


def vector_of(scalars):
    place = jnp.arange(128)[None, :]
    return sum(jnp.where(place == i, scalar, 0.0) for i, scalar in enumerate(scalars))


def lamb_moments(weight, moment_one, moment_two, gradient):
    first_new = BETA * moment_one + (1.0 - BETA) * gradient
    second_new = BETA * moment_two + (1.0 - BETA) * gradient * gradient
    correction = 1.0 - BETA**STEP
    update = (
        first_new / correction / (jnp.sqrt(second_new / correction) + ADAM_EPS)
        + WEIGHT_DECAY * weight
    )
    return (first_new, second_new, update)


def late_moments_kernel(owner_ref, late_ref, squares_ref, *refs):
    weights, firsts, seconds = refs[:3], refs[3:6], refs[6:9]
    outs, squares_out = refs[9:18], refs[18]
    share, cols = weights[0].shape
    lane = lax.broadcasted_iota(jnp.int32, squares_ref.shape, 1)
    squares = squares_ref[...]
    grads = (
        late_ref[:share, :cols],
        late_ref[:share, cols:].T,
        late_ref[share : share + 2, :share],
    )
    for i, grad in enumerate(grads):
        weight = weights[i][...]
        first, second, update = lamb_moments(weight, firsts[i][...], seconds[i][...], grad)
        outs[3 * i][...] = first
        outs[3 * i + 1][...] = second
        outs[3 * i + 2][...] = update
        if i < 2:
            squares = squares + jnp.where(lane == 6 + i, jnp.sum(update * update), 0.0)
            continue
        for row in range(2):
            total = jnp.sum(update[row] * update[row]) * owner_ref[0]
            squares = squares + jnp.where(lane == 10 + row, total, 0.0)
    squares_out[...] = squares


def late_moments(owner, late, squares, weights, firsts, seconds):
    vmem = pl.BlockSpec(memory_space=pltpu.VMEM)
    shapes = [jax.ShapeDtypeStruct(weight.shape, F32) for weight in weights for _ in range(3)]
    *made, squares = pl.pallas_call(
        late_moments_kernel,
        in_specs=[pl.BlockSpec(memory_space=pltpu.SMEM), *[vmem] * 11],
        out_specs=[vmem] * 10,
        out_shape=[*shapes, jax.ShapeDtypeStruct(squares.shape, F32)],
        compiler_params=params(48),
        cost_estimate=NO_COST,
        name="late_moments",
    )(owner.reshape(1), late, squares, *weights, *firsts, *seconds)
    return [tuple(made[3 * i : 3 * i + 3]) for i in range(3)], squares


def body(
    tokens, cotangent, segment_ids, parents, expert_ids, gate_weights, placement_order, capacity,
    w_qkv, w_out, w_gate_up, w_down, norm_gains,
    first_qkv, first_out, first_gate_up, first_down, first_gains,
    second_moment_projection, second_out, second_gate_up, second_down, second_gains,
):
    tok, width = tokens.shape
    local_experts = w_gate_up.shape[0]
    tensor_index = lax.axis_index("tensor")
    tensor_count = lax.axis_size("tensor")
    data_index = lax.axis_index("dp")
    data_count = lax.axis_size("dp")
    owner_mask = (tensor_index == 0).astype(F32)
    share = tok // tensor_count

    def own_slice(source, axis_dim):
        share_len = source.shape[axis_dim] // data_count
        return lax.dynamic_slice_in_dim(source, data_index * share_len, share_len, axis_dim)

    def own_rows(source):
        return lax.dynamic_slice_in_dim(source, tensor_index * share, share, 0)

    weight_shards = (
        own_slice(w_qkv, 0),
        own_slice(w_out, 1),
        own_slice(w_gate_up, 1),
        own_slice(w_down, 2),
        own_slice(norm_gains, 1),
    )
    first_expert = tensor_index * local_experts

    def weights_of(expert_ids, placement_order, gate_weights, limits):
        local_ids = expert_ids - first_expert
        order = placement_order.reshape(expert_ids.shape)
        columns = []
        for e in range(local_experts):
            kept = (local_ids == e) & (order <= limits[e, 0])
            columns.append(jnp.sum(jnp.where(kept, gate_weights, 0.0), axis=1))
        return jnp.stack(columns, axis=1)

    out_shares = lax.all_gather(own_slice(w_out, 0), "tensor")
    n1, bias, heads_own, cos, sin = attention_forward(
        segment_ids, parents, tokens, norm_gains[0:1], w_qkv
    )
    routed = (expert_ids, placement_order, gate_weights)
    later = (heads_own, w_gate_up, w_down, routed)
    heads_own, wgu, wd, routed = lax.optimization_barrier(later)
    limits = order_limits(*routed[:2], capacity, first_expert, local_experts)
    limits, out_shares = lax.optimization_barrier((limits, out_shares))
    all_out = lax.all_gather(out_shares, "dp")
    meanwhile = (all_out, wgu.astype(LOW), wd.astype(LOW), weights_of(*routed, limits))
    heads, sources, meanwhile = gather_heads(heads_own, tensor_index, tensor_count, meanwhile)
    all_out, wgu_low, wd_low, expert_weights = meanwhile
    heads, qkv_share = lax.optimization_barrier((heads, weight_shards[0]))
    qkv_shares = lax.all_gather(qkv_share, "tensor")

    chunks = tok // ROWS
    wide = w_gate_up.shape[2]

    def project(chunk, calls, weights, done):
        return out_projection(
            chunk, calls, heads, sources, tensor_index, tensor_count, weights, tokens,
            norm_gains[1:2], done,
        )

    def expert_chunks(chunk, pieces, n2, made):
        made = experts(
            chunk, pieces, n2, cotangent, expert_weights, wgu_low, wd_low, made
        )
        parts = made[2 : 2 + pieces]
        outs.extend(made[: 1 + pieces : -1])
        return made[:2], parts[::-1]

    def scattered(source):
        return lax.psum_scatter(source, "dp", tiled=True)[0]

    outs = []
    pieces = []
    *normed, wo_low = project(chunks - 1, 1, all_out, ())
    made, parts = expert_chunks(chunks - 1, 1, normed[1], ())
    last_step = 2 * chunks + 1

    def following():
        queue = pieces or outs
        return queue.pop(0) if queue else parts[0]

    totals = Totals(tensor_index, tensor_count, parts[0], following, last_step)
    inner = totals.inner
    step = totals.step
    whole = {}

    def work_zero(normed, made):
        normed = project(chunks - 2, chunks - 1, wo_low, normed)
        normed, shares = lax.optimization_barrier((normed, qkv_shares))
        whole["qkv"] = lax.all_gather(shares, "dp")
        made, parts = expert_chunks(0, chunks - 1, normed[1], made)
        pieces.extend(parts)
        return made, normed

    _, (made, normed) = step(work_zero, normed, made)
    residual, n2 = normed

    def work_one(n2, hidden, d_gate_up):
        return expert_grads(n2, cotangent, expert_weights, d_gate_up, hidden, data_count)

    _, grads = step(work_one, n2, *made)
    expert_shard = scattered(grads)
    dn2, projected = step(lambda w: all_heads(n1, w, cos, sin), whole["qkv"])

    def back_chunk(c, dn2, projected, done):
        return attention_backward(
            c, inner, dn2, residual, cotangent, tokens, norm_gains, projected, wo_low,
            cos, sin, bias, done,
        )

    def last_grads(made, grad_gains):
        d_gains, d_attn, _, d_mixed = made[:4]
        own_mixed = lax.dynamic_index_in_dim(d_mixed, tensor_index, 0, False)
        gains = (grad_gains + d_gains).reshape(2, data_count, -1).transpose(1, 0, 2)
        gains = jnp.pad(gains, ((0, 0), (0, 6), (0, 0)))
        return late_grads(n1, own_mixed, d_attn, heads_own, gains)

    done = ()
    grad_gains = 0.0
    moe = []
    for c in reversed(range(chunks)):

        def work_back(dn2, projected, done, grad_gains):
            made = back_chunk(c, dn2, projected, done)
            return made[1:], made[0] + grad_gains if c else last_grads(made, grad_gains)

        dn2, (done, grad_gains) = step(work_back, dn2, projected, done, grad_gains)
    moe.append(dn2)
    input_grad = done[1]
    share = width // data_count
    late = scattered(grad_gains)
    total, _ = step(lambda: ())
    moe.append(total)

    firsts = (first_qkv, first_out, first_gate_up, first_down, first_gains)
    seconds = (second_moment_projection, second_out, second_gate_up, second_down, second_gains)

    def square_sum(array):
        return jnp.sum(array * array)

    def all_moments(shard):
        grads = (shard[:, :, :wide], shard[:, :, wide:].transpose(0, 2, 1))
        made = [
            lamb_moments(weight_shards[i], firsts[i], seconds[i], grad)
            for i, grad in zip((2, 3), grads)
        ]
        squares = [square_sum(weight) for weight in weight_shards[:4]]
        squares += [square_sum(row) * owner_mask for row in weight_shards[4]]
        squares += [0.0, 0.0, *[square_sum(update) for _, _, update in made]]
        some = lambda arrays: (arrays[0], arrays[1], arrays[4])
        late_made, squares = late_moments(
            owner_mask, late, vector_of(squares), some(weight_shards), some(firsts), some(seconds)
        )
        squares = sum_over(sum_over(squares, "dp", data_count), "tensor", tensor_count)
        return [*late_made[:2], *made, late_made[2]], squares

    total, (all_made, squares) = step(all_moments, expert_shard)
    moe.append(total)

    def apply(all_made, squares):
        norms = jnp.sqrt(squares)[0, :12]
        trust_ratio = norms[:6] / norms[6:]
        rates = [trust_ratio[index] for index in range(4)] + [trust_ratio[4:6][:, None]]
        updated = [
            weight - RATE * rate * made[2]
            for weight, rate, made in zip(weight_shards, rates, all_made)
        ]
        return updated, norms

    total, (updated, norms) = step(apply, all_made, squares)
    moe.append(total)
    block_out = jnp.zeros((tok, width), LOW)
    for c, (middle, end) in zip(reversed(range(chunks)), moe):
        rows = slice(c * ROWS, (c + 1) * ROWS)
        value = residual[rows] + jnp.where(inner[0] > 0, middle, end)
        block_out = block_out.at[rows].set(value.astype(LOW))
    next_firsts = [made[0] for made in all_made]
    next_seconds = [made[1] for made in all_made]
    trust_norms = jnp.stack([norms[:6], norms[6:]], axis=1)
    return (block_out, input_grad, *updated, *next_firsts, *next_seconds, trust_norms)


def solution(mesh):
    moments = (
        P("dp", "tensor"),
        P("tensor", "dp"),
        P("tensor", "dp", None),
        P("tensor", None, "dp"),
        P(None, "dp"),
    )
    in_specs = (
        *((P("dp", None),) * 7),
        P(),
        P(None, "tensor"),
        P("tensor", None),
        P("tensor", None, None),
        P("tensor", None, None),
        P(),
        *moments,
        *moments,
    )
    out_specs = (P("dp", None), P("dp", None), *moments, *moments, *moments, P())
    return jax.shard_map(body, mesh=mesh, in_specs=in_specs, out_specs=out_specs, check_vma=False)
```

```python
import functools

import jax
import jax.numpy as jnp
from jax import lax
from jax.experimental import pallas as pl
from jax.experimental.pallas import tpu as pltpu
from jax.sharding import PartitionSpec as P

QUERY_HEADS = 24
KEY_VALUE_HEADS = 8
PER_GROUP = QUERY_HEADS // KEY_VALUE_HEADS
HEAD_SIZE = 64
HALF = HEAD_SIZE // 2
TOP = 8
STEP = 3
GROUP_COLUMNS = 320

NORM_EPS = 1e-06
ROPE_BASE = 10000.0
BETA = 0.5
WEIGHT_DECAY = 0.01
ADAM_EPS = 1e-06
RATE = 0.5
MASKED = -1e30

ROWS = 256
MIB = 1 << 20
NO_COST = pl.CostEstimate(flops=0, bytes_accessed=0, transcendentals=0)
F32 = jnp.float32
LOW = jnp.bfloat16


def dot(a, b):
    return jnp.dot(a, b, preferred_element_type=F32)


def dot_nt(a, b):
    return lax.dot_general(a, b, (((1,), (1,)), ((), ())), preferred_element_type=F32)


def dot_tn(a, b):
    return lax.dot_general(a, b, (((0,), (0,)), ((), ())), preferred_element_type=F32)


def params(mib):
    return pltpu.CompilerParams(vmem_limit_bytes=mib * MIB)


def limits_kernel(capacity_ref, first_ref, ids_ref, order_ref, limit_ref):
    ids = ids_ref[...]
    order = order_ref[...]
    pairs = ids.shape[0] * ids.shape[1]
    own = []
    caps = []
    limits = []
    for e in range(limit_ref.shape[0]):
        label = first_ref[0] + e
        own.append(jnp.where(ids == label, order, pairs))
        caps.append(capacity_ref[label])
        limits.append(jnp.zeros((1, 1), jnp.int32))
    step = pairs
    while step > 1:
        step //= 2
        for e in range(len(own)):
            trial = limits[e] + step
            count = jnp.sum((own[e] < trial).astype(jnp.int32), axis=(0, 1), keepdims=True)
            limits[e] = jnp.where(count < caps[e], trial, limits[e])
    for e in range(len(own)):
        limit_ref[e : e + 1] = jnp.broadcast_to(limits[e], (1, limit_ref.shape[1]))


def order_limits(expert_ids, placement_order, capacity, first_expert, local_count):
    smem = pl.BlockSpec(memory_space=pltpu.SMEM)
    vmem = pl.BlockSpec(memory_space=pltpu.VMEM)
    return pl.pallas_call(
        limits_kernel,
        in_specs=[smem, smem, vmem, vmem],
        out_specs=vmem,
        out_shape=jax.ShapeDtypeStruct((local_count, 128), jnp.int32),
        compiler_params=params(16),
        cost_estimate=NO_COST,
        name="order_limits",
    )(
        capacity,
        first_expert.reshape(1),
        expert_ids.reshape(-1, 128),
        placement_order.reshape(-1, 128),
    )


def rotate(source, cos, sin):
    a = source[:HALF]
    b = source[HALF:]
    return jnp.concatenate([a * cos - b * sin, b * cos + a * sin], 0)


def rotate_back(source, cos, sin):
    a = source[:HALF]
    b = source[HALF:]
    return jnp.concatenate([a * cos + b * sin, b * cos - a * sin], 0)


def probabilities(keys, query_t, bias):
    scores = dot(keys, query_t) + bias
    top = jnp.max(scores, axis=0, keepdims=True)
    raised = jnp.exp(scores - top)
    return raised * (1.0 / jnp.sum(raised, axis=0, keepdims=True))


SCALE = HEAD_SIZE**-0.5


def tree_layout(parents_ref, row):
    seg_count = parents_ref.shape[1]
    bits = []
    lengths = []
    for s in range(seg_count):
        current = jnp.int32(s)
        mask = jnp.int32(1 << s)
        for repeat in range(seg_count):
            current = parents_ref[0, current]
            mask = mask | (jnp.int32(1) << current)
        bits.append(mask)
        lengths.append(jnp.sum((row == s).astype(jnp.int32), axis=1, keepdims=True))
    start = jnp.zeros((1, 1), jnp.int32)
    offset = jnp.zeros(row.shape, jnp.int32)
    reach = jnp.zeros(row.shape, jnp.int32)
    for s in range(seg_count):
        above = jnp.zeros((1, 1), jnp.int32)
        for a in range(seg_count):
            if a != s:
                above = above + lengths[a] * ((bits[s] >> a) & 1)
        offset = jnp.where(row == s, above - start, offset)
        reach = jnp.where(row == s, bits[s], reach)
        start = start + lengths[s]
    return lax.broadcasted_iota(jnp.int32, row.shape, 1) + offset, reach


def forward_kernel(
    parents_ref, row_ref, col_ref, freq_ref, x_ref, gain_ref, w_hbm,
    n1_hbm, bias_hbm, out_ref, cos_ref, sin_ref,
    w_ref, n1_ref, bias_ref, out_t, sems,
):
    tok = x_ref.shape[0]
    load = pltpu.make_async_copy(w_hbm, w_ref, sems.at[0])
    load.start()
    for lo in range(0, tok, ROWS):
        x = x_ref[lo : lo + ROWS].astype(F32)
        s = lax.rsqrt(jnp.mean(x * x, axis=-1, keepdims=True) + NORM_EPS)
        n1_ref[lo : lo + ROWS] = (x * s * gain_ref[...]).astype(LOW)
    save_n1 = pltpu.make_async_copy(n1_ref, n1_hbm, sems.at[1])
    save_n1.start()
    position, reach = tree_layout(parents_ref, row_ref[...])
    angles = position.astype(F32) * freq_ref[...]
    cos = jnp.cos(angles)
    sin = jnp.sin(angles)
    cos_ref[...] = cos
    sin_ref[...] = sin
    for lo in range(0, tok, ROWS):
        key = lax.broadcasted_iota(jnp.int32, (ROWS, tok), 0) + lo
        query = lax.broadcasted_iota(jnp.int32, (ROWS, tok), 1)
        seen = (jnp.right_shift(reach, col_ref[lo : lo + ROWS]) & 1) > 0
        bias_ref[lo : lo + ROWS] = jnp.where(seen & (key <= query), 0.0, MASKED)
    save_bias = pltpu.make_async_copy(bias_ref, bias_hbm, sems.at[2])
    save_bias.start()
    load.wait()
    mixed = dot(n1_ref[...], w_ref[...].astype(LOW)).T
    for g in range(w_ref.shape[1] // GROUP_COLUMNS):
        base = g * GROUP_COLUMNS
        at_key = base + PER_GROUP * HEAD_SIZE
        at_value = at_key + HEAD_SIZE
        keys = rotate(mixed[at_key:at_value], cos, sin).T.astype(LOW)
        value_t = mixed[at_value : at_value + HEAD_SIZE].astype(LOW)
        for h in range(PER_GROUP):
            lo = base + h * HEAD_SIZE
            query_t = rotate(mixed[lo : lo + HEAD_SIZE], cos, sin).astype(LOW) * SCALE
            query_t = query_t.astype(LOW)
            at = (g * PER_GROUP + h) * HEAD_SIZE
            for block in range(tok // ROWS):
                q0 = block * ROWS
                ext = q0 + ROWS
                probs = probabilities(
                    keys[:ext], query_t[:, q0:ext], bias_ref[:ext, q0:ext]
                ).astype(LOW)
                out_t[at : at + HEAD_SIZE, q0:ext] = dot(value_t[:, :ext], probs)
    out_ref[...] = out_t[...].T.astype(LOW).astype(F32)
    save_n1.wait()
    save_bias.wait()


def attention_forward(segment_ids, parents, x, gain, w_qkv):
    tok, width = x.shape
    cols = w_qkv.shape[1]
    heads = cols // GROUP_COLUMNS * PER_GROUP * HEAD_SIZE
    frequency = ROPE_BASE ** (-2.0 * jnp.arange(HALF, dtype=F32) / HEAD_SIZE)
    smem = pl.BlockSpec(memory_space=pltpu.SMEM)
    vmem = pl.BlockSpec(memory_space=pltpu.VMEM)
    anywhere = pl.BlockSpec(memory_space=pl.ANY)
    return pl.pallas_call(
        forward_kernel,
        in_specs=[smem, vmem, vmem, vmem, vmem, vmem, anywhere],
        out_specs=[anywhere, anywhere, vmem, vmem, vmem],
        out_shape=[
            jax.ShapeDtypeStruct((tok, width), LOW),
            jax.ShapeDtypeStruct((tok, tok), F32),
            jax.ShapeDtypeStruct((tok, heads), F32),
            jax.ShapeDtypeStruct((HALF, tok), F32),
            jax.ShapeDtypeStruct((HALF, tok), F32),
        ],
        scratch_shapes=[
            pltpu.VMEM((width, cols), F32),
            pltpu.VMEM((tok, width), LOW),
            pltpu.VMEM((tok, tok), F32),
            pltpu.VMEM((heads, tok), F32),
            pltpu.SemaphoreType.DMA((3,)),
        ],
        compiler_params=params(56),
        cost_estimate=NO_COST,
        name="attention_forward",
    )(
        parents,
        segment_ids,
        segment_ids.reshape(tok, 1),
        frequency.reshape(HALF, 1),
        x,
        gain,
        w_qkv,
    )


def out_kernel(first, sources, index_ref, *refs):
    heads = refs[: len(sources)]
    w_ref, x_ref, gain_ref = refs[len(sources) : len(sources) + 3]
    if first:
        res_ref, n2_ref, low_ref, stage = refs[-4:]
        shares, slices, rows, _ = w_ref.shape
        for t in range(slices):
            for d in range(shares):
                at = (t * shares + d) * rows
                low_ref[at : at + rows] = w_ref[d, t].astype(LOW)
    else:
        res_ref, n2_ref, stage = refs[-3:]
        low_ref = w_ref
    index = index_ref[0]
    count, _, part = stage.shape
    for i, (ref, offset) in enumerate(zip(heads, sources)):
        if offset is None:
            stage[i] = ref[...].astype(LOW)
        else:
            for j in range(count):

                @pl.when(index + offset == j)
                def _():
                    stage[j] = ref[...].astype(LOW)

    attn = dot(stage[0], low_ref[:part])
    for t in range(1, count):
        attn = attn + dot(stage[t], low_ref[t * part : (t + 1) * part])
    total = x_ref[...].astype(F32) + attn
    res_ref[...] = total
    s = lax.rsqrt(jnp.mean(total * total, axis=-1, keepdims=True) + NORM_EPS)
    n2_ref[...] = (total * s * gain_ref[...]).astype(LOW)


def out_projection(chunk, calls, heads, sources, index, count, weights, x, gain, done):
    first = not done
    tok, part = heads[0].shape
    width = x.shape[1]
    at = lambda i: (chunk - calls + 1 + i, 0)
    rows = pl.BlockSpec((ROWS, width), at)
    low = jax.ShapeDtypeStruct((count * part, width), LOW)
    low_spec = pl.BlockSpec(low.shape, lambda i: (0, 0))
    return pl.pallas_call(
        functools.partial(out_kernel, first, sources),
        grid=(calls,),
        in_specs=[
            pl.BlockSpec(memory_space=pltpu.SMEM),
            *[pl.BlockSpec((ROWS, part), at) for _ in heads],
            pl.BlockSpec(weights.shape, lambda i: (0,) * weights.ndim),
            rows,
            pl.BlockSpec((1, width), lambda i: (0, 0)),
            *[pl.BlockSpec(memory_space=pl.ANY) for _ in done],
        ],
        out_specs=[rows, rows] + [low_spec] * first,
        out_shape=[
            jax.ShapeDtypeStruct((tok, width), F32),
            jax.ShapeDtypeStruct((tok, width), LOW),
        ]
        + [low] * first,
        scratch_shapes=[pltpu.VMEM((count, ROWS, part), LOW)],
        input_output_aliases={len(heads) + 4 + i: i for i in range(len(done))},
        compiler_params=params(56),
        cost_estimate=NO_COST,
        name="out_projection",
    )(index.reshape(1), *heads, weights, x, gain, *done)


def expert_column(weights, e):
    lane = lax.broadcasted_iota(jnp.int32, weights.shape, 1)
    return jnp.sum(jnp.where(lane == e, weights, 0.0), axis=1, keepdims=True)


def expert_kernel(pieces, n2_ref, dy_ref, we_ref, wgu_ref, wd_ref, *refs):
    hid_ref, dgu_ref = refs[-2 - 2 * pieces : len(refs) - 2 * pieces]
    dn2_refs = refs[-2 * pieces : len(refs) - pieces]
    out_refs = refs[-pieces:]
    e = pl.program_id(0)
    ff = wd_ref.shape[0]
    weight = expert_column(we_ref[...], e)
    kept = weight > 0.0
    wgu = wgu_ref[...]
    wd = wd_ref[...]
    gate_up = dot(n2_ref[...], wgu)
    gate = gate_up[:, :ff]
    up = gate_up[:, ff:]
    sig = 1.0 / (1.0 + jnp.exp(-gate))
    silu = gate * sig
    hidden = jnp.where(kept, silu * up, 0.0).astype(LOW)
    hid_ref[...] = hidden
    out = weight * dot(hidden, wd)
    d_out = (weight * dy_ref[...].astype(F32)).astype(LOW)
    d_hidden = dot_nt(d_out, wd)
    d_gate = d_hidden * up * sig * (1.0 + gate * (1.0 - sig))
    d_up = d_hidden * silu
    d_gate_up = jnp.where(kept, jnp.concatenate([d_gate, d_up], 1), 0.0).astype(LOW)
    dgu_ref[...] = d_gate_up
    d_n2 = dot_nt(d_gate_up, wgu)

    for sums, refs in ((d_n2, dn2_refs), (out, out_refs)):
        for i, ref in enumerate(refs):
            part = sums[i * ROWS : (i + 1) * ROWS]

            @pl.when(e == 0)
            def _():
                ref[...] = part

            @pl.when(e > 0)
            def _():
                ref[...] += part


def experts(chunk, pieces, n2, dy, weights, wgu, wd, done):
    tok, width = n2.shape
    count, ff, _ = wd.shape
    rows = pieces * ROWS
    at = chunk * ROWS
    wide = pl.BlockSpec((pl.Element(rows), pl.Element(width)), lambda e: (at, 0))
    tall = lambda cols: pl.BlockSpec(
        (None, pl.Element(rows), pl.Element(cols)), lambda e: (e, at, 0)
    )
    return pl.pallas_call(
        functools.partial(expert_kernel, pieces),
        grid=(count,),
        in_specs=[
            wide,
            wide,
            pl.BlockSpec((pl.Element(rows), pl.Element(count)), lambda e: (at, 0)),
            pl.BlockSpec((None, width, 2 * ff), lambda e: (e, 0, 0)),
            pl.BlockSpec((None, ff, width), lambda e: (e, 0, 0)),
            *[pl.BlockSpec(memory_space=pl.ANY) for _ in done],
        ],
        out_specs=[
            tall(ff),
            tall(2 * ff),
            *[pl.BlockSpec((ROWS, width), lambda e: (0, 0))] * (2 * pieces),
        ],
        out_shape=[
            jax.ShapeDtypeStruct((count, tok, ff), LOW),
            jax.ShapeDtypeStruct((count, tok, 2 * ff), LOW),
            *[jax.ShapeDtypeStruct((ROWS, width), F32)] * (2 * pieces),
        ],
        input_output_aliases={5 + i: i for i in range(len(done))},
        compiler_params=params(56),
        cost_estimate=NO_COST,
        name="experts",
    )(n2, dy, weights, wgu, wd, *done)


def split_store(out_ref, lo, value):
    rows = out_ref.shape[1]
    cols = slice(lo, lo + value.shape[1])
    for i in range(out_ref.shape[0]):
        out_ref[i, :, cols] = value[i * rows : (i + 1) * rows]


def late_grad_kernel(place_ref, n1_ref, dmix_ref, dattn_ref, heads_ref, gains_ref, out_ref):
    shares, lanes = gains_ref.shape[0], gains_ref.shape[2]
    share = n1_ref.shape[1] // shares
    split = dmix_ref.shape[1]
    out_ref[:, share:, :] = jnp.zeros((shares, 8, out_ref.shape[2]), F32)
    out_ref[:, share:, :lanes] = gains_ref[...]
    for left, right, lo in ((n1_ref, dmix_ref, 0), (dattn_ref, heads_ref, split)):
        value = dot_tn(left[...], right[...].astype(LOW))
        for i in range(shares):
            out_ref[i, :share, lo : lo + right.shape[1]] = value[i * share : (i + 1) * share]


def late_grads(place, n1, d_mixed, d_attn, heads, gains):
    tok, width = n1.shape
    count = gains.shape[0]
    steps = 4
    some = count // steps
    rows = width // count + 8
    cols = d_mixed.shape[2] + heads.shape[1]
    part = pl.BlockSpec((tok, width // steps), lambda i, at: (0, i))
    return pl.pallas_call(
        late_grad_kernel,
        grid_spec=pltpu.PrefetchScalarGridSpec(
            num_scalar_prefetch=1,
            grid=(steps,),
            in_specs=[
                part,
                pl.BlockSpec((None, *d_mixed.shape[1:]), lambda i, at: (at[0], 0, 0)),
                part,
                pl.BlockSpec(heads.shape, lambda i, at: (0, 0)),
                pl.BlockSpec((some, *gains.shape[1:]), lambda i, at: (i, 0, 0)),
            ],
            out_specs=pl.BlockSpec((some, rows, cols), lambda i, at: (i, 0, 0)),
        ),
        out_shape=jax.ShapeDtypeStruct((count, rows, cols), F32),
        compiler_params=params(56),
        cost_estimate=NO_COST,
        name="late_grads",
    )(place.reshape(1), n1, d_mixed, d_attn, heads, gains)


def expert_grad_kernel(n2_ref, dy_ref, we_ref, dgu_ref, hid_ref, out_ref):
    weight = expert_column(we_ref[...], pl.program_id(1))
    d_out = (weight * dy_ref[...].astype(F32)).astype(LOW)
    split_store(out_ref, 0, dot_tn(n2_ref[...], dgu_ref[...]))
    split_store(out_ref, dgu_ref.shape[1], dot_tn(d_out, hid_ref[...]))


def expert_grads(n2, dy, weights, d_gate_up, hidden, shares):
    tok, width = n2.shape
    count, _, wide = d_gate_up.shape
    ff = hidden.shape[2]
    share = width // shares
    parts = shares // 2
    rows = pl.BlockSpec((tok, parts * share), lambda i, e: (0, i))
    return pl.pallas_call(
        expert_grad_kernel,
        grid=(shares // parts, count),
        in_specs=[
            rows,
            rows,
            pl.BlockSpec(weights.shape, lambda i, e: (0, 0)),
            pl.BlockSpec((None, tok, wide), lambda i, e: (e, 0, 0)),
            pl.BlockSpec((None, tok, ff), lambda i, e: (e, 0, 0)),
        ],
        out_specs=pl.BlockSpec((parts, None, share, wide + ff), lambda i, e: (i, e, 0, 0)),
        out_shape=jax.ShapeDtypeStruct((shares, count, share, wide + ff), F32),
        compiler_params=params(56),
        cost_estimate=NO_COST,
        name="expert_grads",
    )(n2, dy, weights, d_gate_up, hidden)


def heads_kernel(n1_ref, w_ref, cos_ref, sin_ref, low_ref, qt_ref, kt_ref, k_ref, v_ref):
    cols = w_ref.shape[-1]
    w_low = w_ref[...].reshape(-1, cols).astype(LOW)
    low_ref[...] = w_low
    mixed = dot(n1_ref[...], w_low).T
    cos = cos_ref[...]
    sin = sin_ref[...]
    queries = []
    keys = []
    values = []
    for g in range(cols // GROUP_COLUMNS):
        base = g * GROUP_COLUMNS
        for h in range(PER_GROUP):
            lo = base + h * HEAD_SIZE
            queries.append(rotate(mixed[lo : lo + HEAD_SIZE], cos, sin))
        at_key = base + PER_GROUP * HEAD_SIZE
        at_value = at_key + HEAD_SIZE
        keys.append(rotate(mixed[at_key:at_value], cos, sin))
        values.append(mixed[at_value : at_value + HEAD_SIZE])
    queries = jnp.concatenate(queries, 0)
    keys = jnp.concatenate(keys, 0)
    qt_ref[...] = (queries.astype(LOW) * SCALE).astype(LOW)
    kt_ref[...] = keys.astype(LOW)
    k_ref[...] = keys.T.astype(LOW)
    v_ref[...] = jnp.concatenate(values, 0).T.astype(LOW)


def all_heads(n1, w_slices, cos, sin):
    shares, slices, rows, cols = w_slices.shape
    tok, width = n1.shape
    groups = cols // GROUP_COLUMNS
    keys = groups * HEAD_SIZE
    queries = keys * PER_GROUP
    shapes = [(width, cols), (queries, tok), (keys, tok), (tok, keys), (tok, keys)]
    whole = lambda *shape: pl.BlockSpec(shape, lambda t: (0,) * len(shape))
    return pl.pallas_call(
        heads_kernel,
        grid=(slices,),
        in_specs=[
            whole(tok, width),
            pl.BlockSpec((shares, None, rows, cols), lambda t: (0, t, 0, 0)),
            whole(HALF, tok),
            whole(HALF, tok),
        ],
        out_specs=[pl.BlockSpec((None, *shape), lambda t: (t, 0, 0)) for shape in shapes],
        out_shape=[jax.ShapeDtypeStruct((slices, *shape), LOW) for shape in shapes],
        compiler_params=params(56),
        cost_estimate=NO_COST,
        name="all_heads",
    )(n1, w_slices, cos, sin)


def norm_terms(rows_in, gain, upstream):
    s = lax.rsqrt(jnp.mean(rows_in * rows_in, axis=-1, keepdims=True) + NORM_EPS)
    pulled = upstream * gain
    inner = jnp.mean(rows_in * pulled, axis=-1, keepdims=True)
    grad = s * pulled - rows_in * (s * s * s) * inner
    return grad, jnp.sum(upstream * rows_in * s, axis=0, keepdims=True)


def backward_kernel(
    inner_ref, dn2_hbm, dn2_end_hbm, res_ref, dy_ref, gains_ref, wo_ref, qt_ref, kt_ref, k_ref, v_ref,
    cos_ref, sin_ref, bias_ref, *refs,
):
    later = len(refs) > 10
    d_gain_ref, dattn_ref, dres_ref, dmix_ref, dk_ref, dv_ref = refs[-10:-4]
    dmix_t, dn2_ref, low_dattn, sem = refs[-4:]
    t = pl.program_id(0)
    ext = bias_ref.shape[0]
    old = ext - ROWS

    @pl.when(t == 0)
    def _():
        for flag, source in ((1, dn2_hbm), (0, dn2_end_hbm)):

            @pl.when(inner_ref[0] == flag)
            def _():
                copy = pltpu.make_async_copy(source, dn2_ref, sem)
                copy.start()
                copy.wait()

        grad, gain = norm_terms(res_ref[...], gains_ref[1:2], dn2_ref[...])
        grad = grad + dy_ref[...].astype(F32)
        dres_ref[...] = grad
        low_dattn[...] = grad.astype(LOW)
        dattn_ref[...] = grad.astype(LOW)
        d_gain_ref[...] = gain

    d_heads_t = dot_nt(wo_ref[...], low_dattn[...]).astype(LOW)
    cos = cos_ref[...]
    sin = sin_ref[...]
    bias = bias_ref[...]
    for g in range(k_ref.shape[1] // HEAD_SIZE):
        at_g = g * HEAD_SIZE
        keys = k_ref[:, at_g : at_g + HEAD_SIZE]
        keys_t = kt_ref[at_g : at_g + HEAD_SIZE]
        values = v_ref[:, at_g : at_g + HEAD_SIZE]
        d_keys = jnp.zeros((HEAD_SIZE, ext), F32)
        d_values = jnp.zeros((HEAD_SIZE, ext), F32)
        base = g * GROUP_COLUMNS
        for h in range(PER_GROUP):
            at = (g * PER_GROUP + h) * HEAD_SIZE
            probs = probabilities(keys, qt_ref[at : at + HEAD_SIZE], bias)
            d_probs = dot(values, d_heads_t[at : at + HEAD_SIZE])
            delta = jnp.sum(probs * d_probs, axis=0, keepdims=True)
            d_scores = (probs * (d_probs - delta)).astype(LOW)
            d_query = dot(keys_t, d_scores) * SCALE
            d_keys = d_keys + dot_nt(qt_ref[at : at + HEAD_SIZE], d_scores)
            d_values = d_values + dot_nt(d_heads_t[at : at + HEAD_SIZE], probs.astype(LOW))
            lo = base + h * HEAD_SIZE
            dmix_t[lo : lo + HEAD_SIZE] = rotate_back(d_query, cos, sin)
        if later:
            dk_in, dv_in = refs[-12:-10]
            d_keys = d_keys + dk_in[at_g : at_g + HEAD_SIZE]
            d_values = d_values + dv_in[at_g : at_g + HEAD_SIZE]
        if old:
            dk_ref[at_g : at_g + HEAD_SIZE] = d_keys
            dv_ref[at_g : at_g + HEAD_SIZE] = d_values
        at_key = base + PER_GROUP * HEAD_SIZE
        at_value = at_key + HEAD_SIZE
        dmix_t[at_key:at_value] = rotate_back(d_keys[:, old:], cos, sin)
        dmix_t[at_value : at_value + HEAD_SIZE] = d_values[:, old:]
    dmix_ref[...] = dmix_t[...].T.astype(LOW)


def attention_backward(chunk, inner, dn2, residual, dy, gains, heads, wo, cos, sin, bias, done):
    qt, kt, k, v = heads
    slices, queries, _ = qt.shape
    tok, width = residual.shape
    keys = k.shape[2]
    cols = queries + 2 * keys
    ext = (chunk + 1) * ROWS
    rows = pl.BlockSpec((ROWS, width), lambda t: (chunk, 0))
    sums = pl.BlockSpec((None, keys, ext), lambda t: (t, 0, 0))
    angles = pl.BlockSpec((HALF, ROWS), lambda t: (0, chunk))
    anywhere = pl.BlockSpec(memory_space=pl.ANY)
    hbm = pl.BlockSpec(memory_space=pltpu.HBM)
    part = lambda *shape: pl.BlockSpec((None, *shape), lambda t: (t, 0, 0))
    done_specs = [anywhere, anywhere, anywhere, sums, sums][: len(done)]
    return pl.pallas_call(
        backward_kernel,
        grid=(slices,),
        in_specs=[
            pl.BlockSpec(memory_space=pltpu.SMEM),
            hbm,
            hbm,
            rows,
            rows,
            pl.BlockSpec(gains.shape, lambda t: (0, 0)),
            pl.BlockSpec((queries, width), lambda t: (t, 0)),
            pl.BlockSpec((None, queries, ROWS), lambda t: (t, 0, chunk)),
            part(keys, ext),
            part(ext, keys),
            part(ext, keys),
            angles,
            angles,
            pl.BlockSpec((ext, ROWS), lambda t: (0, chunk)),
            *done_specs,
        ],
        out_specs=[
            pl.BlockSpec((1, width), lambda t: (0, 0)),
            rows,
            rows,
            pl.BlockSpec((None, ROWS, cols), lambda t: (t, chunk, 0)),
            sums,
            sums,
        ],
        out_shape=[
            jax.ShapeDtypeStruct((1, width), F32),
            jax.ShapeDtypeStruct((tok, width), LOW),
            jax.ShapeDtypeStruct((tok, width), F32),
            jax.ShapeDtypeStruct((slices, tok, cols), LOW),
            jax.ShapeDtypeStruct((slices, keys, tok), F32),
            jax.ShapeDtypeStruct((slices, keys, tok), F32),
        ],
        scratch_shapes=[
            pltpu.VMEM((cols, ROWS), F32),
            pltpu.VMEM((ROWS, width), F32),
            pltpu.VMEM((ROWS, width), LOW),
            pltpu.SemaphoreType.DMA,
        ],
        input_output_aliases={14 + i: 1 + i for i in range(len(done))},
        compiler_params=params(56),
        cost_estimate=NO_COST,
        name="attention_backward",
    )(inner, *dn2, residual, dy, gains, wo, qt, kt, k, v, cos, sin, bias, *done)


def input_kernel(dmix_ref, low_ref, dres_ref, x_ref, gains_ref, igrad_ref, d_gain_ref):
    dn1 = dot_nt(dmix_ref[0], low_ref[0])
    for t in range(1, dmix_ref.shape[0]):
        dn1 = dn1 + dot_nt(dmix_ref[t], low_ref[t])
    grad, gain = norm_terms(x_ref[...].astype(F32), gains_ref[0:1], dn1)
    igrad_ref[...] = (dres_ref[...] + grad).astype(LOW)

    @pl.when(pl.program_id(0) == 0)
    def _():
        d_gain_ref[...] = gain

    @pl.when(pl.program_id(0) > 0)
    def _():
        d_gain_ref[...] += gain


def input_gradient(d_mixed, low, d_residual, x, gains):
    slices, tok, cols = d_mixed.shape
    width = x.shape[1]
    rows = pl.BlockSpec((ROWS, width), lambda i: (i, 0))
    return pl.pallas_call(
        input_kernel,
        grid=(tok // ROWS,),
        in_specs=[
            pl.BlockSpec((slices, ROWS, cols), lambda i: (0, i, 0)),
            pl.BlockSpec(low.shape, lambda i: (0, 0, 0)),
            rows,
            rows,
            pl.BlockSpec(gains.shape, lambda i: (0, 0)),
        ],
        out_specs=[rows, pl.BlockSpec((1, width), lambda i: (0, 0))],
        out_shape=[
            jax.ShapeDtypeStruct((tok, width), LOW),
            jax.ShapeDtypeStruct((1, width), F32),
        ],
        compiler_params=params(56),
        cost_estimate=NO_COST,
        name="input_gradient",
    )(d_mixed, low, d_residual, x, gains)


def gather_heads(own, index, count, shares, beside_first, beside_second):
    if count != 4:
        gathered = lax.all_gather(own, "tensor")
        arrays = [gathered[j] for j in range(count)]
        return arrays, [None] * count, lax.all_gather(shares, "dp"), beside_first, beside_second
    up = [own]
    down = [own]
    for hop in range(1, count):
        if hop == 2:
            flight = (up[-1], down[-1], shares, beside_first)
            up[-1], down[-1], shares, beside_first = lax.optimization_barrier(flight)
            gathered = lax.all_gather(shares, "dp")
        if hop == 3:
            flight = (up[-1], down[-1], beside_second)
            up[-1], down[-1], beside_second = lax.optimization_barrier(flight)
        up.append(lax.ppermute(up[-1], "tensor", [(i, i + 1) for i in range(hop - 1, count - 1)]))
        down.append(
            lax.ppermute(down[-1], "tensor", [(i + 1, i) for i in range(count - hop)])
        )
    sources = [0, *[-hop for hop in range(1, count)], *range(1, count)]
    return [own, *up[1:], *down[1:]], sources, gathered, beside_first, beside_second


def combine_kernel(
    inner_ref, mid_hbm, crossed_hbm, piece_hbm, got_hbm, next_hbm, send_hbm, sum_hbm,
    mid, crossed, piece, got, sems,
):
    inner = inner_ref[0] > 0
    half = mid.shape[0] // 2

    @pl.when(inner)
    def _():
        loads = []
        for i in range(2):
            rows = pl.ds(i * half, half)
            pairs = ((mid_hbm, mid), (crossed_hbm, crossed), (piece_hbm, piece), (got_hbm, got))
            for j, (source, target) in enumerate(pairs):
                copy = pltpu.make_async_copy(source.at[rows], target.at[rows], sems.at[i, j])
                copy.start()
                loads.append(copy)
        stores = []
        for i in range(2):
            rows = pl.ds(i * half, half)
            for first, left, right, target in ((0, mid, crossed, send_hbm), (2, piece, got, sum_hbm)):
                loads[i * 4 + first].wait()
                loads[i * 4 + first + 1].wait()
                left[rows] = left[rows] + right[rows]
                copy = pltpu.make_async_copy(left.at[rows], target.at[rows], sems.at[i, 4 + first // 2])
                copy.start()
                stores.append(copy)
        for copy in stores:
            copy.wait()

    @pl.when(jnp.logical_not(inner))
    def _():
        copy = pltpu.make_async_copy(next_hbm, send_hbm, sems.at[0, 0])
        copy.start()
        copy.wait()


def combine(inner, *arrays):
    shape = arrays[0].shape
    hbm = pl.BlockSpec(memory_space=pltpu.HBM)
    return pl.pallas_call(
        combine_kernel,
        in_specs=[pl.BlockSpec(memory_space=pltpu.SMEM), *[hbm] * 5],
        out_specs=[hbm, hbm],
        out_shape=[jax.ShapeDtypeStruct(shape, F32)] * 2,
        scratch_shapes=[*[pltpu.VMEM(shape, F32)] * 4, pltpu.SemaphoreType.DMA((2, 6))],
        compiler_params=params(32),
        cost_estimate=NO_COST,
        name="combine",
    )(inner, *arrays)


class Totals:
    def __init__(self, index, count, piece, following, last):
        self.count = count
        self.last = last
        inner = (index == 1) | (index == 2)
        self.inner = inner.astype(jnp.int32).reshape(1)
        self.sent = self.mid = self.piece = piece
        self.following = following
        self.queue = []
        self.at = 0

    def step(self, work, *inputs):
        flight = (self.sent, self.mid, self.piece, inputs)
        sent, mid, piece, inputs = lax.optimization_barrier(flight)
        if self.count != 4:
            made = work(*inputs)
            self.queue.append(lax.psum(piece, "tensor"))
            done = (self.queue[-3:][0],) * 2
            self.piece = self.following()
        else:
            got = lax.ppermute(sent, "tensor", [(0, 1), (1, 0), (2, 3), (3, 2)])
            crossed = mid
            if 0 < self.at < self.last:
                crossed = lax.ppermute(mid, "tensor", [(1, 2), (2, 1)])
            made = work(*inputs)
            following = self.following()
            got, crossed, made = lax.optimization_barrier((got, crossed, made))
            done = (sent, got)
            if self.at < self.last:
                self.sent, self.mid = combine(self.inner, mid, crossed, piece, got, following)
            self.piece = following
            self.at += 1
        landed = (done, self.sent, self.mid, self.piece, made)
        done, self.sent, self.mid, self.piece, made = lax.optimization_barrier(landed)
        return done, made

    def send_half(self, half, work, *inputs):
        if self.count != 4:
            total = self.queue[self.last - 2]
            rows = total.shape[0] // 2
            return (total[half * rows : (half + 1) * rows],) * 2, work(*inputs)
        rows = self.sent.shape[0] // 2
        sent = self.sent[half * rows : (half + 1) * rows]
        sent, inputs = lax.optimization_barrier((sent, inputs))
        got = lax.ppermute(sent, "tensor", [(0, 1), (1, 0), (2, 3), (3, 2)])
        made = work(*inputs)
        sent, got, made = lax.optimization_barrier((sent, got, made))
        return (sent, got), made


def sum_over(values, axis, count):
    if count & (count - 1):
        return lax.psum(values, axis)
    hop = 1
    while hop < count:
        values = values + lax.ppermute(values, axis, [(i, i ^ hop) for i in range(count)])
        hop *= 2
    return values


def vector_of(scalars):
    place = jnp.arange(128)[None, :]
    return sum(jnp.where(place == i, scalar, 0.0) for i, scalar in enumerate(scalars))


def lamb_moments(weight, moment_one, moment_two, gradient):
    first_new = BETA * moment_one + (1.0 - BETA) * gradient
    second_new = BETA * moment_two + (1.0 - BETA) * gradient * gradient
    correction = 1.0 - BETA**STEP
    update = (
        first_new / correction / (jnp.sqrt(second_new / correction) + ADAM_EPS)
        + WEIGHT_DECAY * weight
    )
    return (first_new, second_new, update)


def late_moments_kernel(owner_ref, late_ref, gain_ref, squares_ref, *refs):
    weights, firsts, seconds = refs[:3], refs[3:6], refs[6:9]
    outs, squares_out = refs[9:18], refs[18]
    share, cols = weights[0].shape
    lane = lax.broadcasted_iota(jnp.int32, squares_ref.shape, 1)
    squares = squares_ref[...]
    grads = (
        late_ref[:share, :cols],
        late_ref[:share, cols:].T,
        jnp.concatenate([gain_ref[...], late_ref[share : share + 1, :share]], 0),
    )
    for i, grad in enumerate(grads):
        weight = weights[i][...]
        first, second, update = lamb_moments(weight, firsts[i][...], seconds[i][...], grad)
        outs[3 * i][...] = first
        outs[3 * i + 1][...] = second
        outs[3 * i + 2][...] = update
        if i < 2:
            squares = squares + jnp.where(lane == 6 + i, jnp.sum(update * update), 0.0)
            continue
        for row in range(2):
            total = jnp.sum(update[row] * update[row]) * owner_ref[0]
            squares = squares + jnp.where(lane == 10 + row, total, 0.0)
    squares_out[...] = squares


def late_moments(owner, late, gain, squares, weights, firsts, seconds):
    vmem = pl.BlockSpec(memory_space=pltpu.VMEM)
    shapes = [jax.ShapeDtypeStruct(weight.shape, F32) for weight in weights for _ in range(3)]
    *made, squares = pl.pallas_call(
        late_moments_kernel,
        in_specs=[pl.BlockSpec(memory_space=pltpu.SMEM), *[vmem] * 12],
        out_specs=[vmem] * 10,
        out_shape=[*shapes, jax.ShapeDtypeStruct(squares.shape, F32)],
        compiler_params=params(48),
        cost_estimate=NO_COST,
        name="late_moments",
    )(owner.reshape(1), late, gain, squares, *weights, *firsts, *seconds)
    return [tuple(made[3 * i : 3 * i + 3]) for i in range(3)], squares


def body(
    tokens, cotangent, segment_ids, parents, expert_ids, gate_weights, placement_order, capacity,
    w_qkv, w_out, w_gate_up, w_down, norm_gains,
    first_qkv, first_out, first_gate_up, first_down, first_gains,
    second_moment_projection, second_out, second_gate_up, second_down, second_gains,
):
    tok, width = tokens.shape
    local_experts = w_gate_up.shape[0]
    tensor_index = lax.axis_index("tensor")
    tensor_count = lax.axis_size("tensor")
    data_index = lax.axis_index("dp")
    data_count = lax.axis_size("dp")
    owner_mask = (tensor_index == 0).astype(F32)
    share = tok // tensor_count

    def own_slice(source, axis_dim):
        share_len = source.shape[axis_dim] // data_count
        return lax.dynamic_slice_in_dim(source, data_index * share_len, share_len, axis_dim)

    def own_rows(source):
        return lax.dynamic_slice_in_dim(source, tensor_index * share, share, 0)

    weight_shards = (
        own_slice(w_qkv, 0),
        own_slice(w_out, 1),
        own_slice(w_gate_up, 1),
        own_slice(w_down, 2),
        own_slice(norm_gains, 1),
    )
    first_expert = tensor_index * local_experts

    def weights_of(expert_ids, placement_order, gate_weights, limits):
        local_ids = expert_ids - first_expert
        order = placement_order.reshape(expert_ids.shape)
        columns = []
        for e in range(local_experts):
            kept = (local_ids == e) & (order <= limits[e, 0])
            columns.append(jnp.sum(jnp.where(kept, gate_weights, 0.0), axis=1))
        return jnp.stack(columns, axis=1)

    out_shares = lax.all_gather(own_slice(w_out, 0), "tensor")
    n1, bias, heads_own, cos, sin = attention_forward(
        segment_ids, parents, tokens, norm_gains[0:1], w_qkv
    )
    routed = (expert_ids, placement_order, gate_weights)
    later = (heads_own, w_gate_up, w_down, routed)
    heads_own, wgu, wd, routed = lax.optimization_barrier(later)
    limits = order_limits(*routed[:2], capacity, first_expert, local_experts)
    beside_first = (wd.astype(LOW), weights_of(*routed, limits))
    beside_second = (wgu.astype(LOW), weight_shards)
    heads, sources, all_out, beside_first, beside_second = gather_heads(
        heads_own, tensor_index, tensor_count, out_shares, beside_first, beside_second
    )
    wd_low, expert_weights = beside_first
    wgu_low, weight_shards = beside_second
    heads, qkv_share = lax.optimization_barrier((heads, weight_shards[0]))
    qkv_shares = lax.all_gather(qkv_share, "tensor")

    chunks = tok // ROWS
    wide = w_gate_up.shape[2]

    def project(chunk, calls, weights, done):
        return out_projection(
            chunk, calls, heads, sources, tensor_index, tensor_count, weights, tokens,
            norm_gains[1:2], done,
        )

    def expert_chunks(chunk, pieces, n2, made):
        made = experts(
            chunk, pieces, n2, cotangent, expert_weights, wgu_low, wd_low, made
        )
        parts = made[2 : 2 + pieces]
        outs.extend(made[: 1 + pieces : -1])
        return made[:2], parts[::-1]

    def scattered(source):
        return lax.psum_scatter(source, "dp", tiled=True)[0]

    outs = []
    pieces = []
    *normed, wo_low = project(chunks - 1, 1, all_out, ())
    made, parts = expert_chunks(chunks - 1, 1, normed[1], ())
    last_step = 2 * chunks + 1

    def following():
        queue = pieces or outs
        return queue.pop(0) if queue else parts[0]

    totals = Totals(tensor_index, tensor_count, parts[0], following, last_step)
    inner = totals.inner
    step = totals.step
    whole = {}

    def work_zero(normed, made):
        normed = project(chunks - 2, chunks - 1, wo_low, normed)
        normed, shares = lax.optimization_barrier((normed, qkv_shares))
        whole["qkv"] = lax.all_gather(shares, "dp")
        made, parts = expert_chunks(0, chunks - 1, normed[1], made)
        pieces.extend(parts)
        return made, normed

    _, (made, normed) = step(work_zero, normed, made)
    residual, n2 = normed

    def work_one(n2, hidden, d_gate_up):
        return expert_grads(n2, cotangent, expert_weights, d_gate_up, hidden, data_count)

    _, grads = step(work_one, n2, *made)
    expert_shard = scattered(grads)
    dn2, projected = step(lambda w: all_heads(n1, w, cos, sin), whole["qkv"])

    def back_chunk(c, dn2, projected, done):
        return attention_backward(
            c, inner, dn2, residual, cotangent, norm_gains, projected[1:], wo_low, cos, sin, bias, done
        )

    def last_grads(made, d_gain):
        gains = (made[0] + d_gain).reshape(data_count, 1, -1)
        gains = jnp.pad(gains, ((0, 0), (0, 7), (0, 0)))
        return late_grads(tensor_index, n1, made[3], made[1], heads_own, gains)

    done = ()
    d_gain = 0.0
    moe = []
    for c in reversed(range(chunks)):

        def work_back(dn2, projected, done, d_gain):
            made = back_chunk(c, dn2, projected, done)
            return made[1:], made[0] + d_gain if c else last_grads(made, d_gain)

        dn2, (done, d_gain) = step(work_back, dn2, projected, done, d_gain)
    moe.append(dn2)
    d_residual, d_mixed = done[1:3]
    share = width // data_count
    late = scattered(d_gain)

    firsts = (first_qkv, first_out, first_gate_up, first_down, first_gains)
    seconds = (second_moment_projection, second_out, second_gate_up, second_down, second_gains)

    def square_sum(array):
        return jnp.sum(array * array)

    def expert_moments():
        shard = expert_shard
        grads = (shard[:, :, :wide], shard[:, :, wide:].transpose(0, 2, 1))
        made = [
            lamb_moments(weight_shards[i], firsts[i], seconds[i], grad)
            for i, grad in zip((2, 3), grads)
        ]
        squares = [square_sum(weight) for weight in weight_shards[:4]]
        squares += [square_sum(row) * owner_mask for row in weight_shards[4]]
        squares += [0.0, 0.0, *[square_sum(update) for _, _, update in made]]
        return made, vector_of(squares)

    total, (made, squares) = step(expert_moments)
    moe.append(total)

    def input_work(d_residual, d_mixed):
        input_grad, d_gain = input_gradient(d_mixed, projected[0], d_residual, tokens, norm_gains)
        return input_grad, own_slice(sum_over(d_gain, "dp", data_count), 1)

    total, (input_grad, d_gain) = step(input_work, d_residual, d_mixed)
    moe.append(total)

    def some(arrays):
        return (arrays[0], arrays[1], arrays[4])

    def late_work(late, squares, d_gain):
        late_made, squares = late_moments(
            owner_mask, late, d_gain, squares, some(weight_shards), some(firsts), some(seconds)
        )
        return late_made, sum_over(squares, "dp", data_count)

    upper, (late_made, squares) = totals.send_half(0, late_work, late, squares, d_gain)
    squares = sum_over(squares, "tensor", tensor_count)
    all_made = [*late_made[:2], *made, late_made[2]]

    def apply(all_made, squares):
        norms = jnp.sqrt(squares)[0, :12]
        trust_ratio = norms[:6] / norms[6:]
        rates = [trust_ratio[index] for index in range(4)] + [trust_ratio[4:6][:, None]]
        updated = [
            weight - RATE * rate * made[2]
            for weight, rate, made in zip(weight_shards, rates, all_made)
        ]
        return updated, norms

    lower, (updated, norms) = totals.send_half(1, apply, all_made, squares)
    moe.append(tuple(jnp.concatenate(halves) for halves in zip(upper, lower)))
    block_out = jnp.zeros((tok, width), LOW)
    for c, (middle, end) in zip(reversed(range(chunks)), moe):
        rows = slice(c * ROWS, (c + 1) * ROWS)
        value = residual[rows] + jnp.where(inner[0] > 0, middle, end)
        block_out = block_out.at[rows].set(value.astype(LOW))
    next_firsts = [made[0] for made in all_made]
    next_seconds = [made[1] for made in all_made]
    trust_norms = jnp.stack([norms[:6], norms[6:]], axis=1)
    return (block_out, input_grad, *updated, *next_firsts, *next_seconds, trust_norms)


def solution(mesh):
    moments = (
        P("dp", "tensor"),
        P("tensor", "dp"),
        P("tensor", "dp", None),
        P("tensor", None, "dp"),
        P(None, "dp"),
    )
    in_specs = (
        *((P("dp", None),) * 7),
        P(),
        P(None, "tensor"),
        P("tensor", None),
        P("tensor", None, None),
        P("tensor", None, None),
        P(),
        *moments,
        *moments,
    )
    out_specs = (P("dp", None), P("dp", None), *moments, *moments, *moments, P())
    return jax.shard_map(body, mesh=mesh, in_specs=in_specs, out_specs=out_specs, check_vma=False)
```

```python
import functools

import jax
import jax.numpy as jnp
from jax import lax
from jax.experimental import pallas as pl
from jax.experimental.pallas import tpu as pltpu
from jax.sharding import PartitionSpec as P

QUERY_HEADS = 24
KEY_VALUE_HEADS = 8
PER_GROUP = QUERY_HEADS // KEY_VALUE_HEADS
HEAD_SIZE = 64
HALF = HEAD_SIZE // 2
TOP = 8
STEP = 3
GROUP_COLUMNS = 320

NORM_EPS = 1e-06
ROPE_BASE = 10000.0
BETA = 0.5
WEIGHT_DECAY = 0.01
ADAM_EPS = 1e-06
RATE = 0.5
MASKED = -1e30

ROWS = 256
MIB = 1 << 20
NO_COST = pl.CostEstimate(flops=0, bytes_accessed=0, transcendentals=0)
F32 = jnp.float32
LOW = jnp.bfloat16


def dot(a, b):
    return jnp.dot(a, b, preferred_element_type=F32)


def dot_nt(a, b):
    return lax.dot_general(a, b, (((1,), (1,)), ((), ())), preferred_element_type=F32)


def dot_tn(a, b):
    return lax.dot_general(a, b, (((0,), (0,)), ((), ())), preferred_element_type=F32)


def params(mib):
    return pltpu.CompilerParams(vmem_limit_bytes=mib * MIB)


def limits_kernel(capacity_ref, first_ref, ids_ref, order_ref, limit_ref):
    ids = ids_ref[...]
    order = order_ref[...]
    pairs = ids.shape[0] * ids.shape[1]
    own = []
    caps = []
    limits = []
    for e in range(limit_ref.shape[0]):
        label = first_ref[0] + e
        own.append(jnp.where(ids == label, order, pairs))
        caps.append(capacity_ref[label])
        limits.append(jnp.zeros((1, 1), jnp.int32))
    step = pairs
    while step > 1:
        step //= 2
        for e in range(len(own)):
            trial = limits[e] + step
            count = jnp.sum((own[e] < trial).astype(jnp.int32), axis=(0, 1), keepdims=True)
            limits[e] = jnp.where(count < caps[e], trial, limits[e])
    for e in range(len(own)):
        limit_ref[e : e + 1] = jnp.broadcast_to(limits[e], (1, limit_ref.shape[1]))


def order_limits(expert_ids, placement_order, capacity, first_expert, local_count):
    smem = pl.BlockSpec(memory_space=pltpu.SMEM)
    vmem = pl.BlockSpec(memory_space=pltpu.VMEM)
    return pl.pallas_call(
        limits_kernel,
        in_specs=[smem, smem, vmem, vmem],
        out_specs=vmem,
        out_shape=jax.ShapeDtypeStruct((local_count, 128), jnp.int32),
        compiler_params=params(16),
        cost_estimate=NO_COST,
        name="order_limits",
    )(
        capacity,
        first_expert.reshape(1),
        expert_ids.reshape(-1, 128),
        placement_order.reshape(-1, 128),
    )


def rotate(source, cos, sin):
    a = source[:HALF]
    b = source[HALF:]
    return jnp.concatenate([a * cos - b * sin, b * cos + a * sin], 0)


def rotate_back(source, cos, sin):
    a = source[:HALF]
    b = source[HALF:]
    return jnp.concatenate([a * cos + b * sin, b * cos - a * sin], 0)


def probabilities(keys, query_t, bias):
    scores = dot(keys, query_t) + bias
    top = jnp.max(scores, axis=0, keepdims=True)
    raised = jnp.exp(scores - top)
    return raised * (1.0 / jnp.sum(raised, axis=0, keepdims=True))


SCALE = HEAD_SIZE**-0.5


def tree_layout(parents_ref, row):
    seg_count = parents_ref.shape[1]
    bits = []
    lengths = []
    for s in range(seg_count):
        current = jnp.int32(s)
        mask = jnp.int32(1 << s)
        for repeat in range(seg_count):
            current = parents_ref[0, current]
            mask = mask | (jnp.int32(1) << current)
        bits.append(mask)
        lengths.append(jnp.sum((row == s).astype(jnp.int32), axis=1, keepdims=True))
    start = jnp.zeros((1, 1), jnp.int32)
    offset = jnp.zeros(row.shape, jnp.int32)
    reach = jnp.zeros(row.shape, jnp.int32)
    for s in range(seg_count):
        above = jnp.zeros((1, 1), jnp.int32)
        for a in range(seg_count):
            if a != s:
                above = above + lengths[a] * ((bits[s] >> a) & 1)
        offset = jnp.where(row == s, above - start, offset)
        reach = jnp.where(row == s, bits[s], reach)
        start = start + lengths[s]
    return lax.broadcasted_iota(jnp.int32, row.shape, 1) + offset, reach


def forward_kernel(
    parents_ref, row_ref, col_ref, freq_ref, x_ref, gain_ref, w_hbm,
    n1_hbm, bias_hbm, out_ref, cos_ref, sin_ref,
    w_ref, n1_ref, bias_ref, out_t, sems,
):
    tok = x_ref.shape[0]
    load = pltpu.make_async_copy(w_hbm, w_ref, sems.at[0])
    load.start()
    for lo in range(0, tok, ROWS):
        x = x_ref[lo : lo + ROWS].astype(F32)
        s = lax.rsqrt(jnp.mean(x * x, axis=-1, keepdims=True) + NORM_EPS)
        n1_ref[lo : lo + ROWS] = (x * s * gain_ref[...]).astype(LOW)
    save_n1 = pltpu.make_async_copy(n1_ref, n1_hbm, sems.at[1])
    save_n1.start()
    position, reach = tree_layout(parents_ref, row_ref[...])
    angles = position.astype(F32) * freq_ref[...]
    cos = jnp.cos(angles)
    sin = jnp.sin(angles)
    cos_ref[...] = cos
    sin_ref[...] = sin
    for lo in range(0, tok, ROWS):
        key = lax.broadcasted_iota(jnp.int32, (ROWS, tok), 0) + lo
        query = lax.broadcasted_iota(jnp.int32, (ROWS, tok), 1)
        seen = (jnp.right_shift(reach, col_ref[lo : lo + ROWS]) & 1) > 0
        bias_ref[lo : lo + ROWS] = jnp.where(seen & (key <= query), 0.0, MASKED)
    save_bias = pltpu.make_async_copy(bias_ref, bias_hbm, sems.at[2])
    save_bias.start()
    load.wait()
    mixed = dot(n1_ref[...], w_ref[...].astype(LOW)).T
    for g in range(w_ref.shape[1] // GROUP_COLUMNS):
        base = g * GROUP_COLUMNS
        at_key = base + PER_GROUP * HEAD_SIZE
        at_value = at_key + HEAD_SIZE
        keys = rotate(mixed[at_key:at_value], cos, sin).T.astype(LOW)
        value_t = mixed[at_value : at_value + HEAD_SIZE].astype(LOW)
        for h in range(PER_GROUP):
            lo = base + h * HEAD_SIZE
            query_t = rotate(mixed[lo : lo + HEAD_SIZE], cos, sin).astype(LOW) * SCALE
            query_t = query_t.astype(LOW)
            at = (g * PER_GROUP + h) * HEAD_SIZE
            for block in range(tok // ROWS):
                q0 = block * ROWS
                ext = q0 + ROWS
                probs = probabilities(
                    keys[:ext], query_t[:, q0:ext], bias_ref[:ext, q0:ext]
                ).astype(LOW)
                out_t[at : at + HEAD_SIZE, q0:ext] = dot(value_t[:, :ext], probs)
    out_ref[...] = out_t[...].T.astype(LOW).astype(F32)
    save_n1.wait()
    save_bias.wait()


def attention_forward(segment_ids, parents, x, gain, w_qkv):
    tok, width = x.shape
    cols = w_qkv.shape[1]
    heads = cols // GROUP_COLUMNS * PER_GROUP * HEAD_SIZE
    frequency = ROPE_BASE ** (-2.0 * jnp.arange(HALF, dtype=F32) / HEAD_SIZE)
    smem = pl.BlockSpec(memory_space=pltpu.SMEM)
    vmem = pl.BlockSpec(memory_space=pltpu.VMEM)
    anywhere = pl.BlockSpec(memory_space=pl.ANY)
    return pl.pallas_call(
        forward_kernel,
        in_specs=[smem, vmem, vmem, vmem, vmem, vmem, anywhere],
        out_specs=[anywhere, anywhere, vmem, vmem, vmem],
        out_shape=[
            jax.ShapeDtypeStruct((tok, width), LOW),
            jax.ShapeDtypeStruct((tok, tok), F32),
            jax.ShapeDtypeStruct((tok, heads), F32),
            jax.ShapeDtypeStruct((HALF, tok), F32),
            jax.ShapeDtypeStruct((HALF, tok), F32),
        ],
        scratch_shapes=[
            pltpu.VMEM((width, cols), F32),
            pltpu.VMEM((tok, width), LOW),
            pltpu.VMEM((tok, tok), F32),
            pltpu.VMEM((heads, tok), F32),
            pltpu.SemaphoreType.DMA((3,)),
        ],
        compiler_params=params(56),
        cost_estimate=NO_COST,
        name="attention_forward",
    )(
        parents,
        segment_ids,
        segment_ids.reshape(tok, 1),
        frequency.reshape(HALF, 1),
        x,
        gain,
        w_qkv,
    )


def out_kernel(first, sources, index_ref, *refs):
    heads = refs[: len(sources)]
    w_ref, x_ref, gain_ref = refs[len(sources) : len(sources) + 3]
    if first:
        res_ref, n2_ref, low_ref, stage = refs[-4:]
        shares, slices, rows, _ = w_ref.shape
        for t in range(slices):
            for d in range(shares):
                at = (t * shares + d) * rows
                low_ref[at : at + rows] = w_ref[d, t].astype(LOW)
    else:
        res_ref, n2_ref, stage = refs[-3:]
        low_ref = w_ref
    index = index_ref[0]
    count, _, part = stage.shape
    for i, (ref, offset) in enumerate(zip(heads, sources)):
        if offset is None:
            stage[i] = ref[...].astype(LOW)
        else:
            for j in range(count):

                @pl.when(index + offset == j)
                def _():
                    stage[j] = ref[...].astype(LOW)

    attn = dot(stage[0], low_ref[:part])
    for t in range(1, count):
        attn = attn + dot(stage[t], low_ref[t * part : (t + 1) * part])
    total = x_ref[...].astype(F32) + attn
    res_ref[...] = total
    s = lax.rsqrt(jnp.mean(total * total, axis=-1, keepdims=True) + NORM_EPS)
    n2_ref[...] = (total * s * gain_ref[...]).astype(LOW)


def out_projection(chunk, calls, heads, sources, index, count, weights, x, gain, done):
    first = not done
    tok, part = heads[0].shape
    width = x.shape[1]
    at = lambda i: (chunk - calls + 1 + i, 0)
    rows = pl.BlockSpec((ROWS, width), at)
    low = jax.ShapeDtypeStruct((count * part, width), LOW)
    low_spec = pl.BlockSpec(low.shape, lambda i: (0, 0))
    return pl.pallas_call(
        functools.partial(out_kernel, first, sources),
        grid=(calls,),
        in_specs=[
            pl.BlockSpec(memory_space=pltpu.SMEM),
            *[pl.BlockSpec((ROWS, part), at) for _ in heads],
            pl.BlockSpec(weights.shape, lambda i: (0,) * weights.ndim),
            rows,
            pl.BlockSpec((1, width), lambda i: (0, 0)),
            *[pl.BlockSpec(memory_space=pl.ANY) for _ in done],
        ],
        out_specs=[rows, rows] + [low_spec] * first,
        out_shape=[
            jax.ShapeDtypeStruct((tok, width), F32),
            jax.ShapeDtypeStruct((tok, width), LOW),
        ]
        + [low] * first,
        scratch_shapes=[pltpu.VMEM((count, ROWS, part), LOW)],
        input_output_aliases={len(heads) + 4 + i: i for i in range(len(done))},
        compiler_params=params(56),
        cost_estimate=NO_COST,
        name="out_projection",
    )(index.reshape(1), *heads, weights, x, gain, *done)


def expert_column(weights, e):
    lane = lax.broadcasted_iota(jnp.int32, weights.shape, 1)
    return jnp.sum(jnp.where(lane == e, weights, 0.0), axis=1, keepdims=True)


def expert_kernel(pieces, n2_ref, dy_ref, we_ref, wgu_ref, wd_ref, *refs):
    hid_ref, dgu_ref = refs[-2 - 2 * pieces : len(refs) - 2 * pieces]
    dn2_refs = refs[-2 * pieces : len(refs) - pieces]
    out_refs = refs[-pieces:]
    e = pl.program_id(0)
    ff = wd_ref.shape[0]
    weight = expert_column(we_ref[...], e)
    kept = weight > 0.0
    wgu = wgu_ref[...]
    wd = wd_ref[...]
    gate_up = dot(n2_ref[...], wgu)
    gate = gate_up[:, :ff]
    up = gate_up[:, ff:]
    sig = 1.0 / (1.0 + jnp.exp(-gate))
    silu = gate * sig
    hidden = jnp.where(kept, silu * up, 0.0).astype(LOW)
    hid_ref[...] = hidden
    out = weight * dot(hidden, wd)
    d_out = (weight * dy_ref[...].astype(F32)).astype(LOW)
    d_hidden = dot_nt(d_out, wd)
    d_gate = d_hidden * up * sig * (1.0 + gate * (1.0 - sig))
    d_up = d_hidden * silu
    d_gate_up = jnp.where(kept, jnp.concatenate([d_gate, d_up], 1), 0.0).astype(LOW)
    dgu_ref[...] = d_gate_up
    d_n2 = dot_nt(d_gate_up, wgu)

    for sums, refs in ((d_n2, dn2_refs), (out, out_refs)):
        for i, ref in enumerate(refs):
            part = sums[i * ROWS : (i + 1) * ROWS]

            @pl.when(e == 0)
            def _():
                ref[...] = part

            @pl.when(e > 0)
            def _():
                ref[...] += part


def experts(chunk, pieces, n2, dy, weights, wgu, wd, done):
    tok, width = n2.shape
    count, ff, _ = wd.shape
    rows = pieces * ROWS
    at = chunk * ROWS
    wide = pl.BlockSpec((pl.Element(rows), pl.Element(width)), lambda e: (at, 0))
    tall = lambda cols: pl.BlockSpec(
        (None, pl.Element(rows), pl.Element(cols)), lambda e: (e, at, 0)
    )
    return pl.pallas_call(
        functools.partial(expert_kernel, pieces),
        grid=(count,),
        in_specs=[
            wide,
            wide,
            pl.BlockSpec((pl.Element(rows), pl.Element(count)), lambda e: (at, 0)),
            pl.BlockSpec((None, width, 2 * ff), lambda e: (e, 0, 0)),
            pl.BlockSpec((None, ff, width), lambda e: (e, 0, 0)),
            *[pl.BlockSpec(memory_space=pl.ANY) for _ in done],
        ],
        out_specs=[
            tall(ff),
            tall(2 * ff),
            *[pl.BlockSpec((ROWS, width), lambda e: (0, 0))] * (2 * pieces),
        ],
        out_shape=[
            jax.ShapeDtypeStruct((count, tok, ff), LOW),
            jax.ShapeDtypeStruct((count, tok, 2 * ff), LOW),
            *[jax.ShapeDtypeStruct((ROWS, width), F32)] * (2 * pieces),
        ],
        input_output_aliases={5 + i: i for i in range(len(done))},
        compiler_params=params(56),
        cost_estimate=NO_COST,
        name="experts",
    )(n2, dy, weights, wgu, wd, *done)


def split_store(out_ref, lo, value):
    rows = out_ref.shape[1]
    cols = slice(lo, lo + value.shape[1])
    for i in range(out_ref.shape[0]):
        out_ref[i, :, cols] = value[i * rows : (i + 1) * rows]


def late_grad_kernel(place_ref, n1_ref, dmix_ref, dattn_ref, heads_ref, gains_ref, out_ref):
    shares, lanes = gains_ref.shape[0], gains_ref.shape[2]
    share = n1_ref.shape[1] // shares
    split = dmix_ref.shape[1]
    out_ref[:, share:, :] = jnp.zeros((shares, 8, out_ref.shape[2]), F32)
    out_ref[:, share:, :lanes] = gains_ref[...]
    for left, right, lo in ((n1_ref, dmix_ref, 0), (dattn_ref, heads_ref, split)):
        value = dot_tn(left[...], right[...].astype(LOW))
        for i in range(shares):
            out_ref[i, :share, lo : lo + right.shape[1]] = value[i * share : (i + 1) * share]


def late_grads(place, n1, d_mixed, d_attn, heads, gains):
    tok, width = n1.shape
    count = gains.shape[0]
    steps = 4
    some = count // steps
    rows = width // count + 8
    cols = d_mixed.shape[2] + heads.shape[1]
    part = pl.BlockSpec((tok, width // steps), lambda i, at: (0, i))
    return pl.pallas_call(
        late_grad_kernel,
        grid_spec=pltpu.PrefetchScalarGridSpec(
            num_scalar_prefetch=1,
            grid=(steps,),
            in_specs=[
                part,
                pl.BlockSpec((None, *d_mixed.shape[1:]), lambda i, at: (at[0], 0, 0)),
                part,
                pl.BlockSpec(heads.shape, lambda i, at: (0, 0)),
                pl.BlockSpec((some, *gains.shape[1:]), lambda i, at: (i, 0, 0)),
            ],
            out_specs=pl.BlockSpec((some, rows, cols), lambda i, at: (i, 0, 0)),
        ),
        out_shape=jax.ShapeDtypeStruct((count, rows, cols), F32),
        compiler_params=params(56),
        cost_estimate=NO_COST,
        name="late_grads",
    )(place.reshape(1), n1, d_mixed, d_attn, heads, gains)


def expert_grad_kernel(n2_ref, dy_ref, we_ref, dgu_ref, hid_ref, out_ref):
    weight = expert_column(we_ref[...], pl.program_id(1))
    d_out = (weight * dy_ref[...].astype(F32)).astype(LOW)
    split_store(out_ref, 0, dot_tn(n2_ref[...], dgu_ref[...]))
    split_store(out_ref, dgu_ref.shape[1], dot_tn(d_out, hid_ref[...]))


def expert_grads(n2, dy, weights, d_gate_up, hidden, shares):
    tok, width = n2.shape
    count, _, wide = d_gate_up.shape
    ff = hidden.shape[2]
    share = width // shares
    parts = shares // 2
    rows = pl.BlockSpec((tok, parts * share), lambda i, e: (0, i))
    return pl.pallas_call(
        expert_grad_kernel,
        grid=(shares // parts, count),
        in_specs=[
            rows,
            rows,
            pl.BlockSpec(weights.shape, lambda i, e: (0, 0)),
            pl.BlockSpec((None, tok, wide), lambda i, e: (e, 0, 0)),
            pl.BlockSpec((None, tok, ff), lambda i, e: (e, 0, 0)),
        ],
        out_specs=pl.BlockSpec((parts, None, share, wide + ff), lambda i, e: (i, e, 0, 0)),
        out_shape=jax.ShapeDtypeStruct((shares, count, share, wide + ff), F32),
        compiler_params=params(56),
        cost_estimate=NO_COST,
        name="expert_grads",
    )(n2, dy, weights, d_gate_up, hidden)


def heads_kernel(n1_ref, w_ref, cos_ref, sin_ref, low_ref, qt_ref, q_ref, kt_ref, k_ref, v_ref):
    cols = w_ref.shape[-1]
    w_low = w_ref[...].reshape(-1, cols).astype(LOW)
    low_ref[...] = w_low
    mixed = dot(n1_ref[...], w_low).T
    cos = cos_ref[...]
    sin = sin_ref[...]
    queries = []
    keys = []
    values = []
    for g in range(cols // GROUP_COLUMNS):
        base = g * GROUP_COLUMNS
        for h in range(PER_GROUP):
            lo = base + h * HEAD_SIZE
            queries.append(rotate(mixed[lo : lo + HEAD_SIZE], cos, sin))
        at_key = base + PER_GROUP * HEAD_SIZE
        at_value = at_key + HEAD_SIZE
        keys.append(rotate(mixed[at_key:at_value], cos, sin))
        values.append(mixed[at_value : at_value + HEAD_SIZE])
    queries = jnp.concatenate(queries, 0)
    keys = jnp.concatenate(keys, 0)
    qt_ref[...] = (queries.astype(LOW) * SCALE).astype(LOW)
    q_ref[...] = queries.T.astype(LOW)
    kt_ref[...] = keys.astype(LOW)
    k_ref[...] = keys.T.astype(LOW)
    v_ref[...] = jnp.concatenate(values, 0).T.astype(LOW)


def all_heads(n1, w_slices, cos, sin):
    shares, slices, rows, cols = w_slices.shape
    tok, width = n1.shape
    groups = cols // GROUP_COLUMNS
    keys = groups * HEAD_SIZE
    queries = keys * PER_GROUP
    shapes = [(width, cols), (queries, tok), (tok, queries), (keys, tok), (tok, keys), (tok, keys)]
    whole = lambda *shape: pl.BlockSpec(shape, lambda t: (0,) * len(shape))
    return pl.pallas_call(
        heads_kernel,
        grid=(slices,),
        in_specs=[
            whole(tok, width),
            pl.BlockSpec((shares, None, rows, cols), lambda t: (0, t, 0, 0)),
            whole(HALF, tok),
            whole(HALF, tok),
        ],
        out_specs=[pl.BlockSpec((None, *shape), lambda t: (t, 0, 0)) for shape in shapes],
        out_shape=[jax.ShapeDtypeStruct((slices, *shape), LOW) for shape in shapes],
        compiler_params=params(56),
        cost_estimate=NO_COST,
        name="all_heads",
    )(n1, w_slices, cos, sin)


def norm_terms(rows_in, gain, upstream):
    s = lax.rsqrt(jnp.mean(rows_in * rows_in, axis=-1, keepdims=True) + NORM_EPS)
    pulled = upstream * gain
    inner = jnp.mean(rows_in * pulled, axis=-1, keepdims=True)
    grad = s * pulled - rows_in * (s * s * s) * inner
    return grad, jnp.sum(upstream * rows_in * s, axis=0, keepdims=True)


def backward_kernel(
    inner_ref, dn2_hbm, dn2_end_hbm, res_ref, dy_ref, gains_ref, wo_ref, qt_ref, q_ref, kt_ref, k_ref,
    v_ref, cos_ref, sin_ref, bias_ref, *refs,
):
    later = len(refs) > 10
    d_gain_ref, dattn_ref, dres_ref, dmix_ref, dk_ref, dv_ref = refs[-10:-4]
    dmix_t, dn2_ref, low_dattn, sem = refs[-4:]
    t = pl.program_id(0)
    ext = bias_ref.shape[0]
    old = ext - ROWS

    @pl.when(t == 0)
    def _():
        for flag, source in ((1, dn2_hbm), (0, dn2_end_hbm)):

            @pl.when(inner_ref[0] == flag)
            def _():
                copy = pltpu.make_async_copy(source, dn2_ref, sem)
                copy.start()
                copy.wait()

        grad, gain = norm_terms(res_ref[...], gains_ref[1:2], dn2_ref[...])
        grad = grad + dy_ref[...].astype(F32)
        dres_ref[...] = grad
        low_dattn[...] = grad.astype(LOW)
        dattn_ref[...] = grad.astype(LOW)
        d_gain_ref[...] = gain

    d_heads = dot_nt(low_dattn[...], wo_ref[...])
    d_heads_t = d_heads.T.astype(LOW)
    d_heads = d_heads.astype(LOW)
    cos = cos_ref[...]
    sin = sin_ref[...]
    bias = bias_ref[...]
    for g in range(k_ref.shape[1] // HEAD_SIZE):
        at_g = g * HEAD_SIZE
        keys = k_ref[:, at_g : at_g + HEAD_SIZE]
        keys_t = kt_ref[at_g : at_g + HEAD_SIZE]
        values = v_ref[:, at_g : at_g + HEAD_SIZE]
        d_keys = jnp.zeros((ext, HEAD_SIZE), F32)
        d_values = jnp.zeros((ext, HEAD_SIZE), F32)
        base = g * GROUP_COLUMNS
        for h in range(PER_GROUP):
            at = (g * PER_GROUP + h) * HEAD_SIZE
            probs = probabilities(keys, qt_ref[at : at + HEAD_SIZE], bias)
            d_probs = dot(values, d_heads_t[at : at + HEAD_SIZE])
            delta = jnp.sum(probs * d_probs, axis=0, keepdims=True)
            d_scores = (probs * (d_probs - delta)).astype(LOW)
            d_query = dot(keys_t, d_scores) * SCALE
            d_keys = d_keys + dot(d_scores, q_ref[:, at : at + HEAD_SIZE])
            d_values = d_values + dot(probs.astype(LOW), d_heads[:, at : at + HEAD_SIZE])
            lo = base + h * HEAD_SIZE
            dmix_t[lo : lo + HEAD_SIZE] = rotate_back(d_query, cos, sin)
        if later:
            dk_in, dv_in = refs[-12:-10]
            d_keys = d_keys + dk_in[:, at_g : at_g + HEAD_SIZE]
            d_values = d_values + dv_in[:, at_g : at_g + HEAD_SIZE]
        if old:
            dk_ref[:, at_g : at_g + HEAD_SIZE] = d_keys
            dv_ref[:, at_g : at_g + HEAD_SIZE] = d_values
        at_key = base + PER_GROUP * HEAD_SIZE
        at_value = at_key + HEAD_SIZE
        dmix_t[at_key:at_value] = rotate_back(d_keys[old:].T * SCALE, cos, sin)
        dmix_t[at_value : at_value + HEAD_SIZE] = d_values[old:].T
    dmix_ref[...] = dmix_t[...].T.astype(LOW)


def attention_backward(chunk, inner, dn2, residual, dy, gains, heads, wo, cos, sin, bias, done):
    qt, q, kt, k, v = heads
    slices, queries, _ = qt.shape
    tok, width = residual.shape
    keys = k.shape[2]
    cols = queries + 2 * keys
    ext = (chunk + 1) * ROWS
    rows = pl.BlockSpec((ROWS, width), lambda t: (chunk, 0))
    sums = pl.BlockSpec((None, ext, keys), lambda t: (t, 0, 0))
    angles = pl.BlockSpec((HALF, ROWS), lambda t: (0, chunk))
    anywhere = pl.BlockSpec(memory_space=pl.ANY)
    hbm = pl.BlockSpec(memory_space=pltpu.HBM)
    part = lambda *shape: pl.BlockSpec((None, *shape), lambda t: (t, 0, 0))
    done_specs = [anywhere, anywhere, anywhere, sums, sums][: len(done)]
    return pl.pallas_call(
        backward_kernel,
        grid=(slices,),
        in_specs=[
            pl.BlockSpec(memory_space=pltpu.SMEM),
            hbm,
            hbm,
            rows,
            rows,
            pl.BlockSpec(gains.shape, lambda t: (0, 0)),
            pl.BlockSpec((queries, width), lambda t: (t, 0)),
            pl.BlockSpec((None, queries, ROWS), lambda t: (t, 0, chunk)),
            pl.BlockSpec((None, ROWS, queries), lambda t: (t, chunk, 0)),
            part(keys, ext),
            part(ext, keys),
            part(ext, keys),
            angles,
            angles,
            pl.BlockSpec((ext, ROWS), lambda t: (0, chunk)),
            *done_specs,
        ],
        out_specs=[
            pl.BlockSpec((1, width), lambda t: (0, 0)),
            rows,
            rows,
            pl.BlockSpec((None, ROWS, cols), lambda t: (t, chunk, 0)),
            sums,
            sums,
        ],
        out_shape=[
            jax.ShapeDtypeStruct((1, width), F32),
            jax.ShapeDtypeStruct((tok, width), LOW),
            jax.ShapeDtypeStruct((tok, width), F32),
            jax.ShapeDtypeStruct((slices, tok, cols), LOW),
            jax.ShapeDtypeStruct((slices, tok, keys), F32),
            jax.ShapeDtypeStruct((slices, tok, keys), F32),
        ],
        scratch_shapes=[
            pltpu.VMEM((cols, ROWS), F32),
            pltpu.VMEM((ROWS, width), F32),
            pltpu.VMEM((ROWS, width), LOW),
            pltpu.SemaphoreType.DMA,
        ],
        input_output_aliases={15 + i: 1 + i for i in range(len(done))},
        compiler_params=params(56),
        cost_estimate=NO_COST,
        name="attention_backward",
    )(inner, *dn2, residual, dy, gains, wo, qt, q, kt, k, v, cos, sin, bias, *done)


def input_kernel(dmix_ref, low_ref, dres_ref, x_ref, gains_ref, igrad_ref, d_gain_ref):
    dn1 = dot_nt(dmix_ref[0], low_ref[0])
    for t in range(1, dmix_ref.shape[0]):
        dn1 = dn1 + dot_nt(dmix_ref[t], low_ref[t])
    grad, gain = norm_terms(x_ref[...].astype(F32), gains_ref[0:1], dn1)
    igrad_ref[...] = (dres_ref[...] + grad).astype(LOW)

    @pl.when(pl.program_id(0) == 0)
    def _():
        d_gain_ref[...] = gain

    @pl.when(pl.program_id(0) > 0)
    def _():
        d_gain_ref[...] += gain


def input_gradient(d_mixed, low, d_residual, x, gains):
    slices, tok, cols = d_mixed.shape
    width = x.shape[1]
    rows = pl.BlockSpec((ROWS, width), lambda i: (i, 0))
    return pl.pallas_call(
        input_kernel,
        grid=(tok // ROWS,),
        in_specs=[
            pl.BlockSpec((slices, ROWS, cols), lambda i: (0, i, 0)),
            pl.BlockSpec(low.shape, lambda i: (0, 0, 0)),
            rows,
            rows,
            pl.BlockSpec(gains.shape, lambda i: (0, 0)),
        ],
        out_specs=[rows, pl.BlockSpec((1, width), lambda i: (0, 0))],
        out_shape=[
            jax.ShapeDtypeStruct((tok, width), LOW),
            jax.ShapeDtypeStruct((1, width), F32),
        ],
        compiler_params=params(56),
        cost_estimate=NO_COST,
        name="input_gradient",
    )(d_mixed, low, d_residual, x, gains)


def gather_heads(own, index, count, shares, beside_first, beside_second):
    if count != 4:
        gathered = lax.all_gather(own, "tensor")
        arrays = [gathered[j] for j in range(count)]
        return arrays, [None] * count, lax.all_gather(shares, "dp"), beside_first, beside_second
    up = [own]
    down = [own]
    for hop in range(1, count):
        if hop == 2:
            flight = (up[-1], down[-1], shares, beside_first)
            up[-1], down[-1], shares, beside_first = lax.optimization_barrier(flight)
            gathered = lax.all_gather(shares, "dp")
        if hop == 3:
            flight = (up[-1], down[-1], beside_second)
            up[-1], down[-1], beside_second = lax.optimization_barrier(flight)
        up.append(lax.ppermute(up[-1], "tensor", [(i, i + 1) for i in range(hop - 1, count - 1)]))
        down.append(
            lax.ppermute(down[-1], "tensor", [(i + 1, i) for i in range(count - hop)])
        )
    sources = [0, *[-hop for hop in range(1, count)], *range(1, count)]
    return [own, *up[1:], *down[1:]], sources, gathered, beside_first, beside_second


def combine_kernel(
    inner_ref, mid_hbm, crossed_hbm, piece_hbm, got_hbm, next_hbm, send_hbm, sum_hbm,
    mid, crossed, piece, got, sems,
):
    inner = inner_ref[0] > 0
    half = mid.shape[0] // 2

    @pl.when(inner)
    def _():
        loads = []
        for i in range(2):
            rows = pl.ds(i * half, half)
            pairs = ((mid_hbm, mid), (crossed_hbm, crossed), (piece_hbm, piece), (got_hbm, got))
            for j, (source, target) in enumerate(pairs):
                copy = pltpu.make_async_copy(source.at[rows], target.at[rows], sems.at[i, j])
                copy.start()
                loads.append(copy)
        stores = []
        for i in range(2):
            rows = pl.ds(i * half, half)
            for first, left, right, target in ((0, mid, crossed, send_hbm), (2, piece, got, sum_hbm)):
                loads[i * 4 + first].wait()
                loads[i * 4 + first + 1].wait()
                left[rows] = left[rows] + right[rows]
                copy = pltpu.make_async_copy(left.at[rows], target.at[rows], sems.at[i, 4 + first // 2])
                copy.start()
                stores.append(copy)
        for copy in stores:
            copy.wait()

    @pl.when(jnp.logical_not(inner))
    def _():
        copy = pltpu.make_async_copy(next_hbm, send_hbm, sems.at[0, 0])
        copy.start()
        copy.wait()


def combine(inner, *arrays):
    shape = arrays[0].shape
    hbm = pl.BlockSpec(memory_space=pltpu.HBM)
    return pl.pallas_call(
        combine_kernel,
        in_specs=[pl.BlockSpec(memory_space=pltpu.SMEM), *[hbm] * 5],
        out_specs=[hbm, hbm],
        out_shape=[jax.ShapeDtypeStruct(shape, F32)] * 2,
        scratch_shapes=[*[pltpu.VMEM(shape, F32)] * 4, pltpu.SemaphoreType.DMA((2, 6))],
        compiler_params=params(32),
        cost_estimate=NO_COST,
        name="combine",
    )(inner, *arrays)


class Totals:
    def __init__(self, index, count, piece, following, last):
        self.count = count
        self.last = last
        inner = (index == 1) | (index == 2)
        self.inner = inner.astype(jnp.int32).reshape(1)
        self.sent = self.mid = self.piece = piece
        self.following = following
        self.queue = []
        self.at = 0

    def step(self, work, *inputs):
        flight = (self.sent, self.mid, self.piece, inputs)
        sent, mid, piece, inputs = lax.optimization_barrier(flight)
        if self.count != 4:
            made = work(*inputs)
            self.queue.append(lax.psum(piece, "tensor"))
            done = (self.queue[-3:][0],) * 2
            self.piece = self.following()
        else:
            got = lax.ppermute(sent, "tensor", [(0, 1), (1, 0), (2, 3), (3, 2)])
            crossed = mid
            if 0 < self.at < self.last:
                crossed = lax.ppermute(mid, "tensor", [(1, 2), (2, 1)])
            made = work(*inputs)
            following = self.following()
            got, crossed, made = lax.optimization_barrier((got, crossed, made))
            done = (sent, got)
            if self.at < self.last:
                self.sent, self.mid = combine(self.inner, mid, crossed, piece, got, following)
            self.piece = following
            self.at += 1
        landed = (done, self.sent, self.mid, self.piece, made)
        done, self.sent, self.mid, self.piece, made = lax.optimization_barrier(landed)
        return done, made

    def send_half(self, half, work, *inputs):
        if self.count != 4:
            return (self.piece, self.piece), work(*inputs)
        rows = self.sent.shape[0] // 2
        sent = self.sent[half * rows : (half + 1) * rows]
        sent, inputs = lax.optimization_barrier((sent, inputs))
        got = lax.ppermute(sent, "tensor", [(0, 1), (1, 0), (2, 3), (3, 2)])
        made = work(*inputs)
        sent, got, made = lax.optimization_barrier((sent, got, made))
        return (sent, got), made


def sum_over(values, axis, count):
    if count & (count - 1):
        return lax.psum(values, axis)
    hop = 1
    while hop < count:
        values = values + lax.ppermute(values, axis, [(i, i ^ hop) for i in range(count)])
        hop *= 2
    return values


def vector_of(scalars):
    place = jnp.arange(128)[None, :]
    return sum(jnp.where(place == i, scalar, 0.0) for i, scalar in enumerate(scalars))


def lamb_moments(weight, moment_one, moment_two, gradient):
    first_new = BETA * moment_one + (1.0 - BETA) * gradient
    second_new = BETA * moment_two + (1.0 - BETA) * gradient * gradient
    correction = 1.0 - BETA**STEP
    update = (
        first_new / correction / (jnp.sqrt(second_new / correction) + ADAM_EPS)
        + WEIGHT_DECAY * weight
    )
    return (first_new, second_new, update)


def late_moments_kernel(owner_ref, late_ref, gain_ref, squares_ref, *refs):
    weights, firsts, seconds = refs[:3], refs[3:6], refs[6:9]
    outs, squares_out = refs[9:18], refs[18]
    share, cols = weights[0].shape
    lane = lax.broadcasted_iota(jnp.int32, squares_ref.shape, 1)
    squares = squares_ref[...]
    grads = (
        late_ref[:share, :cols],
        late_ref[:share, cols:].T,
        jnp.concatenate([gain_ref[...], late_ref[share : share + 1, :share]], 0),
    )
    for i, grad in enumerate(grads):
        weight = weights[i][...]
        first, second, update = lamb_moments(weight, firsts[i][...], seconds[i][...], grad)
        outs[3 * i][...] = first
        outs[3 * i + 1][...] = second
        outs[3 * i + 2][...] = update
        if i < 2:
            squares = squares + jnp.where(lane == 6 + i, jnp.sum(update * update), 0.0)
            continue
        for row in range(2):
            total = jnp.sum(update[row] * update[row]) * owner_ref[0]
            squares = squares + jnp.where(lane == 10 + row, total, 0.0)
    squares_out[...] = squares


def late_moments(owner, late, gain, squares, weights, firsts, seconds):
    vmem = pl.BlockSpec(memory_space=pltpu.VMEM)
    shapes = [jax.ShapeDtypeStruct(weight.shape, F32) for weight in weights for _ in range(3)]
    *made, squares = pl.pallas_call(
        late_moments_kernel,
        in_specs=[pl.BlockSpec(memory_space=pltpu.SMEM), *[vmem] * 12],
        out_specs=[vmem] * 10,
        out_shape=[*shapes, jax.ShapeDtypeStruct(squares.shape, F32)],
        compiler_params=params(48),
        cost_estimate=NO_COST,
        name="late_moments",
    )(owner.reshape(1), late, gain, squares, *weights, *firsts, *seconds)
    return [tuple(made[3 * i : 3 * i + 3]) for i in range(3)], squares


def body(
    tokens, cotangent, segment_ids, parents, expert_ids, gate_weights, placement_order, capacity,
    w_qkv, w_out, w_gate_up, w_down, norm_gains,
    first_qkv, first_out, first_gate_up, first_down, first_gains,
    second_moment_projection, second_out, second_gate_up, second_down, second_gains,
):
    tok, width = tokens.shape
    local_experts = w_gate_up.shape[0]
    tensor_index = lax.axis_index("tensor")
    tensor_count = lax.axis_size("tensor")
    data_index = lax.axis_index("dp")
    data_count = lax.axis_size("dp")
    owner_mask = (tensor_index == 0).astype(F32)
    share = tok // tensor_count

    def own_slice(source, axis_dim):
        share_len = source.shape[axis_dim] // data_count
        return lax.dynamic_slice_in_dim(source, data_index * share_len, share_len, axis_dim)

    def own_rows(source):
        return lax.dynamic_slice_in_dim(source, tensor_index * share, share, 0)

    weight_shards = (
        own_slice(w_qkv, 0),
        own_slice(w_out, 1),
        own_slice(w_gate_up, 1),
        own_slice(w_down, 2),
        own_slice(norm_gains, 1),
    )
    first_expert = tensor_index * local_experts

    def weights_of(expert_ids, placement_order, gate_weights, limits):
        local_ids = expert_ids - first_expert
        order = placement_order.reshape(expert_ids.shape)
        columns = []
        for e in range(local_experts):
            kept = (local_ids == e) & (order <= limits[e, 0])
            columns.append(jnp.sum(jnp.where(kept, gate_weights, 0.0), axis=1))
        return jnp.stack(columns, axis=1)

    out_shares = lax.all_gather(own_slice(w_out, 0), "tensor")
    n1, bias, heads_own, cos, sin = attention_forward(
        segment_ids, parents, tokens, norm_gains[0:1], w_qkv
    )
    routed = (expert_ids, placement_order, gate_weights)
    later = (heads_own, w_gate_up, w_down, routed)
    heads_own, wgu, wd, routed = lax.optimization_barrier(later)
    limits = order_limits(*routed[:2], capacity, first_expert, local_experts)
    beside_first = (wd.astype(LOW), weights_of(*routed, limits))
    beside_second = (wgu.astype(LOW), weight_shards)
    heads, sources, all_out, beside_first, beside_second = gather_heads(
        heads_own, tensor_index, tensor_count, out_shares, beside_first, beside_second
    )
    wd_low, expert_weights = beside_first
    wgu_low, weight_shards = beside_second
    heads, qkv_share = lax.optimization_barrier((heads, weight_shards[0]))
    qkv_shares = lax.all_gather(qkv_share, "tensor")

    chunks = tok // ROWS
    wide = w_gate_up.shape[2]

    def project(chunk, calls, weights, done):
        return out_projection(
            chunk, calls, heads, sources, tensor_index, tensor_count, weights, tokens,
            norm_gains[1:2], done,
        )

    def expert_chunks(chunk, pieces, n2, made):
        made = experts(
            chunk, pieces, n2, cotangent, expert_weights, wgu_low, wd_low, made
        )
        parts = made[2 : 2 + pieces]
        outs.extend(made[: 1 + pieces : -1])
        return made[:2], parts[::-1]

    def scattered(source):
        return lax.psum_scatter(source, "dp", tiled=True)[0]

    outs = []
    pieces = []
    *normed, wo_low = project(chunks - 1, 1, all_out, ())
    made, parts = expert_chunks(chunks - 1, 1, normed[1], ())
    last_step = 2 * chunks + 1

    def following():
        queue = pieces or outs
        return queue.pop(0) if queue else parts[0]

    totals = Totals(tensor_index, tensor_count, parts[0], following, last_step)
    inner = totals.inner
    step = totals.step
    whole = {}

    def work_zero(normed, made):
        normed = project(chunks - 2, chunks - 1, wo_low, normed)
        normed, shares = lax.optimization_barrier((normed, qkv_shares))
        whole["qkv"] = lax.all_gather(shares, "dp")
        made, parts = expert_chunks(0, chunks - 1, normed[1], made)
        pieces.extend(parts)
        return made, normed

    _, (made, normed) = step(work_zero, normed, made)
    residual, n2 = normed
    all_outs = outs[::-1]

    def work_one(n2, hidden, d_gate_up):
        return expert_grads(n2, cotangent, expert_weights, d_gate_up, hidden, data_count)

    _, grads = step(work_one, n2, *made)
    expert_shard = scattered(grads)
    dn2, projected = step(lambda w: all_heads(n1, w, cos, sin), whole["qkv"])

    def back_chunk(c, dn2, projected, done):
        return attention_backward(
            c, inner, dn2, residual, cotangent, norm_gains, projected[1:], wo_low, cos, sin, bias, done
        )

    def last_grads(made, d_gain):
        gains = (made[0] + d_gain).reshape(data_count, 1, -1)
        gains = jnp.pad(gains, ((0, 0), (0, 7), (0, 0)))
        return late_grads(tensor_index, n1, made[3], made[1], heads_own, gains)

    done = ()
    d_gain = 0.0
    moe = []
    for c in reversed(range(chunks)):

        def work_back(dn2, projected, done, d_gain):
            made = back_chunk(c, dn2, projected, done)
            return made[1:], made[0] + d_gain if c else last_grads(made, d_gain)

        dn2, (done, d_gain) = step(work_back, dn2, projected, done, d_gain)
    moe.append(dn2)
    d_residual, d_mixed = done[1:3]
    share = width // data_count
    late = scattered(d_gain)

    firsts = (first_qkv, first_out, first_gate_up, first_down, first_gains)
    seconds = (second_moment_projection, second_out, second_gate_up, second_down, second_gains)

    def square_sum(array):
        return jnp.sum(array * array)

    def expert_moments():
        shard = expert_shard
        grads = (shard[:, :, :wide], shard[:, :, wide:].transpose(0, 2, 1))
        made = [
            lamb_moments(weight_shards[i], firsts[i], seconds[i], grad)
            for i, grad in zip((2, 3), grads)
        ]
        squares = [square_sum(weight) for weight in weight_shards[:4]]
        squares += [square_sum(row) * owner_mask for row in weight_shards[4]]
        squares += [0.0, 0.0, *[square_sum(update) for _, _, update in made]]
        return made, vector_of(squares)

    total, (made, squares) = step(expert_moments)
    moe.append(total)

    def input_work(d_residual, d_mixed):
        input_grad, d_gain = input_gradient(d_mixed, projected[0], d_residual, tokens, norm_gains)
        return input_grad, own_slice(sum_over(d_gain, "dp", data_count), 1)

    total, (input_grad, d_gain) = step(input_work, d_residual, d_mixed)
    moe.append(total)

    def some(arrays):
        return (arrays[0], arrays[1], arrays[4])

    def late_work(late, squares, d_gain):
        late_made, squares = late_moments(
            owner_mask, late, d_gain, squares, some(weight_shards), some(firsts), some(seconds)
        )
        return late_made, sum_over(squares, "dp", data_count)

    upper, (late_made, squares) = totals.send_half(0, late_work, late, squares, d_gain)
    squares = sum_over(squares, "tensor", tensor_count)
    all_made = [*late_made[:2], *made, late_made[2]]

    def apply(all_made, squares):
        norms = jnp.sqrt(squares)[0, :12]
        trust_ratio = norms[:6] / norms[6:]
        rates = [trust_ratio[index] for index in range(4)] + [trust_ratio[4:6][:, None]]
        updated = [
            weight - RATE * rate * made[2]
            for weight, rate, made in zip(weight_shards, rates, all_made)
        ]
        return updated, norms

    lower, (updated, norms) = totals.send_half(1, apply, all_made, squares)
    moe.append(tuple(jnp.concatenate(halves) for halves in zip(upper, lower)))
    if tensor_count != 4:
        total = lax.psum(jnp.concatenate(all_outs), "tensor")
        moe = [(total[c * ROWS : (c + 1) * ROWS],) * 2 for c in reversed(range(chunks))]
    block_out = jnp.zeros((tok, width), LOW)
    for c, (middle, end) in zip(reversed(range(chunks)), moe):
        rows = slice(c * ROWS, (c + 1) * ROWS)
        value = residual[rows] + jnp.where(inner[0] > 0, middle, end)
        block_out = block_out.at[rows].set(value.astype(LOW))
    next_firsts = [made[0] for made in all_made]
    next_seconds = [made[1] for made in all_made]
    trust_norms = jnp.stack([norms[:6], norms[6:]], axis=1)
    return (block_out, input_grad, *updated, *next_firsts, *next_seconds, trust_norms)


def solution(mesh):
    moments = (
        P("dp", "tensor"),
        P("tensor", "dp"),
        P("tensor", "dp", None),
        P("tensor", None, "dp"),
        P(None, "dp"),
    )
    in_specs = (
        *((P("dp", None),) * 7),
        P(),
        P(None, "tensor"),
        P("tensor", None),
        P("tensor", None, None),
        P("tensor", None, None),
        P(),
        *moments,
        *moments,
    )
    out_specs = (P("dp", None), P("dp", None), *moments, *moments, *moments, P())
    return jax.shard_map(body, mesh=mesh, in_specs=in_specs, out_specs=out_specs, check_vma=False)
```
